128 devices in a mesh: view: 32 (over y, x, core), band: 4 (over z).
Axes of the slice: x: 4, y: 4, z: 4, core: 2. Of those that a mesh axis runs over, the one named last changes fastest.
Arguments:
- gaussians: float32 [2048, 62, 256], P(('view', 'band')), may hold values from -8 to 128, as said below
- first_moment: float32 [2048, 62, 256], P(('view', 'band')), may hold values from -0.6 to 0.6
- second_moment: float32 [2048, 62, 256], P(('view', 'band')), may hold values from 0.0001 to 0.1
- camera: float32 [32, 9], P('view'), may hold values from -352 to 352, as said below
- target: float32 [32, 3, 64, 128], P('view', None, 'band'), may hold values from 0 to 1
- block_list: int32 [32, 4, 16], P('view', 'band'), may hold values from -1 to 2047, as said below
- block_count: int32 [32, 4], P('view', 'band'), may hold values from 12 to 16, as said below
- tile_start: int32 [32, 4, 8], P('view', 'band'), may hold values from 0 to 15, as said below
- tile_end: int32 [32, 4, 8], P('view', 'band'), may hold values from 1 to 16, as said below
Outputs:
- new_gaussians: float32 [2048, 62, 256], P(('view', 'band'))
- new_first_moment: float32 [2048, 62, 256], P(('view', 'band'))
- new_second_moment: float32 [2048, 62, 256], P(('view', 'band'))
- mean_loss: float32 [], replicated
- grads: float32 [2048, 62, 256], P(('view', 'band'))
The draws below stay inside these ranges and needn't reach their ends.
Inputs may be any that keep to these rules, and one draw needn't show every extreme that they name: Block k is held by device k // 16, devices counted with view slowest. Entry i of block_list[v, b] is a block for i < block_count[v, b] and -1 after; the live entries of one band are distinct, at most 1 of them are held by one device, and in every band some device holds exactly 1 of them. `block_count`: some band has exactly 16. tile_start < tile_end <= block_count of the band; tile_end - tile_start is at most 2, and exactly 2 for some tile of every band; the tiles of a band together cover every live position. `tile_end`: see tile_start. `gaussians`: component 9 of every Gaussian lies in [1, 2]; components 6 to 8 lie in [0, 2]. `camera`: A0 x A1 has a third entry of 0.6 or more.
All inputs are finite; a program needn't handle non-finite values.
Results may differ from the reference program's by a relative error of at most 0.0003.
Values sent between devices are 32-bit elements; how exact they have to be, the bound alone decides.
No kernel may reach another device: no remote copies, remote signals or barrier semaphores. Data moves between devices by JAX's collectives and lax.ppermute only.
A program may use at most 128 MiB of HBM per device.

```python
import math
import jax
import jax.numpy as jnp
import numpy as np
from jax import lax

PARAMS = 62
BLOCK = 256
TILE = 16
ROWS = 16
COLS = 128
BLK_DEV = 16
LIST = 16
TILE_MOST = 2
VIEWS = 32
BANDS = 4
IMG_ROWS = 64
NBLK = 2048
TILES = 8
CAP = 1
DEVICES = 128


def lists_helper(key):
    base_key = jax.random.fold_in(key, 7311)
    key_full, key_count, key_device = jax.random.split(base_key, 3)
    dev_total = VIEWS * BANDS
    slot_total = DEVICES * CAP
    counts = jax.random.randint(key_count, (dev_total,), 3 * LIST // 4, LIST + 1)
    full_device = jax.random.randint(key_full, (), 0, dev_total)
    counts = jnp.where(jnp.arange(dev_total) == full_device, LIST, counts)

    def draw_device(device_key, live_count):
        key_list = jax.random.split(device_key, 8)
        full_owner = jax.random.randint(key_list[0], (), 0, DEVICES)
        scores = jax.random.permutation(key_list[1], slot_total)
        slot_ids = jnp.arange(slot_total)
        scores = jnp.where(slot_ids // CAP == full_owner, scores - slot_total, scores)
        ranking = jnp.argsort(scores, stable=True)
        chosen = ranking[:LIST]
        half_list = LIST // 2
        front_half = chosen[:half_list][jax.random.permutation(key_list[2], half_list)]
        back_half = chosen[half_list:][jax.random.permutation(key_list[3], LIST - half_list)]
        chosen = jnp.concatenate([front_half, back_half])
        owners = chosen // CAP
        slot_rank = chosen % CAP
        local_perm = jax.vmap(lambda subkey: jax.random.permutation(subkey, BLK_DEV))(jax.random.split(key_list[4], DEVICES))
        local_ids = local_perm[owners, slot_rank]
        block_ids = owners * BLK_DEV + local_ids
        block_ids = jnp.where(jnp.arange(LIST) < live_count, block_ids, -1)
        tile_index = jnp.arange(TILES)
        low_end = tile_index * live_count // TILES
        high_end = (tile_index + 1) * live_count // TILES
        length = jax.random.randint(key_list[5], (TILES,), jnp.maximum(high_end - low_end, 1), TILE_MOST + 1)
        forced = jax.random.randint(key_list[6], (), 0, TILES)
        length = jnp.where(tile_index == forced, TILE_MOST, length)
        first_ok = jnp.maximum(0, high_end - length)
        last_ok = jnp.minimum(low_end, live_count - length)
        starts = jax.random.randint(key_list[7], (TILES,), first_ok, last_ok + 1)
        return (block_ids, starts, starts + length)
    block_ids, starts, endings = jax.vmap(draw_device)(jax.random.split(key_device, dev_total), counts)
    return (block_ids.reshape(VIEWS, BANDS, LIST).astype(jnp.int32), counts.reshape(VIEWS, BANDS).astype(jnp.int32), starts.reshape(VIEWS, BANDS, TILES).astype(jnp.int32), endings.reshape(VIEWS, BANDS, TILES).astype(jnp.int32))


def draw_block_list(key, part):
    return lists_helper(key)[0]


def draw_block_count(key, part):
    return lists_helper(key)[1]


def draw_tile_start(key, part):
    return lists_helper(key)[2]


def draw_tile_end(key, part):
    return lists_helper(key)[3]


def draw_gaussians(key, part):
    key_list = jax.random.split(jax.random.fold_in(key, 23), 8)
    grid_shape = (NBLK, BLOCK)
    extent = jnp.array([COLS * 1.0, IMG_ROWS * 1.0, 64.0], jnp.float32)[:, None, None]
    centre = jax.random.uniform(key_list[0], (3,) + grid_shape) * extent
    velocity = jnp.clip(2.0 * jax.random.normal(key_list[1], (3,) + grid_shape), -8.0, 8.0)
    log_scale = jax.random.uniform(key_list[2], (3,) + grid_shape, minval=math.log(1.2), maxval=math.log(4.0))
    quat_real = jax.random.uniform(key_list[3], (1,) + grid_shape, minval=1.0, maxval=2.0)
    quat_vec = jnp.clip(0.5 * jax.random.normal(key_list[4], (3,) + grid_shape), -2.0, 2.0)
    opacity = jax.random.uniform(key_list[5], (1,) + grid_shape, minval=-4.5, maxval=-2.5)
    sh_base = jnp.clip(0.6 * jax.random.normal(key_list[6], (3,) + grid_shape), -3.0, 3.0)
    sh_rest = jnp.clip(0.25 * jax.random.normal(key_list[7], (45,) + grid_shape), -1.5, 1.5)
    stacked = jnp.concatenate([centre, velocity, log_scale, quat_real, quat_vec, opacity, sh_base, sh_rest], axis=0)
    return stacked.transpose(1, 0, 2).astype(jnp.float32)


def draw_camera(key, part):
    key_list = jax.random.split(jax.random.fold_in(key, 41), 5)
    tilt_range = 0.3
    spin_angle = jax.random.uniform(key_list[0], (VIEWS,), minval=-0.15, maxval=0.15)
    tilt_a = jax.random.uniform(key_list[1], (VIEWS,), minval=-tilt_range, maxval=tilt_range)
    tilt_b = jax.random.uniform(key_list[2], (VIEWS,), minval=-tilt_range, maxval=tilt_range)
    zoom_factor = jax.random.uniform(key_list[3], (VIEWS,), minval=0.9, maxval=1.1)
    view_time = jax.random.uniform(key_list[4], (VIEWS,))
    row_top = zoom_factor[:, None] * jnp.stack([jnp.cos(spin_angle), -jnp.sin(spin_angle), tilt_a], axis=1)
    row_low = zoom_factor[:, None] * jnp.stack([jnp.sin(spin_angle), jnp.cos(spin_angle), tilt_b], axis=1)
    centre = jnp.array([COLS * 0.5, IMG_ROWS * 0.5, 32.0], jnp.float32)
    off_top = COLS * 0.5 - jnp.sum(row_top * centre[None, :], axis=1)
    off_low = IMG_ROWS * 0.5 - jnp.sum(row_low * centre[None, :], axis=1)
    return jnp.concatenate([row_top, row_low, off_top[:, None], off_low[:, None], view_time[:, None]], axis=1).astype(jnp.float32)


def block_scale(key, shape, pieces, low, top_value):
    loudness = 1.0
    for axis_at, blocks in pieces:
        heights = jax.random.uniform(jax.random.fold_in(jax.random.fold_in(key, 6), axis_at), (blocks,), jnp.float32, low / len(pieces), top_value / len(pieces))
        loudness = loudness * jnp.repeat(jnp.exp(heights), shape[axis_at] // blocks).reshape((-1,) + (1,) * (len(shape) - 1 - axis_at))
    return loudness


def noise(rng, shape, scale, reach, shards=(), held_as=jnp.bfloat16):
    entries = jax.random.normal(rng, shape, jnp.float32) * scale
    if len(shards) > 0:
        entries = block_scale(rng, shape, shards, -0.22, 0.18) * entries
    return jnp.clip(entries, min=-reach, max=reach).astype(held_as)


def setup_inputs(seed: int = 0) -> dict:
    key_of = jax.random.split(jax.random.key(seed), 10)
    return {
        "gaussians": draw_gaussians(jax.random.fold_in(key_of[9], 71), 0),
        "first_moment": noise(key_of[1], (NBLK, PARAMS, BLOCK), 0.1, 0.6, ((0, 128),), jnp.float32),
        "second_moment": jnp.clip(jnp.exp(math.log(0.1) - 6.9077553 * jax.random.uniform(key_of[2], (NBLK, PARAMS, BLOCK), jnp.float32) ** block_scale(key_of[2], (NBLK, PARAMS, BLOCK), ((0, 128),), -0.2, 0.2)), 0.0001, 0.1),
        "camera": draw_camera(jax.random.fold_in(key_of[9], 71), 0),
        "target": jnp.clip(1.0 * jax.random.uniform(key_of[4], (VIEWS, 3, IMG_ROWS, COLS), jnp.float32) ** block_scale(key_of[4], (VIEWS, 3, IMG_ROWS, COLS), ((0, 32), (2, 4)), -0.2, 0.2), 0.0, 1.0),
        "block_list": draw_block_list(jax.random.fold_in(key_of[9], 71), 0),
        "block_count": draw_block_count(jax.random.fold_in(key_of[9], 71), 0),
        "tile_start": draw_tile_start(jax.random.fold_in(key_of[9], 71), 0),
        "tile_end": draw_tile_end(jax.random.fold_in(key_of[9], 71), 0),
    }


HIGHEST_MODE = lax.Precision.HIGHEST
SSIM_WEIGHT = 0.2
ABS_WEIGHT = 0.8
STAB_MEAN = 0.0001
STAB_VAR = 0.0009
BIAS_FIRST = 1.0 - math.exp(100.0 * math.log(0.9))
BIAS_SECOND = 1.0 - math.exp(100.0 * math.log(0.999))
SH_ZERO = 0.28209479177387814
SH_ONE = 0.4886025119029199
SH_TWO = [1.0925484305920792, -1.0925484305920792, 0.31539156525252005, -1.0925484305920792, 0.5462742152960396]
SH_THREE = [-0.5900435899266435, 2.890611442640554, -0.4570457994644658, 0.3731763325901154, -0.4570457994644658, 1.445305721320277, -0.5900435899266435]

def learning_rates():
    return np.concatenate([np.full(6, 0.016), np.full(3, 0.005), np.full(4, 0.001), np.full(1, 0.05), np.full(3, 0.0025), np.full(45, 0.000125)]).astype(np.float32)

def kernel_taps():
    raw_taps = [math.exp(-(offset * offset) / 4.5) for offset in range(-5, 6)]
    tap_total = sum(raw_taps)
    return [raw_tap / tap_total for raw_tap in raw_taps]

def smooth(source, rows_out):
    kernel = kernel_taps()
    rows_done = kernel[0] * source[..., 0:rows_out, :]
    for offset in range(1, 11):
        rows_done = rows_done + kernel[offset] * source[..., offset:offset + rows_out, :]
    cols_n = source.shape[-1]
    padded = jnp.pad(rows_done, [(0, 0)] * (source.ndim - 1) + [(5, 5)])
    result = kernel[0] * padded[..., 0:cols_n]
    for offset in range(1, 11):
        result = result + kernel[offset] * padded[..., offset:offset + cols_n]
    return result

def ssim_value(mean_x, mean_y, square_x, square_y, cross_xy):
    var_x = square_x - mean_x * mean_x
    var_y = square_y - mean_y * mean_y
    covar = cross_xy - mean_x * mean_y
    upper = (2.0 * mean_x * mean_y + STAB_MEAN) * (2.0 * covar + STAB_VAR)
    lower = (mean_x * mean_x + mean_y * mean_y + STAB_MEAN) * (var_x + var_y + STAB_VAR)
    return upper / lower

def ssim_terms(pred_ext, target_ext, rows_out):
    mean_x = smooth(pred_ext, rows_out)
    mean_y = smooth(target_ext, rows_out)
    square_x = smooth(pred_ext * pred_ext, rows_out)
    square_y = smooth(target_ext * target_ext, rows_out)
    cross_xy = smooth(pred_ext * target_ext, rows_out)
    ssim_map, pullback = jax.vjp(ssim_value, mean_x, mean_y, square_x, square_y, cross_xy)
    partials = pullback(jnp.full_like(ssim_map, -SSIM_WEIGHT / 3.0))
    return (ssim_map, partials[0], partials[2], partials[4])

def harmonics(facing):
    dir_x, dir_y, dir_z = (facing[0], facing[1], facing[2])
    sq_x, sq_y, sq_z = (dir_x * dir_x, dir_y * dir_y, dir_z * dir_z)
    return jnp.stack([SH_ZERO + 0.0 * dir_x, -SH_ONE * dir_y, SH_ONE * dir_z, -SH_ONE * dir_x, SH_TWO[0] * dir_x * dir_y, SH_TWO[1] * dir_y * dir_z, SH_TWO[2] * (2.0 * sq_z - sq_x - sq_y), SH_TWO[3] * dir_x * dir_z, SH_TWO[4] * (sq_x - sq_y), SH_THREE[0] * dir_y * (3.0 * sq_x - sq_y), SH_THREE[1] * dir_x * dir_y * dir_z, SH_THREE[2] * dir_y * (4.0 * sq_z - sq_x - sq_y), SH_THREE[3] * dir_z * (2.0 * sq_z - 3.0 * sq_x - 3.0 * sq_y), SH_THREE[4] * dir_x * (4.0 * sq_z - sq_x - sq_y), SH_THREE[5] * dir_z * (sq_x - sq_y), SH_THREE[6] * dir_x * (sq_x - 3.0 * sq_y)])

def project(window, cam_row):
    affine = cam_row[0:6].reshape(2, 3)
    cam_time = cam_row[8]
    centre = [window[:, axis_k, :] + cam_time * window[:, 3 + axis_k, :] for axis_k in range(3)]
    col_pos = affine[0, 0] * centre[0] + affine[0, 1] * centre[1] + affine[0, 2] * centre[2] + cam_row[6]
    row_pos = affine[1, 0] * centre[0] + affine[1, 1] * centre[1] + affine[1, 2] * centre[2] + cam_row[7]
    scales = [jnp.exp(window[:, 6 + axis_k, :]) for axis_k in range(3)]
    quat_len = jnp.sqrt(window[:, 9, :] * window[:, 9, :] + window[:, 10, :] * window[:, 10, :] + window[:, 11, :] * window[:, 11, :] + window[:, 12, :] * window[:, 12, :])
    quat_r = window[:, 9, :] / quat_len
    quat_i = window[:, 10, :] / quat_len
    quat_j = window[:, 11, :] / quat_len
    quat_k = window[:, 12, :] / quat_len
    rotation = [[1.0 - 2.0 * (quat_j * quat_j + quat_k * quat_k), 2.0 * (quat_i * quat_j - quat_r * quat_k), 2.0 * (quat_i * quat_k + quat_r * quat_j)], [2.0 * (quat_i * quat_j + quat_r * quat_k), 1.0 - 2.0 * (quat_i * quat_i + quat_k * quat_k), 2.0 * (quat_j * quat_k - quat_r * quat_i)], [2.0 * (quat_i * quat_k - quat_r * quat_j), 2.0 * (quat_j * quat_k + quat_r * quat_i), 1.0 - 2.0 * (quat_i * quat_i + quat_j * quat_j)]]
    spread_rows = [[(affine[out_row, 0] * rotation[0][in_col] + affine[out_row, 1] * rotation[1][in_col] + affine[out_row, 2] * rotation[2][in_col]) * scales[in_col] for in_col in range(3)] for out_row in range(2)]
    conic_a = spread_rows[0][0] * spread_rows[0][0] + spread_rows[0][1] * spread_rows[0][1] + spread_rows[0][2] * spread_rows[0][2] + 0.3
    conic_b = spread_rows[0][0] * spread_rows[1][0] + spread_rows[0][1] * spread_rows[1][1] + spread_rows[0][2] * spread_rows[1][2]
    conic_c = spread_rows[1][0] * spread_rows[1][0] + spread_rows[1][1] * spread_rows[1][1] + spread_rows[1][2] * spread_rows[1][2] + 0.3
    determinant = conic_a * conic_c - conic_b * conic_b
    opacity = jax.nn.sigmoid(window[:, 13, :])
    normal = jnp.cross(affine[0], affine[1])
    facing = normal / jnp.sqrt(jnp.sum(normal * normal))
    sh_basis = harmonics(facing)
    sh_coef = window[:, 14:, :].reshape(window.shape[0], 16, 3, window.shape[2])
    colour = 0.5 + jnp.einsum('k,tkcb->ctb', sh_basis, sh_coef, precision=HIGHEST_MODE)
    return (col_pos, row_pos, conic_a, conic_b, conic_c, determinant, opacity, colour)

def render_tile(window, cam_row, first_pos, live_low, live_high, row_start, col_start):
    window_len = window.shape[0]
    block_len = window.shape[2]
    col_pos, row_pos, conic_a, conic_b, conic_c, determinant, opacity, colour = project(window, cam_row)
    positions = first_pos + jnp.arange(window_len, dtype=jnp.int32)
    is_live = (positions >= live_low) & (positions < live_high)
    live_flat = jnp.repeat(is_live, block_len)
    pixels = jnp.arange(TILE * TILE, dtype=jnp.int32)
    pix_row = (row_start + pixels // TILE).astype(jnp.float32) + 0.5
    pix_col = (col_start + pixels % TILE).astype(jnp.float32) + 0.5
    delta_col = pix_col[None, :] - col_pos.reshape(-1)[:, None]
    delta_row = pix_row[None, :] - row_pos.reshape(-1)[:, None]
    exponent = -0.5 * (conic_c.reshape(-1)[:, None] * delta_col * delta_col - 2.0 * conic_b.reshape(-1)[:, None] * delta_col * delta_row + conic_a.reshape(-1)[:, None] * delta_row * delta_row) / determinant.reshape(-1)[:, None]
    alphas = jnp.where(live_flat[:, None], opacity.reshape(-1)[:, None] * jnp.exp(exponent), 0.0)
    keep_log = jnp.log1p(-alphas).reshape(window_len, block_len, -1)
    inner_sum = jnp.cumsum(keep_log, axis=1)
    block_total = inner_sum[:, -1, :]
    outer_sum = jnp.cumsum(block_total, axis=0) - block_total
    log_trans = inner_sum - keep_log + outer_sum[:, None, :]
    weight = alphas * jnp.exp(log_trans.reshape(window_len * block_len, -1))
    return jnp.dot(colour.reshape(3, -1), weight, precision=HIGHEST_MODE)

def tile_frame(tile_index, starts, list_len, row_base):
    tile_cols = COLS // TILE
    first_pos = jnp.minimum(starts[tile_index], list_len - TILE_MOST).astype(jnp.int32)
    row_start = row_base + tile_index // tile_cols * TILE
    col_start = tile_index % tile_cols * TILE
    return (first_pos, row_start, col_start)

def from_tiles(tiles_out):
    tile_rows = ROWS // TILE
    tile_cols = COLS // TILE
    return tiles_out.reshape(tile_rows, tile_cols, 3, TILE, TILE).transpose(2, 0, 3, 1, 4).reshape(3, ROWS, COLS)

def to_tiles(image):
    tile_rows = ROWS // TILE
    tile_cols = COLS // TILE
    return image.reshape(3, tile_rows, TILE, tile_cols, TILE).transpose(1, 3, 0, 2, 4).reshape(tile_rows * tile_cols, 3, TILE * TILE)

def render_band(listed, cam_row, starts, endings, row_base):
    list_len = listed.shape[0]

    def draw_tile(tile_index):
        first_pos, row_start, col_start = tile_frame(tile_index, starts, list_len, row_base)
        window = lax.dynamic_slice_in_dim(listed, first_pos, TILE_MOST, 0)
        return render_tile(window, cam_row, first_pos, starts[tile_index], endings[tile_index], row_start, col_start)
    tiles_out = lax.map(draw_tile, jnp.arange(starts.shape[0], dtype=jnp.int32))
    return from_tiles(tiles_out)

def backward_band(listed, cam_row, starts, endings, row_base, grad_pred):
    list_len = listed.shape[0]
    cot_tiles = to_tiles(grad_pred)

    def tile_back(summed, tile_index):
        first_pos, row_start, col_start = tile_frame(tile_index, starts, list_len, row_base)
        window = lax.dynamic_slice_in_dim(listed, first_pos, TILE_MOST, 0)

        def draw_window(chosen):
            return render_tile(chosen, cam_row, first_pos, starts[tile_index], endings[tile_index], row_start, col_start)
        unused, pullback = jax.vjp(draw_window, window)
        grad_window = pullback(cot_tiles[tile_index])[0]
        current = lax.dynamic_slice_in_dim(summed, first_pos, TILE_MOST, 0)
        summed = lax.dynamic_update_slice_in_dim(summed, current + grad_window, first_pos, 0)
        return (summed, None)
    summed, unused = lax.scan(tile_back, jnp.zeros_like(listed), jnp.arange(starts.shape[0], dtype=jnp.int32))
    return summed

def image_loss(pred_img, target_img):
    pad_rows = [(0, 0), (5, 5), (0, 0)]
    ssim_map, part_mean, part_square, part_cross = ssim_terms(jnp.pad(pred_img, pad_rows), jnp.pad(target_img, pad_rows), IMG_ROWS)
    adjoint = jnp.pad(jnp.stack([part_mean, part_square, part_cross]), [(0, 0), (0, 0), (5, 5), (0, 0)])
    spread = smooth(adjoint, IMG_ROWS)
    error_map = pred_img - target_img
    grad_pred = ABS_WEIGHT / 3.0 * jnp.sign(error_map) + spread[0] + 2.0 * pred_img * spread[1] + target_img * spread[2]
    summed = jnp.sum(ABS_WEIGHT / 3.0 * jnp.abs(error_map) + SSIM_WEIGHT / 3.0 * (1.0 - ssim_map))
    return (summed, grad_pred)

def adam_update(params, moment_one, moment_two, gradient):
    learn_rates = jnp.asarray(learning_rates())[None, :, None]
    new_one = 0.9 * moment_one + 0.1 * gradient
    new_two = 0.999 * moment_two + 0.001 * gradient * gradient
    change = learn_rates * (new_one / BIAS_FIRST) / (jnp.sqrt(new_two / BIAS_SECOND) + 1e-08)
    return (params - change, new_one, new_two)

def reference(gaussians, first_moment, second_moment, camera, target, block_list, block_count, tile_start, tile_end):
    nblk_total = gaussians.shape[0]
    list_len = block_list.shape[2]
    dev_total = VIEWS * BANDS
    list_rows = block_list.reshape(dev_total, list_len)
    counts = block_count.reshape(dev_total)
    starts = tile_start.reshape(dev_total, -1)
    endings = tile_end.reshape(dev_total, -1)
    position = jnp.arange(list_len, dtype=jnp.int32)

    def fetch(device):
        safe_ids = jnp.where(position < counts[device], list_rows[device], 0).astype(jnp.int32)
        return jnp.take(gaussians, safe_ids, axis=0)

    def render_device(device):
        view_index = device // BANDS
        band_index = device % BANDS
        return render_band(fetch(device), camera[view_index], starts[device], endings[device], band_index * ROWS)
    rendered = lax.map(render_device, jnp.arange(dev_total, dtype=jnp.int32))
    images = rendered.reshape(VIEWS, BANDS, 3, ROWS, COLS).transpose(0, 2, 1, 3, 4).reshape(VIEWS, 3, IMG_ROWS, COLS)
    totals, grad_images = jax.vmap(image_loss)(images, target)
    mean_loss = jnp.sum(totals) / (VIEWS * IMG_ROWS * COLS)
    grad_bands = grad_images.reshape(VIEWS, 3, BANDS, ROWS, COLS).transpose(0, 2, 1, 3, 4).reshape(dev_total, 3, ROWS, COLS)

    def accumulate(summed, device):
        view_index = device // BANDS
        band_index = device % BANDS
        grads_list = backward_band(fetch(device), camera[view_index], starts[device], endings[device], band_index * ROWS, grad_bands[device])
        target_rows = jnp.where(position < counts[device], list_rows[device], nblk_total).astype(jnp.int32)
        summed = summed.at[target_rows].add(grads_list, mode='drop')
        return (summed, None)
    gradient, unused = lax.scan(accumulate, jnp.zeros_like(gaussians), jnp.arange(dev_total, dtype=jnp.int32))
    new_params, new_one, new_two = adam_update(gaussians, first_moment, second_moment, gradient)
    return (new_params, new_one, new_two, mean_loss, gradient)
```

```python
import math

import jax
import jax.numpy as jnp
import numpy as np
from jax import lax
from jax.experimental import pallas as pl
from jax.experimental.pallas import tpu as pltpu
from jax.sharding import PartitionSpec as P

TILE = 16
ROWS = 16
COLS = 128
TILES = 8
LIST = 16
BLOCK = 256
BLK_DEV = 16
DEVICES = 128
BANDS = 4
COMPS = 62
TILE_MOST = 2
GAUSS = TILE_MOST * BLOCK
HALO = 10
EXT = 40
RECORD = 9 * BLOCK
SLOT = RECORD + 128
ASK = 128
IMG_ROWS = BANDS * ROWS
AXES = ("view", "band")

HIGHEST_MODE = lax.Precision.HIGHEST
SSIM_WEIGHT = 0.2
ABS_WEIGHT = 0.8
STAB_MEAN = 0.0001
STAB_VAR = 0.0009
BIAS_FIRST = 1.0 - math.exp(100.0 * math.log(0.9))
BIAS_SECOND = 1.0 - math.exp(100.0 * math.log(0.999))
SH_ZERO = 0.28209479177387814
SH_ONE = 0.4886025119029199
SH_TWO = [
    1.0925484305920792,
    -1.0925484305920792,
    0.31539156525252005,
    -1.0925484305920792,
    0.5462742152960396,
]
SH_THREE = [
    -0.5900435899266435,
    2.890611442640554,
    -0.4570457994644658,
    0.3731763325901154,
    -0.4570457994644658,
    1.445305721320277,
    -0.5900435899266435,
]

W_ID = 0
W_CAM = 1
W_SH = 10
W_CA = 26
W_CB = 32
W_CC = 38

SMEM = pltpu.SMEM
VMEM = pltpu.VMEM


def spec(space):
    return pl.BlockSpec(memory_space=space)


def params(mib):
    return pltpu.CompilerParams(vmem_limit_bytes=mib * 1024 * 1024)


def kernel_taps():
    raw_taps = [math.exp(-(offset * offset) / 4.5) for offset in range(-5, 6)]
    tap_total = sum(raw_taps)
    return [raw_tap / tap_total for raw_tap in raw_taps]


def tap_matrices():
    taps = kernel_taps()
    first = np.zeros((32, EXT), np.float32)
    for r in range(ROWS + 10):
        for o in range(11):
            first[r, r + o] = taps[o]
    second = np.zeros((ROWS, 32), np.float32)
    for r in range(ROWS):
        for o in range(11):
            second[r, r + o] = taps[o]
    across = np.zeros((COLS, COLS), np.float32)
    for c in range(COLS):
        for o in range(11):
            if 0 <= c + o - 5 < COLS:
                across[c + o - 5, c] = taps[o]
    return first, second, across


def learning_rates():
    return np.concatenate(
        [
            np.full(6, 0.016),
            np.full(3, 0.005),
            np.full(4, 0.001),
            np.full(1, 0.05),
            np.full(3, 0.0025),
            np.full(45, 0.000125),
        ]
    ).astype(np.float32)


def harmonics(dir_x, dir_y, dir_z):
    sq_x, sq_y, sq_z = (dir_x * dir_x, dir_y * dir_y, dir_z * dir_z)
    return [
        SH_ZERO + 0.0 * dir_x,
        -SH_ONE * dir_y,
        SH_ONE * dir_z,
        -SH_ONE * dir_x,
        SH_TWO[0] * dir_x * dir_y,
        SH_TWO[1] * dir_y * dir_z,
        SH_TWO[2] * (2.0 * sq_z - sq_x - sq_y),
        SH_TWO[3] * dir_x * dir_z,
        SH_TWO[4] * (sq_x - sq_y),
        SH_THREE[0] * dir_y * (3.0 * sq_x - sq_y),
        SH_THREE[1] * dir_x * dir_y * dir_z,
        SH_THREE[2] * dir_y * (4.0 * sq_z - sq_x - sq_y),
        SH_THREE[3] * dir_z * (2.0 * sq_z - 3.0 * sq_x - 3.0 * sq_y),
        SH_THREE[4] * dir_x * (4.0 * sq_z - sq_x - sq_y),
        SH_THREE[5] * dir_z * (sq_x - sq_y),
        SH_THREE[6] * dir_x * (sq_x - 3.0 * sq_y),
    ]


def request_kernel(list_ref, count_ref, cam_ref, out_ref):
    cam = [jnp.full((1, ASK), cam_ref[0, i], jnp.float32) for i in range(9)]
    a, b = cam[0:3], cam[3:6]
    normal = [
        a[1] * b[2] - a[2] * b[1],
        a[2] * b[0] - a[0] * b[2],
        a[0] * b[1] - a[1] * b[0],
    ]
    size = jnp.sqrt(normal[0] * normal[0] + normal[1] * normal[1] + normal[2] * normal[2])
    basis = harmonics(normal[0] / size, normal[1] / size, normal[2] / size)
    pairs = [(0, 0), (0, 1), (0, 2), (1, 1), (1, 2), (2, 2)]

    def product(p, q):
        return [p[i] * q[i] if i == j else p[i] * q[j] + p[j] * q[i] for i, j in pairs]

    words = [jnp.full((1, ASK), -1.0, jnp.float32)] + cam + basis
    words = words + product(a, a) + product(a, b) + product(b, b)
    lane = lax.broadcasted_iota(jnp.int32, (1, ASK), 1)
    row = jnp.zeros((1, ASK), jnp.float32)
    for i, word in enumerate(words):
        row = jnp.where(lane == i, word, row)

    def fill(s, carry):
        out_ref[s] = row
        return carry

    lax.fori_loop(0, DEVICES, fill, 0, unroll=8)
    for i in range(LIST):

        @pl.when(i < count_ref[0, 0])
        def _(i=i):
            block = list_ref[0, 0, i]
            local = jnp.full((1, ASK), block % BLK_DEV, jnp.int32).astype(jnp.float32)
            out_ref[block // BLK_DEV] = jnp.where(lane == 0, local, row)


def shape_terms(g_ref):
    squares = [jnp.exp(2.0 * g_ref[:, 6 + c, :]) for c in range(3)]
    quat = [g_ref[:, 9 + c, :] for c in range(4)]
    size = jnp.sqrt(quat[0] * quat[0] + quat[1] * quat[1] + quat[2] * quat[2] + quat[3] * quat[3])
    r, x, y, z = [q / size for q in quat]
    rotation = [
        [1.0 - 2.0 * (y * y + z * z), 2.0 * (x * y - r * z), 2.0 * (x * z + r * y)],
        [2.0 * (x * y + r * z), 1.0 - 2.0 * (x * x + z * z), 2.0 * (y * z - r * x)],
        [2.0 * (x * z - r * y), 2.0 * (y * z + r * x), 1.0 - 2.0 * (x * x + y * y)],
    ]
    return squares, rotation, (r, x, y, z), size


def records_kernel(ask_ref, g_ref, out_ref, shape_ref):
    squares, rot, unused, unused_size = shape_terms(g_ref)
    at = 0
    for i in range(3):
        for j in range(i, 3):
            shape_ref[at] = (
                rot[i][0] * rot[j][0] * squares[0]
                + rot[i][1] * rot[j][1] * squares[1]
                + rot[i][2] * rot[j][2] * squares[2]
            )
            at += 1
    shape_ref[6] = 1.0 / (1.0 + jnp.exp(-g_ref[:, 13, :]))

    def slot(s, carry):
        local = ask_ref[s, 0, W_ID]

        @pl.when(local >= 0.0)
        def _():
            k = local.astype(jnp.int32)

            def word(i):
                return ask_ref[s, 0, i]

            def comp(i):
                return g_ref[k, pl.ds(i, 1), :]

            def put(p, value):
                out_ref[s, :, pl.ds(p * BLOCK, BLOCK)] = value

            time = word(W_CAM + 8)
            centre = [comp(c) + time * comp(3 + c) for c in range(3)]
            for p in range(2):
                put(
                    p,
                    word(W_CAM + 3 * p) * centre[0]
                    + word(W_CAM + 3 * p + 1) * centre[1]
                    + word(W_CAM + 3 * p + 2) * centre[2]
                    + word(W_CAM + 6 + p),
                )
            shapes = [shape_ref[i, pl.ds(k, 1), :] for i in range(6)]
            for p, (at, extra) in enumerate(((W_CA, 0.3), (W_CB, 0.0), (W_CC, 0.3))):
                total = word(at) * shapes[0]
                for i in range(1, 6):
                    total = total + word(at + i) * shapes[i]
                put(2 + p, total + extra)
            put(5, shape_ref[6, pl.ds(k, 1), :])
            colour = word(W_SH) * g_ref[k, pl.ds(14, 3), :]
            for q in range(1, 16):
                colour = colour + word(W_SH + q) * g_ref[k, pl.ds(14 + 3 * q, 3), :]
            colour = colour + 0.5
            for ch in range(3):
                put(6 + ch, colour[ch : ch + 1])

        return carry

    lax.fori_loop(0, DEVICES, slot, 0)


def pixel_rows(row_base):
    px = lax.broadcasted_iota(jnp.int32, (ROWS, COLS), 1).astype(jnp.float32) + 0.5
    py = lax.broadcasted_iota(jnp.int32, (ROWS, COLS), 0).astype(jnp.float32) + 0.5
    return px, py + row_base.astype(jnp.float32)


def row_of(ref, p, i):
    return jnp.broadcast_to(ref[p, pl.ds(i, 1), :], (ROWS, COLS))


def alpha_of(table, i, px, py):
    dx = px - row_of(table, 0, i)
    dy = py - row_of(table, 1, i)
    power = row_of(table, 2, i) * dx * dx + dy * (
        row_of(table, 3, i) * dx + row_of(table, 4, i) * dy
    )
    return row_of(table, 5, i) * jnp.exp(power)


def render_kernel(
    list_ref, start_ref, end_ref, base_ref, got_ref, pred_ref, compact_ref, table_ref
):
    for t in range(TILES):
        first = start_ref[0, 0, t]
        last = end_ref[0, 0, t]
        for j in range(TILE_MOST):
            live = first + j < last
            place = jnp.where(live, first + j, first)
            owner = list_ref[0, 0, place] // BLK_DEV
            there = jnp.where(live, 1.0, 0.0)
            for p in range(9):
                row = got_ref[owner, :, pl.ds(p * BLOCK, BLOCK)]
                if p == 5:
                    row = row * there
                compact_ref[p, pl.ds(t, 1), pl.ds(j * BLOCK, BLOCK)] = row
    ca, cb, cc = compact_ref[2], compact_ref[3], compact_ref[4]
    det = ca * cc - cb * cb
    forms = [
        compact_ref[0],
        compact_ref[1],
        -0.5 * cc / det,
        cb / det,
        -0.5 * ca / det,
        compact_ref[5],
        compact_ref[6],
        compact_ref[7],
        compact_ref[8],
    ]
    for p, form in enumerate(forms):
        wide = jnp.broadcast_to(form[:, None, :], (TILES, TILE, GAUSS)).reshape(COLS, GAUSS)
        table_ref[p] = wide.T
    px, py = pixel_rows(base_ref[0])

    def blend(i, carry):
        trans, red, green, blue = carry
        weight = alpha_of(table_ref, i, px, py) * trans
        return (
            trans - weight,
            red + weight * row_of(table_ref, 6, i),
            green + weight * row_of(table_ref, 7, i),
            blue + weight * row_of(table_ref, 8, i),
        )

    zero = jnp.zeros((ROWS, COLS), jnp.float32)
    done = lax.fori_loop(0, GAUSS, blend, (zero + 1.0, zero, zero, zero), unroll=8)
    for ch in range(3):
        pred_ref[ch] = done[1 + ch]


def ssim_value(mean_x, mean_y, square_x, square_y, cross_xy):
    var_x = square_x - mean_x * mean_x
    var_y = square_y - mean_y * mean_y
    covar = cross_xy - mean_x * mean_y
    upper = (2.0 * mean_x * mean_y + STAB_MEAN) * (2.0 * covar + STAB_VAR)
    lower = (mean_x * mean_x + mean_y * mean_y + STAB_MEAN) * (var_x + var_y + STAB_VAR)
    return upper / lower


def exact_dot(a, b):
    return jnp.dot(a, b, precision=HIGHEST_MODE, preferred_element_type=jnp.float32)


def loss_gradient(
    base, pred_ref, target_ref, before_ref, after_ref, first_ref, second_ref, across_ref, ext_ref
):
    ext_ref[...] = jnp.zeros(ext_ref.shape, jnp.float32)
    for part, mine in enumerate((pred_ref, target_ref)):
        for ch in range(3):
            ext_ref[part, ch, pl.ds(0, HALO), :] = before_ref[part, ch]
            ext_ref[part, ch, pl.ds(HALO, ROWS), :] = mine[ch]
            ext_ref[part, ch, pl.ds(HALO + ROWS, HALO), :] = after_ref[part, ch]
    first, second, across = first_ref[...], second_ref[...], across_ref[...]
    row = lax.broadcasted_iota(jnp.int32, (32, COLS), 0)
    image_row = row + base - 5
    inside = (image_row >= 0) & (image_row < IMG_ROWS) & (row < ROWS + 10)
    total = jnp.zeros((ROWS, COLS), jnp.float32)
    slopes = []
    for ch in range(3):
        x, y = ext_ref[0, ch], ext_ref[1, ch]
        maps = jnp.concatenate([x, y, x * x, y * y, x * y], axis=0)
        maps = exact_dot(maps, across)
        smooth = [exact_dot(first, maps[EXT * m : EXT * (m + 1)]) for m in range(5)]
        value, pullback = jax.vjp(ssim_value, *smooth)
        parts = pullback(jnp.full_like(value, -SSIM_WEIGHT / 3.0))
        adjoint = [jnp.where(inside, parts[m], 0.0) for m in (0, 2, 4)]
        back = [exact_dot(second, part) for part in adjoint]
        back = exact_dot(jnp.concatenate(back, axis=0), across)
        pred, target = pred_ref[ch], target_ref[ch]
        error = pred - target
        sign = jnp.where(error > 0.0, 1.0, jnp.where(error < 0.0, -1.0, 0.0))
        slopes.append(
            ABS_WEIGHT / 3.0 * sign
            + back[0:ROWS]
            + 2.0 * pred * back[ROWS : 2 * ROWS]
            + target * back[2 * ROWS : 3 * ROWS]
        )
        total = total + (
            ABS_WEIGHT / 3.0 * jnp.abs(error)
            + SSIM_WEIGHT / 3.0 * (1.0 - value[5 : 5 + ROWS])
        )
    total = jnp.sum(jnp.sum(total, axis=1, keepdims=True), axis=0, keepdims=True)
    return total, slopes


def backward_kernel(
    list_ref,
    start_ref,
    end_ref,
    base_ref,
    pred_ref,
    target_ref,
    before_ref,
    after_ref,
    first_ref,
    second_ref,
    across_ref,
    seg_ref,
    compact_ref,
    table_ref,
    out_ref,
    ext_ref,
    alpha_ref,
    trans_ref,
    part_ref,
    moment_ref,
    grad_ref,
):
    total, slopes = loss_gradient(
        base_ref[0],
        pred_ref,
        target_ref,
        before_ref,
        after_ref,
        first_ref,
        second_ref,
        across_ref,
        ext_ref,
    )
    loss_row = jnp.broadcast_to(total, (1, 128))
    empty = jnp.zeros((1, RECORD), jnp.float32)

    def clear(s, carry):
        out_ref[s, :, pl.ds(RECORD, 128)] = loss_row
        out_ref[s, :, pl.ds(0, RECORD)] = empty
        return carry

    lax.fori_loop(0, DEVICES, clear, 0, unroll=4)
    px, py = pixel_rows(base_ref[0])

    def forward(i, trans):
        alpha = alpha_of(table_ref, i, px, py)
        alpha_ref[i] = alpha
        trans_ref[i] = trans
        return trans - alpha * trans

    one = jnp.ones((ROWS, COLS), jnp.float32)
    lax.fori_loop(0, GAUSS, forward, one, unroll=8)
    py_top, py_low = py[0:8], py[8:16]

    def fold(value):
        return value[0:8] + value[8:16]

    def reverse(step, behind):
        chunk = GAUSS // 8 - 1 - step
        for r in range(7, -1, -1):
            i = chunk * 8 + r
            alpha = alpha_ref[i]
            trans = trans_ref[i]
            weight = alpha * trans
            seen = (
                row_of(table_ref, 6, i) * slopes[0]
                + row_of(table_ref, 7, i) * slopes[1]
                + row_of(table_ref, 8, i) * slopes[2]
            )
            ahead = seen - behind
            behind = behind + alpha * ahead
            d_power = weight * ahead
            dy = py - row_of(table_ref, 1, i)
            d_row = d_power * dy
            part_ref[0, pl.ds(8 * r, 8), :] = fold(d_power)
            part_ref[1, pl.ds(8 * r, 8), :] = fold(d_row)
            part_ref[2, pl.ds(8 * r, 8), :] = fold(d_row * dy)
            for ch in range(3):
                part_ref[3 + ch, pl.ds(8 * r, 8), :] = fold(weight * slopes[ch])
        sums = []
        for p in range(6):
            piece = part_ref[p, pl.ds(0, 8, stride=8), :]
            for s in range(1, 8):
                piece = piece + part_ref[p, pl.ds(s, 8, stride=8), :]
            sums.append(piece)
        here = pl.ds(pl.multiple_of(chunk * 8, 8), 8)
        dx = px[0:8] - table_ref[0, here, :]
        first_x = sums[0] * dx
        moment_ref[0, here, :] = sums[0]
        moment_ref[1, here, :] = first_x
        moment_ref[2, here, :] = first_x * dx
        moment_ref[3, here, :] = sums[1]
        moment_ref[4, here, :] = sums[1] * dx
        moment_ref[5, here, :] = sums[2]
        for ch in range(3):
            moment_ref[6 + ch, here, :] = sums[3 + ch]
        return behind

    lax.fori_loop(0, GAUSS // 8, reverse, jnp.zeros((ROWS, COLS), jnp.float32))
    seg = seg_ref[...]
    m = [
        lax.dot_general(
            seg,
            moment_ref[p],
            (((1,), (1,)), ((), ())),
            precision=HIGHEST_MODE,
            preferred_element_type=jnp.float32,
        )
        for p in range(9)
    ]
    ca, cb, cc = compact_ref[2], compact_ref[3], compact_ref[4]
    inverse = 1.0 / (ca * cc - cb * cb)
    d_inverse = -0.5 * cc * m[2] + cb * m[4] - 0.5 * ca * m[5]
    d_det = -inverse * inverse * d_inverse
    grad_ref[0] = (cc * m[1] - cb * m[3]) * inverse
    grad_ref[1] = (ca * m[3] - cb * m[1]) * inverse
    grad_ref[2] = -0.5 * inverse * m[5] + cc * d_det
    grad_ref[3] = inverse * m[4] - 2.0 * cb * d_det
    grad_ref[4] = -0.5 * inverse * m[2] + ca * d_det
    grad_ref[5] = m[0]
    for ch in range(3):
        grad_ref[6 + ch] = m[6 + ch]
    for t in range(TILES):
        first = start_ref[0, 0, t]
        for j in range(TILE_MOST):

            @pl.when(first + j < end_ref[0, 0, t])
            def _(t=t, j=j, first=first):
                owner = list_ref[0, 0, first + j] // BLK_DEV
                for p in range(9):
                    lanes = pl.ds(p * BLOCK, BLOCK)
                    out_ref[owner, :, lanes] = (
                        out_ref[owner, :, lanes]
                        + grad_ref[p, pl.ds(t, 1), pl.ds(j * BLOCK, BLOCK)]
                    )


def pullback_kernel(ask_ref, g_ref, got_ref, grad_ref, loss_ref, shape_ref):
    losses = got_ref[:, :, pl.ds(RECORD, 128)]
    loss_ref[...] = jnp.sum(losses, axis=0) * (1.0 / (DEVICES * ROWS * COLS))
    grad_ref[...] = jnp.zeros(grad_ref.shape, jnp.float32)
    shape_ref[...] = jnp.zeros(shape_ref.shape, jnp.float32)

    def slot(s, carry):
        local = ask_ref[s, 0, W_ID]

        @pl.when(local >= 0.0)
        def _():
            k = local.astype(jnp.int32)

            def word(i):
                return ask_ref[s, 0, i]

            d = [got_ref[s, :, pl.ds(p * BLOCK, BLOCK)] for p in range(9)]
            time = word(W_CAM + 8)
            for c in range(3):
                d_centre = word(W_CAM + c) * d[0] + word(W_CAM + 3 + c) * d[1]
                grad_ref[k, pl.ds(c, 1), :] = grad_ref[k, pl.ds(c, 1), :] + d_centre
                grad_ref[k, pl.ds(3 + c, 1), :] = grad_ref[k, pl.ds(3 + c, 1), :] + time * d_centre
            here = pl.ds(k, 1)
            for i in range(6):
                shape_ref[i, here, :] = shape_ref[i, here, :] + (
                    word(W_CA + i) * d[2] + word(W_CB + i) * d[3] + word(W_CC + i) * d[4]
                )
            shape_ref[6, here, :] = shape_ref[6, here, :] + d[5]
            colour = jnp.concatenate(d[6:9], axis=0)
            for q in range(16):
                at = pl.ds(14 + 3 * q, 3)
                grad_ref[k, at, :] = grad_ref[k, at, :] + word(W_SH + q) * colour

        return carry

    lax.fori_loop(0, DEVICES, slot, 0)
    squares, rot, quat, size = shape_terms(g_ref)
    s00, s01, s02, s11, s12, s22 = [shape_ref[i] for i in range(6)]
    twice = [[2.0 * s00, s01, s02], [s01, 2.0 * s11, s12], [s02, s12, 2.0 * s22]]
    d_rot = [[None] * 3 for _ in range(3)]
    for c in range(3):
        pulled = [
            twice[i][0] * rot[0][c] + twice[i][1] * rot[1][c] + twice[i][2] * rot[2][c]
            for i in range(3)
        ]
        along = rot[0][c] * pulled[0] + rot[1][c] * pulled[1] + rot[2][c] * pulled[2]
        grad_ref[:, 6 + c, :] = squares[c] * along
        for i in range(3):
            d_rot[i][c] = pulled[i] * squares[c]
    r, x, y, z = quat
    n = d_rot
    d_r = 2.0 * (
        -z * n[0][1] + y * n[0][2] + z * n[1][0] - x * n[1][2] - y * n[2][0] + x * n[2][1]
    )
    d_x = 2.0 * (
        y * n[0][1] + z * n[0][2] + y * n[1][0] - 2.0 * x * n[1][1] - r * n[1][2]
        + z * n[2][0] + r * n[2][1] - 2.0 * x * n[2][2]
    )
    d_y = 2.0 * (
        -2.0 * y * n[0][0] + x * n[0][1] + r * n[0][2] + x * n[1][0] + z * n[1][2]
        - r * n[2][0] + z * n[2][1] - 2.0 * y * n[2][2]
    )
    d_z = 2.0 * (
        -2.0 * z * n[0][0] - r * n[0][1] + x * n[0][2] + r * n[1][0] - 2.0 * z * n[1][1]
        + y * n[1][2] + x * n[2][0] + y * n[2][1]
    )
    d_quat = [d_r, d_x, d_y, d_z]
    along = r * d_r + x * d_x + y * d_y + z * d_z
    for c in range(4):
        grad_ref[:, 9 + c, :] = (d_quat[c] - quat[c] * along) / size
    opacity = 1.0 / (1.0 + jnp.exp(-g_ref[:, 13, :]))
    grad_ref[:, 13, :] = shape_ref[6] * (1.0 - opacity)


def adam_update(gaussians, moment_one, moment_two, gradient):
    learn_rates = jnp.asarray(learning_rates())[None, :, None]
    new_one = 0.9 * moment_one + 0.1 * gradient
    new_two = 0.999 * moment_two + 0.001 * gradient * gradient
    change = learn_rates * (new_one / BIAS_FIRST) / (jnp.sqrt(new_two / BIAS_SECOND) + 1e-08)
    return (gaussians - change, new_one, new_two)


def shaped(*shape):
    return jax.ShapeDtypeStruct(shape, jnp.float32)


def exchanged(slots):
    return lax.all_to_all(slots, AXES, split_axis=0, concat_axis=0, tiled=True)


def halo(array):
    up = [(i, i + 1) for i in range(BANDS - 1)]
    down = [(i + 1, i) for i in range(BANDS - 1)]
    before = lax.ppermute(array[:, ROWS - HALO :], "band", up)
    after = lax.ppermute(array[:, :HALO], "band", down)
    return before, after


def per_device(
    gaussians,
    first_moment,
    second_moment,
    camera,
    target,
    block_list,
    block_count,
    tile_start,
    tile_end,
):
    base = (lax.axis_index("band") * ROWS).astype(jnp.int32).reshape(1)
    request = pl.pallas_call(
        request_kernel,
        in_specs=[spec(SMEM)] * 3,
        out_specs=spec(VMEM),
        out_shape=shaped(DEVICES, 1, ASK),
        name="request",
    )(block_list, block_count, camera)
    asked = exchanged(request)
    target_band = target[0]
    target_before, target_after = halo(target_band)
    records = pl.pallas_call(
        records_kernel,
        in_specs=[spec(SMEM), spec(VMEM)],
        out_specs=spec(VMEM),
        out_shape=shaped(DEVICES, 1, RECORD),
        scratch_shapes=[VMEM((7, BLK_DEV, BLOCK), jnp.float32)],
        compiler_params=params(32),
        name="records",
    )(asked, gaussians)
    received = exchanged(records)
    pred, compact, table = pl.pallas_call(
        render_kernel,
        in_specs=[spec(SMEM)] * 4 + [spec(VMEM)],
        out_specs=[spec(VMEM)] * 3,
        out_shape=[
            shaped(3, ROWS, COLS),
            shaped(9, TILES, GAUSS),
            shaped(9, GAUSS, COLS),
        ],
        compiler_params=params(32),
        name="render",
    )(block_list, tile_start, tile_end, base, received)
    pred_before, pred_after = halo(pred)
    first, second, across = tap_matrices()
    seg = (np.arange(COLS)[None, :] // TILE == np.arange(TILES)[:, None]).astype(np.float32)
    outgoing = pl.pallas_call(
        backward_kernel,
        in_specs=[spec(SMEM)] * 4 + [spec(VMEM)] * 10,
        out_specs=spec(VMEM),
        out_shape=shaped(DEVICES, 1, SLOT),
        scratch_shapes=[
            VMEM((2, 3, EXT, COLS), jnp.float32),
            VMEM((GAUSS, ROWS, COLS), jnp.float32),
            VMEM((GAUSS, ROWS, COLS), jnp.float32),
            VMEM((6, 64, COLS), jnp.float32),
            VMEM((9, GAUSS, COLS), jnp.float32),
            VMEM((9, TILES, GAUSS), jnp.float32),
        ],
        compiler_params=params(48),
        name="backward",
    )(
        block_list,
        tile_start,
        tile_end,
        base,
        pred,
        target_band,
        jnp.stack([pred_before, target_before]),
        jnp.stack([pred_after, target_after]),
        first,
        second,
        across,
        seg,
        compact,
        table,
    )
    incoming = exchanged(outgoing)
    gradient, loss = pl.pallas_call(
        pullback_kernel,
        in_specs=[spec(SMEM)] + [spec(VMEM)] * 2,
        out_specs=[spec(VMEM)] * 2,
        out_shape=[shaped(BLK_DEV, COMPS, BLOCK), shaped(1, 128)],
        scratch_shapes=[VMEM((7, BLK_DEV, BLOCK), jnp.float32)],
        compiler_params=params(32),
        name="pullback",
    )(asked, gaussians, incoming)
    new_params, new_one, new_two = adam_update(gaussians, first_moment, second_moment, gradient)
    return (new_params, new_one, new_two, loss[0, 0], gradient)


def solution(mesh):
    return jax.shard_map(
        per_device,
        mesh=mesh,
        in_specs=(
            P(AXES, None, None),
            P(AXES, None, None),
            P(AXES, None, None),
            P("view", None),
            P("view", None, "band", None),
            P("view", "band", None),
            P("view", "band"),
            P("view", "band", None),
            P("view", "band", None),
        ),
        out_specs=(
            P(AXES, None, None),
            P(AXES, None, None),
            P(AXES, None, None),
            P(),
            P(AXES, None, None),
        ),
        check_vma=False,
    )
```

```python
import math

import jax
import jax.numpy as jnp
import numpy as np
from jax import lax
from jax.experimental import pallas as pl
from jax.experimental.pallas import tpu as pltpu
from jax.sharding import PartitionSpec as P

TILE = 16
ROWS = 16
COLS = 128
TILES = 8
LIST = 16
BLOCK = 256
BLK_DEV = 16
DEVICES = 128
BANDS = 4
COMPS = 62
TILE_MOST = 2
GAUSS = TILE_MOST * BLOCK
HALO = 10
EXT = 40
RECORD = 9 * BLOCK
SLOT = RECORD + 128
ASK = 128
UNROLL = 4
KEPT = 18
IMG_ROWS = BANDS * ROWS
AXES = ("view", "band")

HIGHEST_MODE = lax.Precision.HIGHEST
SSIM_WEIGHT = 0.2
ABS_WEIGHT = 0.8
STAB_MEAN = 0.0001
STAB_VAR = 0.0009
BIAS_FIRST = 1.0 - math.exp(100.0 * math.log(0.9))
BIAS_SECOND = 1.0 - math.exp(100.0 * math.log(0.999))
SH_ZERO = 0.28209479177387814
SH_ONE = 0.4886025119029199
SH_TWO = [
    1.0925484305920792,
    -1.0925484305920792,
    0.31539156525252005,
    -1.0925484305920792,
    0.5462742152960396,
]
SH_THREE = [
    -0.5900435899266435,
    2.890611442640554,
    -0.4570457994644658,
    0.3731763325901154,
    -0.4570457994644658,
    1.445305721320277,
    -0.5900435899266435,
]

W_ID = 0
W_CAM = 1
W_SH = 10
W_CA = 26
W_CB = 32
W_CC = 38

SMEM = pltpu.SMEM
VMEM = pltpu.VMEM


def spec(space):
    return pl.BlockSpec(memory_space=space)


def params(mib):
    return pltpu.CompilerParams(vmem_limit_bytes=mib * 1024 * 1024)


def kernel_taps():
    raw_taps = [math.exp(-(offset * offset) / 4.5) for offset in range(-5, 6)]
    tap_total = sum(raw_taps)
    return [raw_tap / tap_total for raw_tap in raw_taps]


def tap_matrices():
    taps = kernel_taps()
    first = np.zeros((32, EXT), np.float32)
    for r in range(ROWS + 10):
        for o in range(11):
            first[r, r + o] = taps[o]
    second = np.zeros((ROWS, 32), np.float32)
    for r in range(ROWS):
        for o in range(11):
            second[r, r + o] = taps[o]
    across = np.zeros((COLS, COLS), np.float32)
    for c in range(COLS):
        for o in range(11):
            if 0 <= c + o - 5 < COLS:
                across[c + o - 5, c] = taps[o]
    return first, second, across


def learning_rates():
    return np.concatenate(
        [
            np.full(6, 0.016),
            np.full(3, 0.005),
            np.full(4, 0.001),
            np.full(1, 0.05),
            np.full(3, 0.0025),
            np.full(45, 0.000125),
        ]
    ).astype(np.float32)


def harmonics(dir_x, dir_y, dir_z):
    sq_x, sq_y, sq_z = (dir_x * dir_x, dir_y * dir_y, dir_z * dir_z)
    return [
        SH_ZERO + 0.0 * dir_x,
        -SH_ONE * dir_y,
        SH_ONE * dir_z,
        -SH_ONE * dir_x,
        SH_TWO[0] * dir_x * dir_y,
        SH_TWO[1] * dir_y * dir_z,
        SH_TWO[2] * (2.0 * sq_z - sq_x - sq_y),
        SH_TWO[3] * dir_x * dir_z,
        SH_TWO[4] * (sq_x - sq_y),
        SH_THREE[0] * dir_y * (3.0 * sq_x - sq_y),
        SH_THREE[1] * dir_x * dir_y * dir_z,
        SH_THREE[2] * dir_y * (4.0 * sq_z - sq_x - sq_y),
        SH_THREE[3] * dir_z * (2.0 * sq_z - 3.0 * sq_x - 3.0 * sq_y),
        SH_THREE[4] * dir_x * (4.0 * sq_z - sq_x - sq_y),
        SH_THREE[5] * dir_z * (sq_x - sq_y),
        SH_THREE[6] * dir_x * (sq_x - 3.0 * sq_y),
    ]


def request_kernel(list_ref, count_ref, cam_ref, out_ref):
    cam = [jnp.full((1, ASK), cam_ref[0, i], jnp.float32) for i in range(9)]
    a, b = cam[0:3], cam[3:6]
    normal = [
        a[1] * b[2] - a[2] * b[1],
        a[2] * b[0] - a[0] * b[2],
        a[0] * b[1] - a[1] * b[0],
    ]
    size = jnp.sqrt(normal[0] * normal[0] + normal[1] * normal[1] + normal[2] * normal[2])
    basis = harmonics(normal[0] / size, normal[1] / size, normal[2] / size)
    pairs = [(0, 0), (0, 1), (0, 2), (1, 1), (1, 2), (2, 2)]

    def product(p, q):
        return [p[i] * q[i] if i == j else p[i] * q[j] + p[j] * q[i] for i, j in pairs]

    words = [jnp.full((1, ASK), -1.0, jnp.float32)] + cam + basis
    words = words + product(a, a) + product(a, b) + product(b, b)
    lane = lax.broadcasted_iota(jnp.int32, (1, ASK), 1)
    row = jnp.zeros((1, ASK), jnp.float32)
    for i, word in enumerate(words):
        row = jnp.where(lane == i, word, row)

    def fill(s, carry):
        out_ref[s] = row
        return carry

    lax.fori_loop(0, DEVICES, fill, 0, unroll=8)
    for i in range(LIST):

        @pl.when(i < count_ref[0, 0])
        def _(i=i):
            block = list_ref[0, 0, i]
            local = jnp.full((1, ASK), block % BLK_DEV, jnp.int32).astype(jnp.float32)
            out_ref[block // BLK_DEV] = jnp.where(lane == 0, local, row)


def component(ref, c):
    return ref[c]


def shape_terms(g_ref):
    squares = [jnp.exp(2.0 * component(g_ref, 6 + c)) for c in range(3)]
    quat = [component(g_ref, 9 + c) for c in range(4)]
    size = jnp.sqrt(quat[0] * quat[0] + quat[1] * quat[1] + quat[2] * quat[2] + quat[3] * quat[3])
    r, x, y, z = [q / size for q in quat]
    rotation = [
        [1.0 - 2.0 * (y * y + z * z), 2.0 * (x * y - r * z), 2.0 * (x * z + r * y)],
        [2.0 * (x * y + r * z), 1.0 - 2.0 * (x * x + z * z), 2.0 * (y * z - r * x)],
        [2.0 * (x * z - r * y), 2.0 * (y * z + r * x), 1.0 - 2.0 * (x * x + y * y)],
    ]
    return squares, rotation, (r, x, y, z), size


def opacity_of(g_ref):
    return 1.0 / (1.0 + jnp.exp(-component(g_ref, 13)))


def shapes_kernel(g_ref, shape_ref, kept_ref):
    squares, rot, quat, size = shape_terms(g_ref)
    opacity = opacity_of(g_ref)
    kept = squares + rot[0] + rot[1] + rot[2] + list(quat) + [1.0 / size, 1.0 - opacity]
    for i, value in enumerate(kept):
        kept_ref[i] = value
    at = 0
    for i in range(3):
        for j in range(i, 3):
            shape_ref[at] = (
                rot[i][0] * rot[j][0] * squares[0]
                + rot[i][1] * rot[j][1] * squares[1]
                + rot[i][2] * rot[j][2] * squares[2]
            )
            at += 1
    shape_ref[6] = opacity


def listed_slots(ask_ref, order_ref):
    def look(s, found):
        order_ref[found] = s
        return found + jnp.where(ask_ref[s, 0, W_ID] >= 0.0, 1, 0)

    return lax.fori_loop(0, DEVICES, look, 0, unroll=8)


def records_kernel(ask_ref, g_ref, shape_ref, out_ref, order_ref, count_ref):
    count = listed_slots(ask_ref, order_ref)
    count_ref[0] = count

    def slot(n, carry):
        s = order_ref[n]
        k = ask_ref[s, 0, W_ID].astype(jnp.int32)

        def word(i):
            return ask_ref[s, 0, i]

        def comp(i):
            return g_ref[i, pl.ds(k, 1), :]

        def put(p, value):
            out_ref[s, :, pl.ds(p * BLOCK, BLOCK)] = value

        time = word(W_CAM + 8)
        centre = [comp(c) + time * comp(3 + c) for c in range(3)]
        for p in range(2):
            put(
                p,
                word(W_CAM + 3 * p) * centre[0]
                + word(W_CAM + 3 * p + 1) * centre[1]
                + word(W_CAM + 3 * p + 2) * centre[2]
                + word(W_CAM + 6 + p),
            )
        shapes = [shape_ref[i, pl.ds(k, 1), :] for i in range(6)]
        for p, (at, extra) in enumerate(((W_CA, 0.3), (W_CB, 0.0), (W_CC, 0.3))):
            total = word(at) * shapes[0]
            for i in range(1, 6):
                total = total + word(at + i) * shapes[i]
            put(2 + p, total + extra)
        put(5, shape_ref[6, pl.ds(k, 1), :])
        basis = [word(W_SH + q) for q in range(16)]
        for ch in range(3):
            colour = basis[0] * comp(14 + ch)
            for q in range(1, 16):
                colour = colour + basis[q] * comp(14 + 3 * q + ch)
            put(6 + ch, colour + 0.5)
        return carry

    lax.fori_loop(0, count, slot, 0)


def pixel_rows(row_base):
    px = lax.broadcasted_iota(jnp.int32, (ROWS, COLS), 1).astype(jnp.float32) + 0.5
    py = lax.broadcasted_iota(jnp.int32, (ROWS, COLS), 0).astype(jnp.float32) + 0.5
    return px, py + row_base.astype(jnp.float32)


def row_of(ref, p, i):
    return jnp.broadcast_to(ref[p, pl.ds(i, 1), :], (ROWS, COLS))


def alpha_of(table, i, px, py):
    dx = px - row_of(table, 0, i)
    dy = py - row_of(table, 1, i)
    power = row_of(table, 2, i) * dx * dx + dy * (
        row_of(table, 3, i) * dx + row_of(table, 4, i) * dy
    )
    return row_of(table, 5, i) * jnp.exp(power)


def render_kernel(
    list_ref,
    start_ref,
    end_ref,
    base_ref,
    got_ref,
    pred_ref,
    compact_ref,
    table_ref,
    alpha_ref,
    weight_ref,
):
    for t in range(TILES):
        first = start_ref[0, 0, t]
        last = end_ref[0, 0, t]
        for j in range(TILE_MOST):
            live = first + j < last
            place = jnp.where(live, first + j, first)
            owner = list_ref[0, 0, place] // BLK_DEV
            there = jnp.where(live, 1.0, 0.0)
            for p in range(9):
                row = got_ref[owner, :, pl.ds(p * BLOCK, BLOCK)]
                if p == 5:
                    row = row * there
                compact_ref[p, pl.ds(t, 1), pl.ds(j * BLOCK, BLOCK)] = row
    ca, cb, cc = compact_ref[2], compact_ref[3], compact_ref[4]
    det = ca * cc - cb * cb
    forms = [
        compact_ref[0],
        compact_ref[1],
        -0.5 * cc / det,
        cb / det,
        -0.5 * ca / det,
        compact_ref[5],
        compact_ref[6],
        compact_ref[7],
        compact_ref[8],
    ]
    for p, form in enumerate(forms):
        wide = jnp.broadcast_to(form[:, None, :], (TILES, TILE, GAUSS)).reshape(COLS, GAUSS)
        table_ref[p] = wide.T
    px, py = pixel_rows(base_ref[0])

    def blend(i, carry):
        trans, red, green, blue = carry
        alpha = alpha_of(table_ref, i, px, py)
        weight = alpha * trans
        alpha_ref[i] = alpha
        weight_ref[i] = weight
        return (
            trans - weight,
            red + weight * row_of(table_ref, 6, i),
            green + weight * row_of(table_ref, 7, i),
            blue + weight * row_of(table_ref, 8, i),
        )

    zero = jnp.zeros((ROWS, COLS), jnp.float32)
    done = lax.fori_loop(0, GAUSS, blend, (zero + 1.0, zero, zero, zero), unroll=16)
    for ch in range(3):
        pred_ref[ch] = done[1 + ch]


def ssim_value(mean_x, mean_y, square_x, square_y, cross_xy):
    var_x = square_x - mean_x * mean_x
    var_y = square_y - mean_y * mean_y
    covar = cross_xy - mean_x * mean_y
    upper = (2.0 * mean_x * mean_y + STAB_MEAN) * (2.0 * covar + STAB_VAR)
    lower = (mean_x * mean_x + mean_y * mean_y + STAB_MEAN) * (var_x + var_y + STAB_VAR)
    return upper / lower


def exact_dot(a, b):
    return jnp.dot(a, b, precision=HIGHEST_MODE, preferred_element_type=jnp.float32)


def extended(mine, before, after):
    rest = jnp.zeros((EXT - ROWS - 2 * HALO, COLS), jnp.float32)
    return jnp.concatenate([before, mine, after, rest], axis=0)


def smoothed(maps, first, across):
    wide = exact_dot(jnp.concatenate(maps, axis=0), across)
    return [exact_dot(first, wide[EXT * m : EXT * (m + 1)]) for m in range(len(maps))]


def target_kernel(target_ref, before_ref, after_ref, first_ref, across_ref, ext_ref, maps_ref):
    first, across = first_ref[...], across_ref[...]
    for ch in range(3):
        y = extended(target_ref[ch], before_ref[ch], after_ref[ch])
        ext_ref[ch] = y
        maps_ref[ch, 0], maps_ref[ch, 1] = smoothed([y, y * y], first, across)


def loss_gradient(
    base, pred_ref, before_ref, after_ref, target_ref, maps_ref, first_ref, second_ref, across_ref
):
    first, second, across = first_ref[...], second_ref[...], across_ref[...]
    row = lax.broadcasted_iota(jnp.int32, (32, COLS), 0)
    image_row = row + base - 5
    inside = (image_row >= 0) & (image_row < IMG_ROWS) & (row < ROWS + 10)
    total = jnp.zeros((ROWS, COLS), jnp.float32)
    slopes = []
    for ch in range(3):
        pred = pred_ref[ch]
        x, y = extended(pred, before_ref[ch], after_ref[ch]), target_ref[ch]
        mean, square, cross = smoothed([x, x * x, x * y], first, across)
        smooth = [mean, maps_ref[ch, 0], square, maps_ref[ch, 1], cross]
        value, pullback = jax.vjp(ssim_value, *smooth)
        parts = pullback(jnp.full_like(value, -SSIM_WEIGHT / 3.0))
        adjoint = [jnp.where(inside, parts[m], 0.0) for m in (0, 2, 4)]
        back = [exact_dot(second, part) for part in adjoint]
        back = exact_dot(jnp.concatenate(back, axis=0), across)
        target = y[HALO : HALO + ROWS]
        error = pred - target
        sign = jnp.where(error > 0.0, 1.0, jnp.where(error < 0.0, -1.0, 0.0))
        slopes.append(
            ABS_WEIGHT / 3.0 * sign
            + back[0:ROWS]
            + 2.0 * pred * back[ROWS : 2 * ROWS]
            + target * back[2 * ROWS : 3 * ROWS]
        )
        total = total + (
            ABS_WEIGHT / 3.0 * jnp.abs(error)
            + SSIM_WEIGHT / 3.0 * (1.0 - value[5 : 5 + ROWS])
        )
    total = jnp.sum(jnp.sum(total, axis=1, keepdims=True), axis=0, keepdims=True)
    return total, slopes


def backward_kernel(
    list_ref,
    count_ref,
    start_ref,
    end_ref,
    base_ref,
    pred_ref,
    before_ref,
    after_ref,
    target_ref,
    maps_ref,
    first_ref,
    second_ref,
    across_ref,
    seg_ref,
    compact_ref,
    table_ref,
    alpha_ref,
    weight_ref,
    out_ref,
    part_ref,
    moment_ref,
    grad_ref,
):
    total, slopes = loss_gradient(
        base_ref[0],
        pred_ref,
        before_ref,
        after_ref,
        target_ref,
        maps_ref,
        first_ref,
        second_ref,
        across_ref,
    )
    loss_row = jnp.broadcast_to(total, (1, 128))
    empty = jnp.zeros((1, RECORD), jnp.float32)

    def tell(s, carry):
        out_ref[s, :, pl.ds(RECORD, 128)] = loss_row
        return carry

    lax.fori_loop(0, DEVICES, tell, 0, unroll=8)

    def clear(i, carry):
        out_ref[list_ref[0, 0, i] // BLK_DEV, :, pl.ds(0, RECORD)] = empty
        return carry

    lax.fori_loop(0, count_ref[0, 0], clear, 0)
    px, py = pixel_rows(base_ref[0])

    def fold(value):
        return value[0:8] + value[8:16]

    def reverse(step, behind):
        for half in range(UNROLL - 1, -1, -1):
            chunk = GAUSS // 8 - UNROLL * (step + 1) + half
            for r in range(7, -1, -1):
                i = chunk * 8 + r
                alpha = alpha_ref[i]
                weight = weight_ref[i]
                seen = (
                    row_of(table_ref, 6, i) * slopes[0]
                    + row_of(table_ref, 7, i) * slopes[1]
                    + row_of(table_ref, 8, i) * slopes[2]
                )
                ahead = seen - behind
                behind = behind + alpha * ahead
                d_power = weight * ahead
                dy = py - row_of(table_ref, 1, i)
                d_row = d_power * dy
                part_ref[half, 0, pl.ds(8 * r, 8), :] = fold(d_power)
                part_ref[half, 1, pl.ds(8 * r, 8), :] = fold(d_row)
                part_ref[half, 2, pl.ds(8 * r, 8), :] = fold(d_row * dy)
                for ch in range(3):
                    part_ref[half, 3 + ch, pl.ds(8 * r, 8), :] = fold(weight * slopes[ch])
            sums = []
            for p in range(6):
                piece = part_ref[half, p, pl.ds(0, 8, stride=8), :]
                for s in range(1, 8):
                    piece = piece + part_ref[half, p, pl.ds(s, 8, stride=8), :]
                sums.append(piece)
            here = pl.ds(pl.multiple_of(chunk * 8, 8), 8)
            dx = px[0:8] - table_ref[0, here, :]
            first_x = sums[0] * dx
            moment_ref[0, here, :] = sums[0]
            moment_ref[1, here, :] = first_x
            moment_ref[2, here, :] = first_x * dx
            moment_ref[3, here, :] = sums[1]
            moment_ref[4, here, :] = sums[1] * dx
            moment_ref[5, here, :] = sums[2]
            for ch in range(3):
                moment_ref[6 + ch, here, :] = sums[3 + ch]
        return behind

    lax.fori_loop(0, GAUSS // 8 // UNROLL, reverse, jnp.zeros((ROWS, COLS), jnp.float32))
    seg = seg_ref[...].astype(jnp.bfloat16)

    def over_tile(value):
        return lax.dot_general(
            seg, value, (((1,), (1,)), ((), ())), preferred_element_type=jnp.float32
        )

    m = []
    for p in range(9):
        value = moment_ref[p]
        large = value.astype(jnp.bfloat16)
        small = (value - large.astype(jnp.float32)).astype(jnp.bfloat16)
        m.append(over_tile(large) + over_tile(small))
    ca, cb, cc = compact_ref[2], compact_ref[3], compact_ref[4]
    inverse = 1.0 / (ca * cc - cb * cb)
    d_inverse = -0.5 * cc * m[2] + cb * m[4] - 0.5 * ca * m[5]
    d_det = -inverse * inverse * d_inverse
    grad_ref[0] = (cc * m[1] - cb * m[3]) * inverse
    grad_ref[1] = (ca * m[3] - cb * m[1]) * inverse
    grad_ref[2] = -0.5 * inverse * m[5] + cc * d_det
    grad_ref[3] = inverse * m[4] - 2.0 * cb * d_det
    grad_ref[4] = -0.5 * inverse * m[2] + ca * d_det
    grad_ref[5] = m[0]
    for ch in range(3):
        grad_ref[6 + ch] = m[6 + ch]
    for t in range(TILES):
        first = start_ref[0, 0, t]
        for j in range(TILE_MOST):

            @pl.when(first + j < end_ref[0, 0, t])
            def _(t=t, j=j, first=first):
                owner = list_ref[0, 0, first + j] // BLK_DEV
                for p in range(9):
                    lanes = pl.ds(p * BLOCK, BLOCK)
                    out_ref[owner, :, lanes] = (
                        out_ref[owner, :, lanes]
                        + grad_ref[p, pl.ds(t, 1), pl.ds(j * BLOCK, BLOCK)]
                    )


def update_kernel(
    order_ref,
    count_ref,
    ask_ref,
    kept_ref,
    g_ref,
    one_ref,
    two_ref,
    got_ref,
    loss_ref,
    new_out,
    one_out,
    two_out,
    grad_out,
    new_ref,
    new_one_ref,
    new_two_ref,
    grad_ref,
    shape_ref,
    done_sem,
):
    rates = [float(rate) / BIAS_FIRST for rate in learning_rates()]
    copies = []

    def finish(low, high):
        for c in range(low, high):
            gradient = grad_ref[c]
            new_one = 0.9 * one_ref[c] + 0.1 * gradient
            new_two = 0.999 * two_ref[c] + 0.001 * gradient * gradient
            root = jnp.sqrt(new_two * (1.0 / BIAS_SECOND)) + 1e-08
            new_ref[c] = g_ref[c] - rates[c] * new_one / root
            new_one_ref[c] = new_one
            new_two_ref[c] = new_two
        here = pl.ds(low, high - low)
        for held, out in (
            (new_ref, new_out),
            (new_one_ref, one_out),
            (new_two_ref, two_out),
            (grad_ref, grad_out),
        ):
            copy = pltpu.make_async_copy(held.at[here], out.at[here], done_sem.at[len(copies)])
            copy.start()
            copies.append(copy)

    losses = got_ref[:, :, pl.ds(RECORD, 128)]
    loss_ref[...] = jnp.sum(losses, axis=0) * (1.0 / (DEVICES * ROWS * COLS))
    grad_ref[...] = jnp.zeros(grad_ref.shape, jnp.float32)
    shape_ref[...] = jnp.zeros(shape_ref.shape, jnp.float32)
    count = count_ref[0]

    def slot(n, carry):
        s = order_ref[n]
        k = ask_ref[s, 0, W_ID].astype(jnp.int32)

        def word(i):
            return ask_ref[s, 0, i]

        here = pl.ds(k, 1)

        def add(c, value):
            grad_ref[c, here, :] = grad_ref[c, here, :] + value

        d = [got_ref[s, :, pl.ds(p * BLOCK, BLOCK)] for p in range(9)]
        time = word(W_CAM + 8)
        for c in range(3):
            d_centre = word(W_CAM + c) * d[0] + word(W_CAM + 3 + c) * d[1]
            add(c, d_centre)
            add(3 + c, time * d_centre)
        for i in range(6):
            shape_ref[i, here, :] = shape_ref[i, here, :] + (
                word(W_CA + i) * d[2] + word(W_CB + i) * d[3] + word(W_CC + i) * d[4]
            )
        shape_ref[6, here, :] = shape_ref[6, here, :] + d[5]
        for q in range(16):
            basis = word(W_SH + q)
            for ch in range(3):
                add(14 + 3 * q + ch, basis * d[6 + ch])
        return carry

    lax.fori_loop(0, count, slot, 0)
    for low, high in ((14, 30), (30, 46), (46, COMPS)):
        finish(low, high)
    squares = [kept_ref[c] for c in range(3)]
    rot = [[kept_ref[3 + 3 * i + c] for c in range(3)] for i in range(3)]
    quat = [kept_ref[12 + c] for c in range(4)]
    s00, s01, s02, s11, s12, s22 = [shape_ref[i] for i in range(6)]
    twice = [[2.0 * s00, s01, s02], [s01, 2.0 * s11, s12], [s02, s12, 2.0 * s22]]
    d_rot = [[None] * 3 for _ in range(3)]

    def put(c, value):
        grad_ref[c] = value

    for c in range(3):
        pulled = [
            twice[i][0] * rot[0][c] + twice[i][1] * rot[1][c] + twice[i][2] * rot[2][c]
            for i in range(3)
        ]
        along = rot[0][c] * pulled[0] + rot[1][c] * pulled[1] + rot[2][c] * pulled[2]
        put(6 + c, squares[c] * along)
        for i in range(3):
            d_rot[i][c] = pulled[i] * squares[c]
    r, x, y, z = quat
    n = d_rot
    d_r = 2.0 * (
        -z * n[0][1] + y * n[0][2] + z * n[1][0] - x * n[1][2] - y * n[2][0] + x * n[2][1]
    )
    d_x = 2.0 * (
        y * n[0][1] + z * n[0][2] + y * n[1][0] - 2.0 * x * n[1][1] - r * n[1][2]
        + z * n[2][0] + r * n[2][1] - 2.0 * x * n[2][2]
    )
    d_y = 2.0 * (
        -2.0 * y * n[0][0] + x * n[0][1] + r * n[0][2] + x * n[1][0] + z * n[1][2]
        - r * n[2][0] + z * n[2][1] - 2.0 * y * n[2][2]
    )
    d_z = 2.0 * (
        -2.0 * z * n[0][0] - r * n[0][1] + x * n[0][2] + r * n[1][0] - 2.0 * z * n[1][1]
        + y * n[1][2] + x * n[2][0] + y * n[2][1]
    )
    d_quat = [d_r, d_x, d_y, d_z]
    along = r * d_r + x * d_x + y * d_y + z * d_z
    for c in range(4):
        put(9 + c, (d_quat[c] - quat[c] * along) * kept_ref[16])
    put(13, shape_ref[6] * kept_ref[17])
    finish(0, 14)
    for copy in copies:
        copy.wait()


def shaped(*shape):
    return jax.ShapeDtypeStruct(shape, jnp.float32)


def exchanged(slots):
    return lax.all_to_all(slots, AXES, split_axis=0, concat_axis=0, tiled=True)


def halo(array):
    up = [(i, i + 1) for i in range(BANDS - 1)]
    down = [(i + 1, i) for i in range(BANDS - 1)]
    before = lax.ppermute(array[:, ROWS - HALO :], "band", up)
    after = lax.ppermute(array[:, :HALO], "band", down)
    return before, after


def per_device(
    gaussians,
    first_moment,
    second_moment,
    camera,
    target,
    block_list,
    block_count,
    tile_start,
    tile_end,
):
    flat, flat_one, flat_two = [
        jnp.transpose(a, (1, 0, 2))
        for a in (gaussians, first_moment, second_moment)
    ]
    first, second, across = tap_matrices()
    base = (lax.axis_index("band") * ROWS).astype(jnp.int32).reshape(1)
    request = pl.pallas_call(
        request_kernel,
        in_specs=[spec(SMEM)] * 3,
        out_specs=spec(VMEM),
        out_shape=shaped(DEVICES, 1, ASK),
        name="request",
    )(block_list, block_count, camera)
    asked = exchanged(request)
    target_band = target[0]
    shapes, kept = pl.pallas_call(
        shapes_kernel,
        in_specs=[spec(VMEM)],
        out_specs=[spec(VMEM)] * 2,
        out_shape=[shaped(7, BLK_DEV, BLOCK), shaped(KEPT, BLK_DEV, BLOCK)],
        compiler_params=params(16),
        name="shapes",
    )(flat)
    asked, shapes, kept = lax.optimization_barrier((asked, shapes, kept))
    records, order, count = pl.pallas_call(
        records_kernel,
        in_specs=[spec(SMEM), spec(VMEM), spec(VMEM)],
        out_specs=[spec(VMEM), spec(SMEM), spec(SMEM)],
        out_shape=[
            shaped(DEVICES, 1, RECORD),
            jax.ShapeDtypeStruct((DEVICES + 1,), jnp.int32),
            jax.ShapeDtypeStruct((1,), jnp.int32),
        ],
        compiler_params=params(16),
        name="records",
    )(asked, flat, shapes)
    records, target_band = lax.optimization_barrier((records, target_band))
    received = exchanged(records)
    target_ext, target_maps = pl.pallas_call(
        target_kernel,
        in_specs=[spec(VMEM)] * 5,
        out_specs=[spec(VMEM)] * 2,
        out_shape=[shaped(3, EXT, COLS), shaped(3, 2, 32, COLS)],
        compiler_params=params(16),
        name="target",
    )(target_band, *halo(target_band), first, across)
    received, target_ext, target_maps = lax.optimization_barrier(
        (received, target_ext, target_maps)
    )
    pred, compact, table, alpha, weight = pl.pallas_call(
        render_kernel,
        in_specs=[spec(SMEM)] * 4 + [spec(VMEM)],
        out_specs=[spec(VMEM)] * 5,
        out_shape=[
            shaped(3, ROWS, COLS),
            shaped(9, TILES, GAUSS),
            shaped(9, GAUSS, COLS),
            shaped(GAUSS, ROWS, COLS),
            shaped(GAUSS, ROWS, COLS),
        ],
        compiler_params=params(16),
        name="render",
    )(block_list, tile_start, tile_end, base, received)
    pred_before, pred_after = halo(pred)
    seg = (np.arange(COLS)[None, :] // TILE == np.arange(TILES)[:, None]).astype(np.float32)
    outgoing = pl.pallas_call(
        backward_kernel,
        in_specs=[spec(SMEM)] * 5 + [spec(VMEM)] * 13,
        out_specs=spec(VMEM),
        out_shape=shaped(DEVICES, 1, SLOT),
        scratch_shapes=[
            VMEM((UNROLL, 6, 64, COLS), jnp.float32),
            VMEM((9, GAUSS, COLS), jnp.float32),
            VMEM((9, TILES, GAUSS), jnp.float32),
        ],
        compiler_params=params(16),
        name="backward",
    )(
        block_list,
        block_count,
        tile_start,
        tile_end,
        base,
        pred,
        pred_before,
        pred_after,
        target_ext,
        target_maps,
        first,
        second,
        across,
        seg,
        compact,
        table,
        alpha,
        weight,
    )
    incoming = exchanged(outgoing)
    loss, *flats = pl.pallas_call(
        update_kernel,
        in_specs=[spec(SMEM)] * 3 + [spec(VMEM)] * 5,
        out_specs=[spec(VMEM)] + [spec(pl.ANY)] * 4,
        out_shape=[shaped(1, 128)] + [shaped(COMPS, BLK_DEV, BLOCK)] * 4,
        scratch_shapes=[VMEM((COMPS, BLK_DEV, BLOCK), jnp.float32)] * 4
        + [VMEM((7, BLK_DEV, BLOCK), jnp.float32), pltpu.SemaphoreType.DMA((16,))],
        compiler_params=params(16),
        name="update",
    )(order, count, asked, kept, flat, flat_one, flat_two, incoming)
    new_params, new_one, new_two, gradient = [jnp.transpose(a, (1, 0, 2)) for a in flats]
    return (new_params, new_one, new_two, loss[0, 0], gradient)


def solution(mesh):
    return jax.shard_map(
        per_device,
        mesh=mesh,
        in_specs=(
            P(AXES, None, None),
            P(AXES, None, None),
            P(AXES, None, None),
            P("view", None),
            P("view", None, "band", None),
            P("view", "band", None),
            P("view", "band"),
            P("view", "band", None),
            P("view", "band", None),
        ),
        out_specs=(
            P(AXES, None, None),
            P(AXES, None, None),
            P(AXES, None, None),
            P(),
            P(AXES, None, None),
        ),
        check_vma=False,
    )
```

```python
import math

import jax
import jax.numpy as jnp
import numpy as np
from jax import lax
from jax.experimental import pallas as pl
from jax.experimental.pallas import tpu as pltpu
from jax.sharding import PartitionSpec as P

TILE = 16
ROWS = 16
COLS = 128
TILES = 8
LIST = 16
BLOCK = 256
BLK_DEV = 16
DEVICES = 128
BANDS = 4
COMPS = 62
TILE_MOST = 2
GAUSS = TILE_MOST * BLOCK
HALO = 10
EXT = 40
RECORD = 9 * BLOCK
SLOT = RECORD + 128
ASK = 128
UNROLL = 4
KEPT = 18
IMG_ROWS = BANDS * ROWS
AXES = ("view", "band")

HIGHEST_MODE = lax.Precision.HIGHEST
SSIM_WEIGHT = 0.2
ABS_WEIGHT = 0.8
STAB_MEAN = 0.0001
STAB_VAR = 0.0009
BIAS_FIRST = 1.0 - math.exp(100.0 * math.log(0.9))
BIAS_SECOND = 1.0 - math.exp(100.0 * math.log(0.999))
SH_ZERO = 0.28209479177387814
SH_ONE = 0.4886025119029199
SH_TWO = [
    1.0925484305920792,
    -1.0925484305920792,
    0.31539156525252005,
    -1.0925484305920792,
    0.5462742152960396,
]
SH_THREE = [
    -0.5900435899266435,
    2.890611442640554,
    -0.4570457994644658,
    0.3731763325901154,
    -0.4570457994644658,
    1.445305721320277,
    -0.5900435899266435,
]

W_ID = 0
W_CAM = 1
W_SH = 10
WORDS = 32

LOG2_E = math.log2(math.e)

SMEM = pltpu.SMEM
VMEM = pltpu.VMEM


def spec(space):
    return pl.BlockSpec(memory_space=space)


def params(mib):
    return pltpu.CompilerParams(vmem_limit_bytes=mib * 1024 * 1024)


def kernel_taps():
    raw_taps = [math.exp(-(offset * offset) / 4.5) for offset in range(-5, 6)]
    tap_total = sum(raw_taps)
    return [raw_tap / tap_total for raw_tap in raw_taps]


def tap_matrices():
    taps = kernel_taps()
    first = np.zeros((32, EXT), np.float32)
    for r in range(ROWS + 10):
        for o in range(11):
            first[r, r + o] = taps[o]
    second = np.zeros((ROWS, 32), np.float32)
    for r in range(ROWS):
        for o in range(11):
            second[r, r + o] = taps[o]
    across = np.zeros((COLS, COLS), np.float32)
    for c in range(COLS):
        for o in range(11):
            if 0 <= c + o - 5 < COLS:
                across[c + o - 5, c] = taps[o]
    return first, second, across


def learning_rates():
    return np.concatenate(
        [
            np.full(6, 0.016),
            np.full(3, 0.005),
            np.full(4, 0.001),
            np.full(1, 0.05),
            np.full(3, 0.0025),
            np.full(45, 0.000125),
        ]
    ).astype(np.float32)


def harmonics(dir_x, dir_y, dir_z):
    sq_x, sq_y, sq_z = (dir_x * dir_x, dir_y * dir_y, dir_z * dir_z)
    return [
        SH_ZERO + 0.0 * dir_x,
        -SH_ONE * dir_y,
        SH_ONE * dir_z,
        -SH_ONE * dir_x,
        SH_TWO[0] * dir_x * dir_y,
        SH_TWO[1] * dir_y * dir_z,
        SH_TWO[2] * (2.0 * sq_z - sq_x - sq_y),
        SH_TWO[3] * dir_x * dir_z,
        SH_TWO[4] * (sq_x - sq_y),
        SH_THREE[0] * dir_y * (3.0 * sq_x - sq_y),
        SH_THREE[1] * dir_x * dir_y * dir_z,
        SH_THREE[2] * dir_y * (4.0 * sq_z - sq_x - sq_y),
        SH_THREE[3] * dir_z * (2.0 * sq_z - 3.0 * sq_x - 3.0 * sq_y),
        SH_THREE[4] * dir_x * (4.0 * sq_z - sq_x - sq_y),
        SH_THREE[5] * dir_z * (sq_x - sq_y),
        SH_THREE[6] * dir_x * (sq_x - 3.0 * sq_y),
    ]


def request_kernel(list_ref, count_ref, cam_ref, out_ref):
    cam = [jnp.full((1, ASK), cam_ref[0, i], jnp.float32) for i in range(9)]
    a, b = cam[0:3], cam[3:6]
    normal = [
        a[1] * b[2] - a[2] * b[1],
        a[2] * b[0] - a[0] * b[2],
        a[0] * b[1] - a[1] * b[0],
    ]
    size = jnp.sqrt(normal[0] * normal[0] + normal[1] * normal[1] + normal[2] * normal[2])
    basis = harmonics(normal[0] / size, normal[1] / size, normal[2] / size)
    words = [jnp.full((1, ASK), -1.0, jnp.float32)] + cam + basis
    lane = lax.broadcasted_iota(jnp.int32, (1, ASK), 1)
    row = jnp.zeros((1, ASK), jnp.float32)
    for i, word in enumerate(words):
        row = jnp.where(lane == i, word, row)

    def fill(s, carry):
        out_ref[s] = row
        return carry

    lax.fori_loop(0, DEVICES, fill, 0, unroll=8)
    for i in range(LIST):

        @pl.when(i < count_ref[0, 0])
        def _(i=i):
            block = list_ref[0, 0, i]
            local = jnp.full((1, ASK), block % BLK_DEV, jnp.int32).astype(jnp.float32)
            out_ref[block // BLK_DEV] = jnp.where(lane == 0, local, row)


PAIRS = [(0, 0), (0, 1), (0, 2), (1, 1), (1, 2), (2, 2)]


def products(word):
    a = [word(W_CAM + i) for i in range(3)]
    b = [word(W_CAM + 3 + i) for i in range(3)]

    def product(p, q):
        return [p[i] * q[i] if i == j else p[i] * q[j] + p[j] * q[i] for i, j in PAIRS]

    return product(a, a), product(a, b), product(b, b)


def component(ref, c):
    return ref[c]


def shape_terms(g_ref):
    squares = [jnp.exp(2.0 * component(g_ref, 6 + c)) for c in range(3)]
    quat = [component(g_ref, 9 + c) for c in range(4)]
    size = jnp.sqrt(quat[0] * quat[0] + quat[1] * quat[1] + quat[2] * quat[2] + quat[3] * quat[3])
    r, x, y, z = [q / size for q in quat]
    rotation = [
        [1.0 - 2.0 * (y * y + z * z), 2.0 * (x * y - r * z), 2.0 * (x * z + r * y)],
        [2.0 * (x * y + r * z), 1.0 - 2.0 * (x * x + z * z), 2.0 * (y * z - r * x)],
        [2.0 * (x * z - r * y), 2.0 * (y * z + r * x), 1.0 - 2.0 * (x * x + y * y)],
    ]
    return squares, rotation, (r, x, y, z), size


def opacity_of(g_ref):
    return 1.0 / (1.0 + jnp.exp(-component(g_ref, 13)))


def shapes_kernel(g_ref, shape_ref, kept_ref):
    squares, rot, quat, size = shape_terms(g_ref)
    opacity = opacity_of(g_ref)
    kept = squares + rot[0] + rot[1] + rot[2] + list(quat) + [1.0 / size, 1.0 - opacity]
    for i, value in enumerate(kept):
        kept_ref[i] = value
    at = 0
    for i in range(3):
        for j in range(i, 3):
            shape_ref[at] = (
                rot[i][0] * rot[j][0] * squares[0]
                + rot[i][1] * rot[j][1] * squares[1]
                + rot[i][2] * rot[j][2] * squares[2]
            )
            at += 1
    shape_ref[6] = opacity


def listed_slots(word_ref, order_ref):
    def look(s, found):
        order_ref[found] = s
        return found + jnp.where(word_ref[W_ID, s] >= 0.0, 1, 0)

    return lax.fori_loop(0, DEVICES, look, 0, unroll=8)


def records_kernel(ask_ref, g_ref, shape_ref, out_ref, turned_ref, word_ref, order_ref, sem):
    turned_ref[...] = ask_ref[...].reshape(DEVICES, ASK).T[0:WORDS]
    copy = pltpu.make_async_copy(turned_ref, word_ref, sem)
    copy.start()
    copy.wait()
    count = listed_slots(word_ref, order_ref)

    def slot(n, carry):
        s = order_ref[n]
        k = word_ref[W_ID, s].astype(jnp.int32)

        def word(i):
            return word_ref[i, s]

        def comp(i):
            return g_ref[i, pl.ds(k, 1), :]

        def put(p, value):
            out_ref[s, :, pl.ds(p * BLOCK, BLOCK)] = value

        time = word(W_CAM + 8)
        centre = [comp(c) + time * comp(3 + c) for c in range(3)]
        for p in range(2):
            put(
                p,
                word(W_CAM + 3 * p) * centre[0]
                + word(W_CAM + 3 * p + 1) * centre[1]
                + word(W_CAM + 3 * p + 2) * centre[2]
                + word(W_CAM + 6 + p),
            )
        shapes = [shape_ref[i, pl.ds(k, 1), :] for i in range(6)]
        for p, (factor, extra) in enumerate(zip(products(word), (0.3, 0.0, 0.3))):
            total = factor[0] * shapes[0]
            for i in range(1, 6):
                total = total + factor[i] * shapes[i]
            put(2 + p, total + extra)
        put(5, shape_ref[6, pl.ds(k, 1), :])
        basis = [word(W_SH + q) for q in range(16)]
        for ch in range(3):
            colour = basis[0] * comp(14 + ch)
            for q in range(1, 16):
                colour = colour + basis[q] * comp(14 + 3 * q + ch)
            put(6 + ch, colour + 0.5)
        return carry

    lax.fori_loop(0, count, slot, 0)


def pixel_rows(row_base):
    px = lax.broadcasted_iota(jnp.int32, (ROWS, COLS), 1).astype(jnp.float32) + 0.5
    py = lax.broadcasted_iota(jnp.int32, (ROWS, COLS), 0).astype(jnp.float32) + 0.5
    py = py + row_base.astype(jnp.float32)
    return px[0:8], (py[0:8], py[8:16])


def row_of(ref, p, i):
    return jnp.broadcast_to(ref[p, pl.ds(i, 1), :], (8, COLS))


def alpha_of(table, i, px, py):
    dx = px - row_of(table, 0, i)
    slope = row_of(table, 3, i) * dx
    level = row_of(table, 2, i) * dx * dx
    bend, peak, middle = row_of(table, 4, i), row_of(table, 5, i), row_of(table, 1, i)
    return [
        peak * jnp.exp2(level + dy * (slope + bend * dy)) for dy in (py[0] - middle, py[1] - middle)
    ]


def render_kernel(
    list_ref,
    start_ref,
    end_ref,
    base_ref,
    got_ref,
    pred_ref,
    send_ref,
    compact_ref,
    table_ref,
    alpha_ref,
    weight_ref,
):
    for t in range(TILES):
        first = start_ref[0, 0, t]
        last = end_ref[0, 0, t]
        for j in range(TILE_MOST):
            live = first + j < last
            place = jnp.where(live, first + j, first)
            owner = list_ref[0, 0, place] // BLK_DEV
            there = jnp.where(live, 1.0, 0.0)
            for p in range(9):
                row = got_ref[owner, :, pl.ds(p * BLOCK, BLOCK)]
                if p == 5:
                    row = row * there
                compact_ref[p, pl.ds(t, 1), pl.ds(j * BLOCK, BLOCK)] = row
    ca, cb, cc = compact_ref[2], compact_ref[3], compact_ref[4]
    det = ca * cc - cb * cb
    forms = [
        compact_ref[0],
        compact_ref[1],
        (-0.5 * LOG2_E) * cc / det,
        LOG2_E * cb / det,
        (-0.5 * LOG2_E) * ca / det,
        compact_ref[5],
        compact_ref[6],
        compact_ref[7],
        compact_ref[8],
    ]
    for p, form in enumerate(forms):
        wide = jnp.broadcast_to(form[:, None, :], (TILES, TILE, GAUSS)).reshape(COLS, GAUSS)
        table_ref[p] = wide.T
    px, py = pixel_rows(base_ref[0])

    def blend(i, carry):
        alphas = alpha_of(table_ref, i, px, py)
        colours = [row_of(table_ref, 6 + ch, i) for ch in range(3)]
        after = []
        for half, alpha in enumerate(alphas):
            trans, *sums = carry[half]
            weight = alpha * trans
            rows = pl.ds(8 * half, 8)
            alpha_ref[i, rows, :] = alpha
            weight_ref[i, rows, :] = weight
            after.append(
                (trans - weight, *[a + weight * c for a, c in zip(sums, colours)])
            )
        return tuple(after)

    zero = jnp.zeros((8, COLS), jnp.float32)
    start = (zero + 1.0, zero, zero, zero)
    done = lax.fori_loop(0, GAUSS, blend, (start, start), unroll=16)
    even = base_ref[0] % (2 * ROWS) == 0
    for ch in range(3):
        pred = jnp.concatenate([done[0][1 + ch], done[1][1 + ch]], axis=0)
        pred_ref[ch] = pred
        low, top = pred[ROWS - HALO :], pred[:HALO]
        send_ref[0, ch] = jnp.where(even, low, top)
        send_ref[1, ch] = jnp.where(even, top, low)


def ssim_value(mean_x, mean_y, square_x, square_y, cross_xy):
    var_x = square_x - mean_x * mean_x
    var_y = square_y - mean_y * mean_y
    covar = cross_xy - mean_x * mean_y
    upper = (2.0 * mean_x * mean_y + STAB_MEAN) * (2.0 * covar + STAB_VAR)
    lower = (mean_x * mean_x + mean_y * mean_y + STAB_MEAN) * (var_x + var_y + STAB_VAR)
    return upper / lower


def exact_dot(a, b):
    return jnp.dot(a, b, precision=HIGHEST_MODE, preferred_element_type=jnp.float32)


def extended(mine, even, one, two):
    before, after = jnp.where(even, two, one), jnp.where(even, one, two)
    rest = jnp.zeros((EXT - ROWS - 2 * HALO, COLS), jnp.float32)
    return jnp.concatenate([before, mine, after, rest], axis=0)


def smoothed(maps, first, across):
    wide = exact_dot(jnp.concatenate(maps, axis=0), across)
    return [exact_dot(first, wide[EXT * m : EXT * (m + 1)]) for m in range(len(maps))]


def target_kernel(
    base_ref, target_ref, one_ref, two_ref, first_ref, across_ref, ext_ref, maps_ref
):
    even = base_ref[0] % (2 * ROWS) == 0
    first, across = first_ref[...], across_ref[...]
    for ch in range(3):
        y = extended(target_ref[ch], even, one_ref[ch], two_ref[ch])
        ext_ref[ch] = y
        maps_ref[ch, 0], maps_ref[ch, 1] = smoothed([y, y * y], first, across)


def loss_gradient(
    base, pred_ref, one_ref, two_ref, target_ref, maps_ref, first_ref, second_ref, across_ref
):
    first, second, across = first_ref[...], second_ref[...], across_ref[...]
    even = base % (2 * ROWS) == 0
    row = lax.broadcasted_iota(jnp.int32, (32, COLS), 0)
    image_row = row + base - 5
    inside = (image_row >= 0) & (image_row < IMG_ROWS) & (row < ROWS + 10)
    total = jnp.zeros((ROWS, COLS), jnp.float32)
    slopes = []
    for ch in range(3):
        pred = pred_ref[ch]
        x, y = extended(pred, even, one_ref[ch], two_ref[ch]), target_ref[ch]
        mean, square, cross = smoothed([x, x * x, x * y], first, across)
        smooth = [mean, maps_ref[ch, 0], square, maps_ref[ch, 1], cross]
        value, pullback = jax.vjp(ssim_value, *smooth)
        parts = pullback(jnp.full_like(value, -SSIM_WEIGHT / 3.0))
        adjoint = [jnp.where(inside, parts[m], 0.0) for m in (0, 2, 4)]
        back = [exact_dot(second, part) for part in adjoint]
        back = exact_dot(jnp.concatenate(back, axis=0), across)
        target = y[HALO : HALO + ROWS]
        error = pred - target
        sign = jnp.where(error > 0.0, 1.0, jnp.where(error < 0.0, -1.0, 0.0))
        slopes.append(
            ABS_WEIGHT / 3.0 * sign
            + back[0:ROWS]
            + 2.0 * pred * back[ROWS : 2 * ROWS]
            + target * back[2 * ROWS : 3 * ROWS]
        )
        total = total + (
            ABS_WEIGHT / 3.0 * jnp.abs(error)
            + SSIM_WEIGHT / 3.0 * (1.0 - value[5 : 5 + ROWS])
        )
    total = jnp.sum(jnp.sum(total, axis=1, keepdims=True), axis=0, keepdims=True)
    return total, slopes


def backward_kernel(
    list_ref,
    count_ref,
    start_ref,
    end_ref,
    base_ref,
    pred_ref,
    one_ref,
    two_ref,
    target_ref,
    maps_ref,
    first_ref,
    second_ref,
    across_ref,
    seg_ref,
    compact_ref,
    table_ref,
    alpha_ref,
    weight_ref,
    out_ref,
    power_ref,
    part_ref,
    moment_ref,
    grad_ref,
):
    total, slopes = loss_gradient(
        base_ref[0],
        pred_ref,
        one_ref,
        two_ref,
        target_ref,
        maps_ref,
        first_ref,
        second_ref,
        across_ref,
    )
    loss_row = jnp.broadcast_to(total, (1, 128))
    empty = jnp.zeros((1, RECORD), jnp.float32)

    def tell(s, carry):
        out_ref[s, :, pl.ds(RECORD, 128)] = loss_row
        return carry

    lax.fori_loop(0, DEVICES, tell, 0, unroll=8)

    def clear(i, carry):
        out_ref[list_ref[0, 0, i] // BLK_DEV, :, pl.ds(0, RECORD)] = empty
        return carry

    lax.fori_loop(0, count_ref[0, 0], clear, 0)
    px, unused_py = pixel_rows(base_ref[0])
    middle = (base_ref[0] + ROWS // 2).astype(jnp.float32)
    slopes = [[slope[0:8], slope[8:16]] for slope in slopes]

    def reverse(step, behind):
        for part in range(UNROLL - 1, -1, -1):
            chunk = GAUSS // 8 - UNROLL * (step + 1) + part
            for r in range(7, -1, -1):
                i = chunk * 8 + r
                colours = [row_of(table_ref, 6 + ch, i) for ch in range(3)]
                weights, after = [], []
                for half in range(2):
                    rows = pl.ds(8 * half, 8)
                    weight = weight_ref[i, rows, :]
                    seen = (
                        colours[0] * slopes[0][half]
                        + colours[1] * slopes[1][half]
                        + colours[2] * slopes[2][half]
                    )
                    ahead = seen - behind[half]
                    after.append(behind[half] + alpha_ref[i, rows, :] * ahead)
                    power_ref[part, pl.ds(16 * r + 8 * half, 8), :] = weight * ahead
                    weights.append(weight)
                behind = after
                for ch in range(3):
                    part_ref[part, ch, pl.ds(8 * r, 8), :] = (
                        weights[0] * slopes[ch][0] + weights[1] * slopes[ch][1]
                    )
            plain = level = bend = None
            for s in range(8):
                upper = power_ref[part, pl.ds(s, 8, stride=16), :]
                lower = power_ref[part, pl.ds(15 - s, 8, stride=16), :]
                offset = 7.5 - s
                total, tilt = upper + lower, (lower - upper) * offset
                round_ = total * (offset * offset)
                plain = total if s == 0 else plain + total
                level = tilt if s == 0 else level + tilt
                bend = round_ if s == 0 else bend + round_
            here = pl.ds(pl.multiple_of(chunk * 8, 8), 8)
            dx = px - table_ref[0, here, :]
            rise = middle - table_ref[1, here, :]
            first_x = plain * dx
            first_y = level + rise * plain
            moment_ref[0, here, :] = plain
            moment_ref[1, here, :] = first_x
            moment_ref[2, here, :] = first_x * dx
            moment_ref[3, here, :] = first_y
            moment_ref[4, here, :] = first_y * dx
            moment_ref[5, here, :] = bend + rise * (level + first_y)
            for ch in range(3):
                piece = part_ref[part, ch, pl.ds(0, 8, stride=8), :]
                for s in range(1, 8):
                    piece = piece + part_ref[part, ch, pl.ds(s, 8, stride=8), :]
                moment_ref[6 + ch, here, :] = piece
        return tuple(behind)

    nothing = jnp.zeros((8, COLS), jnp.float32)
    lax.fori_loop(0, GAUSS // 8 // UNROLL, reverse, (nothing, nothing))
    seg = seg_ref[...].astype(jnp.bfloat16)

    def over_tile(value):
        return lax.dot_general(
            seg, value, (((1,), (1,)), ((), ())), preferred_element_type=jnp.float32
        )

    m = []
    for p in range(9):
        value = moment_ref[p]
        large = value.astype(jnp.bfloat16)
        small = (value - large.astype(jnp.float32)).astype(jnp.bfloat16)
        m.append(over_tile(large) + over_tile(small))
    ca, cb, cc = compact_ref[2], compact_ref[3], compact_ref[4]
    inverse = 1.0 / (ca * cc - cb * cb)
    d_inverse = -0.5 * cc * m[2] + cb * m[4] - 0.5 * ca * m[5]
    d_det = -inverse * inverse * d_inverse
    grad_ref[0] = (cc * m[1] - cb * m[3]) * inverse
    grad_ref[1] = (ca * m[3] - cb * m[1]) * inverse
    grad_ref[2] = -0.5 * inverse * m[5] + cc * d_det
    grad_ref[3] = inverse * m[4] - 2.0 * cb * d_det
    grad_ref[4] = -0.5 * inverse * m[2] + ca * d_det
    grad_ref[5] = m[0]
    for ch in range(3):
        grad_ref[6 + ch] = m[6 + ch]
    for t in range(TILES):
        first = start_ref[0, 0, t]
        for j in range(TILE_MOST):

            @pl.when(first + j < end_ref[0, 0, t])
            def _(t=t, j=j, first=first):
                owner = list_ref[0, 0, first + j] // BLK_DEV
                for p in range(9):
                    lanes = pl.ds(p * BLOCK, BLOCK)
                    out_ref[owner, :, lanes] = (
                        out_ref[owner, :, lanes]
                        + grad_ref[p, pl.ds(t, 1), pl.ds(j * BLOCK, BLOCK)]
                    )


def update_kernel(
    word_ref,
    kept_ref,
    g_ref,
    one_ref,
    two_ref,
    got_ref,
    loss_ref,
    new_out,
    one_out,
    two_out,
    grad_out,
    new_ref,
    new_one_ref,
    new_two_ref,
    grad_ref,
    shape_ref,
    order_ref,
    done_sem,
):
    rates = [float(rate) / BIAS_FIRST for rate in learning_rates()]
    copies = []

    def finish(low, high):
        for c in range(low, high):
            gradient = grad_ref[c]
            new_one = 0.9 * one_ref[c] + 0.1 * gradient
            new_two = 0.999 * two_ref[c] + 0.001 * gradient * gradient
            root = jnp.sqrt(new_two * (1.0 / BIAS_SECOND)) + 1e-08
            new_ref[c] = g_ref[c] - rates[c] * new_one / root
            new_one_ref[c] = new_one
            new_two_ref[c] = new_two
        here = pl.ds(low, high - low)
        for held, out in (
            (new_ref, new_out),
            (new_one_ref, one_out),
            (new_two_ref, two_out),
            (grad_ref, grad_out),
        ):
            copy = pltpu.make_async_copy(held.at[here], out.at[here], done_sem.at[len(copies)])
            copy.start()
            copies.append(copy)

    losses = got_ref[:, :, pl.ds(RECORD, 128)]
    loss_ref[...] = jnp.sum(losses, axis=0) * (1.0 / (DEVICES * ROWS * COLS))
    grad_ref[...] = jnp.zeros(grad_ref.shape, jnp.float32)
    shape_ref[...] = jnp.zeros(shape_ref.shape, jnp.float32)
    count = listed_slots(word_ref, order_ref)

    def slot(n, carry):
        s = order_ref[n]
        k = word_ref[W_ID, s].astype(jnp.int32)

        def word(i):
            return word_ref[i, s]

        here = pl.ds(k, 1)

        def add(c, value):
            grad_ref[c, here, :] = grad_ref[c, here, :] + value

        d = [got_ref[s, :, pl.ds(p * BLOCK, BLOCK)] for p in range(9)]
        time = word(W_CAM + 8)
        for c in range(3):
            d_centre = word(W_CAM + c) * d[0] + word(W_CAM + 3 + c) * d[1]
            add(c, d_centre)
            add(3 + c, time * d_centre)
        factors = products(word)
        for i in range(6):
            shape_ref[i, here, :] = shape_ref[i, here, :] + (
                factors[0][i] * d[2] + factors[1][i] * d[3] + factors[2][i] * d[4]
            )
        shape_ref[6, here, :] = shape_ref[6, here, :] + d[5]
        for q in range(16):
            basis = word(W_SH + q)
            for ch in range(3):
                add(14 + 3 * q + ch, basis * d[6 + ch])
        return carry

    lax.fori_loop(0, count, slot, 0)
    for low, high in ((14, 30), (30, 46), (46, COMPS)):
        finish(low, high)
    squares = [kept_ref[c] for c in range(3)]
    rot = [[kept_ref[3 + 3 * i + c] for c in range(3)] for i in range(3)]
    quat = [kept_ref[12 + c] for c in range(4)]
    s00, s01, s02, s11, s12, s22 = [shape_ref[i] for i in range(6)]
    twice = [[2.0 * s00, s01, s02], [s01, 2.0 * s11, s12], [s02, s12, 2.0 * s22]]
    d_rot = [[None] * 3 for _ in range(3)]

    def put(c, value):
        grad_ref[c] = value

    for c in range(3):
        pulled = [
            twice[i][0] * rot[0][c] + twice[i][1] * rot[1][c] + twice[i][2] * rot[2][c]
            for i in range(3)
        ]
        along = rot[0][c] * pulled[0] + rot[1][c] * pulled[1] + rot[2][c] * pulled[2]
        put(6 + c, squares[c] * along)
        for i in range(3):
            d_rot[i][c] = pulled[i] * squares[c]
    r, x, y, z = quat
    n = d_rot
    d_r = 2.0 * (
        -z * n[0][1] + y * n[0][2] + z * n[1][0] - x * n[1][2] - y * n[2][0] + x * n[2][1]
    )
    d_x = 2.0 * (
        y * n[0][1] + z * n[0][2] + y * n[1][0] - 2.0 * x * n[1][1] - r * n[1][2]
        + z * n[2][0] + r * n[2][1] - 2.0 * x * n[2][2]
    )
    d_y = 2.0 * (
        -2.0 * y * n[0][0] + x * n[0][1] + r * n[0][2] + x * n[1][0] + z * n[1][2]
        - r * n[2][0] + z * n[2][1] - 2.0 * y * n[2][2]
    )
    d_z = 2.0 * (
        -2.0 * z * n[0][0] - r * n[0][1] + x * n[0][2] + r * n[1][0] - 2.0 * z * n[1][1]
        + y * n[1][2] + x * n[2][0] + y * n[2][1]
    )
    d_quat = [d_r, d_x, d_y, d_z]
    along = r * d_r + x * d_x + y * d_y + z * d_z
    for c in range(4):
        put(9 + c, (d_quat[c] - quat[c] * along) * kept_ref[16])
    put(13, shape_ref[6] * kept_ref[17])
    finish(0, 14)
    for copy in copies:
        copy.wait()


def shaped(*shape):
    return jax.ShapeDtypeStruct(shape, jnp.float32)


def exchanged(slots):
    return lax.all_to_all(slots, AXES, split_axis=0, concat_axis=0, tiled=True)


def swapped(sent):
    first = [(i, i ^ 1) for i in range(BANDS)]
    second = [(i + 1, (i ^ 1) + 1) for i in range(BANDS - 2)]
    return (lax.ppermute(sent[0], "band", first), lax.ppermute(sent[1], "band", second))


def per_device(
    gaussians,
    first_moment,
    second_moment,
    camera,
    target,
    block_list,
    block_count,
    tile_start,
    tile_end,
):
    flat, flat_one, flat_two = [
        jnp.transpose(a, (1, 0, 2))
        for a in (gaussians, first_moment, second_moment)
    ]
    first, second, across = tap_matrices()
    base = (lax.axis_index("band") * ROWS).astype(jnp.int32).reshape(1)
    request = pl.pallas_call(
        request_kernel,
        in_specs=[spec(SMEM)] * 3,
        out_specs=spec(VMEM),
        out_shape=shaped(DEVICES, 1, ASK),
        name="request",
    )(block_list, block_count, camera)
    asked = exchanged(request)
    target_band = target[0]
    shapes, kept = pl.pallas_call(
        shapes_kernel,
        in_specs=[spec(VMEM)],
        out_specs=[spec(VMEM)] * 2,
        out_shape=[shaped(7, BLK_DEV, BLOCK), shaped(KEPT, BLK_DEV, BLOCK)],
        compiler_params=params(16),
        name="shapes",
    )(flat)
    asked, shapes, kept = lax.optimization_barrier((asked, shapes, kept))
    records, words = pl.pallas_call(
        records_kernel,
        in_specs=[spec(VMEM)] * 3,
        out_specs=[spec(VMEM)] * 2,
        out_shape=[shaped(DEVICES, 1, RECORD), shaped(WORDS, DEVICES)],
        scratch_shapes=[
            SMEM((WORDS, DEVICES), jnp.float32),
            SMEM((DEVICES + 1,), jnp.int32),
            pltpu.SemaphoreType.DMA,
        ],
        compiler_params=params(16),
        name="records",
    )(asked, flat, shapes)
    records, target_band = lax.optimization_barrier((records, target_band))
    received = exchanged(records)
    even = base[0] % (2 * ROWS) == 0
    low, top = target_band[:, ROWS - HALO :], target_band[:, :HALO]
    target_sent = (jnp.where(even, low, top), jnp.where(even, top, low))
    target_ext, target_maps = pl.pallas_call(
        target_kernel,
        in_specs=[spec(SMEM)] + [spec(VMEM)] * 5,
        out_specs=[spec(VMEM)] * 2,
        out_shape=[shaped(3, EXT, COLS), shaped(3, 2, 32, COLS)],
        compiler_params=params(16),
        name="target",
    )(base, target_band, *swapped(target_sent), first, across)
    received, target_ext, target_maps = lax.optimization_barrier(
        (received, target_ext, target_maps)
    )
    pred, sent, compact, table, alpha, weight = pl.pallas_call(
        render_kernel,
        in_specs=[spec(SMEM)] * 4 + [spec(VMEM)],
        out_specs=[spec(VMEM)] * 6,
        out_shape=[
            shaped(3, ROWS, COLS),
            shaped(2, 3, HALO, COLS),
            shaped(9, TILES, GAUSS),
            shaped(9, GAUSS, COLS),
            shaped(GAUSS, ROWS, COLS),
            shaped(GAUSS, ROWS, COLS),
        ],
        compiler_params=params(16),
        name="render",
    )(block_list, tile_start, tile_end, base, received)
    pred_one, pred_two = swapped(sent)
    seg = (np.arange(COLS)[None, :] // TILE == np.arange(TILES)[:, None]).astype(np.float32)
    outgoing = pl.pallas_call(
        backward_kernel,
        in_specs=[spec(SMEM)] * 5 + [spec(VMEM)] * 13,
        out_specs=spec(VMEM),
        out_shape=shaped(DEVICES, 1, SLOT),
        scratch_shapes=[
            VMEM((UNROLL, 128, COLS), jnp.float32),
            VMEM((UNROLL, 3, 64, COLS), jnp.float32),
            VMEM((9, GAUSS, COLS), jnp.float32),
            VMEM((9, TILES, GAUSS), jnp.float32),
        ],
        compiler_params=params(16),
        name="backward",
    )(
        block_list,
        block_count,
        tile_start,
        tile_end,
        base,
        pred,
        pred_one,
        pred_two,
        target_ext,
        target_maps,
        first,
        second,
        across,
        seg,
        compact,
        table,
        alpha,
        weight,
    )
    incoming = exchanged(outgoing)
    loss, *flats = pl.pallas_call(
        update_kernel,
        in_specs=[spec(SMEM)] + [spec(VMEM)] * 5,
        out_specs=[spec(VMEM)] + [spec(pl.ANY)] * 4,
        out_shape=[shaped(1, 128)] + [shaped(COMPS, BLK_DEV, BLOCK)] * 4,
        scratch_shapes=[VMEM((COMPS, BLK_DEV, BLOCK), jnp.float32)] * 4
        + [
            VMEM((7, BLK_DEV, BLOCK), jnp.float32),
            SMEM((DEVICES + 1,), jnp.int32),
            pltpu.SemaphoreType.DMA((16,)),
        ],
        compiler_params=params(16),
        name="update",
    )(words, kept, flat, flat_one, flat_two, incoming)
    new_params, new_one, new_two, gradient = [jnp.transpose(a, (1, 0, 2)) for a in flats]
    return (new_params, new_one, new_two, loss[0, 0], gradient)


def solution(mesh):
    return jax.shard_map(
        per_device,
        mesh=mesh,
        in_specs=(
            P(AXES, None, None),
            P(AXES, None, None),
            P(AXES, None, None),
            P("view", None),
            P("view", None, "band", None),
            P("view", "band", None),
            P("view", "band"),
            P("view", "band", None),
            P("view", "band", None),
        ),
        out_specs=(
            P(AXES, None, None),
            P(AXES, None, None),
            P(AXES, None, None),
            P(),
            P(AXES, None, None),
        ),
        check_vma=False,
    )
```

```python
import math

import jax
import jax.numpy as jnp
import numpy as np
from jax import lax
from jax.experimental import pallas as pl
from jax.experimental.pallas import tpu as pltpu
from jax.sharding import PartitionSpec as P

TILE = 16
ROWS = 16
COLS = 128
TILES = 8
LIST = 16
BLOCK = 256
BLK_DEV = 16
DEVICES = 128
BANDS = 4
COMPS = 62
TILE_MOST = 2
GAUSS = TILE_MOST * BLOCK
HALO = 10
EXT = 40
RECORD = 9 * BLOCK
SLOT = RECORD + 128
ASK = 128
UNROLL = 4
KEPT = 18
IMG_ROWS = BANDS * ROWS
AXES = ("view", "band")

HIGHEST_MODE = lax.Precision.HIGHEST
SSIM_WEIGHT = 0.2
ABS_WEIGHT = 0.8
STAB_MEAN = 0.0001
STAB_VAR = 0.0009
BIAS_FIRST = 1.0 - math.exp(100.0 * math.log(0.9))
BIAS_SECOND = 1.0 - math.exp(100.0 * math.log(0.999))
SH_ZERO = 0.28209479177387814
SH_ONE = 0.4886025119029199
SH_TWO = [
    1.0925484305920792,
    -1.0925484305920792,
    0.31539156525252005,
    -1.0925484305920792,
    0.5462742152960396,
]
SH_THREE = [
    -0.5900435899266435,
    2.890611442640554,
    -0.4570457994644658,
    0.3731763325901154,
    -0.4570457994644658,
    1.445305721320277,
    -0.5900435899266435,
]

W_ID = 0
W_CAM = 1
W_SH = 10
WORDS = 32

LOG2_E = math.log2(math.e)

SMEM = pltpu.SMEM
VMEM = pltpu.VMEM


def spec(space):
    return pl.BlockSpec(memory_space=space)


def params(mib):
    return pltpu.CompilerParams(vmem_limit_bytes=mib * 1024 * 1024)


def kernel_taps():
    raw_taps = [math.exp(-(offset * offset) / 4.5) for offset in range(-5, 6)]
    tap_total = sum(raw_taps)
    return [raw_tap / tap_total for raw_tap in raw_taps]


def tap_matrices():
    taps = kernel_taps()
    first = np.zeros((32, EXT), np.float32)
    for r in range(ROWS + 10):
        for o in range(11):
            first[r, r + o] = taps[o]
    second = np.zeros((ROWS, 32), np.float32)
    for r in range(ROWS):
        for o in range(11):
            second[r, r + o] = taps[o]
    across = np.zeros((COLS, COLS), np.float32)
    for c in range(COLS):
        for o in range(11):
            if 0 <= c + o - 5 < COLS:
                across[c + o - 5, c] = taps[o]
    return first, second, across


def learning_rates():
    return np.concatenate(
        [
            np.full(6, 0.016),
            np.full(3, 0.005),
            np.full(4, 0.001),
            np.full(1, 0.05),
            np.full(3, 0.0025),
            np.full(45, 0.000125),
        ]
    ).astype(np.float32)


def harmonics(dir_x, dir_y, dir_z):
    sq_x, sq_y, sq_z = (dir_x * dir_x, dir_y * dir_y, dir_z * dir_z)
    return [
        SH_ZERO + 0.0 * dir_x,
        -SH_ONE * dir_y,
        SH_ONE * dir_z,
        -SH_ONE * dir_x,
        SH_TWO[0] * dir_x * dir_y,
        SH_TWO[1] * dir_y * dir_z,
        SH_TWO[2] * (2.0 * sq_z - sq_x - sq_y),
        SH_TWO[3] * dir_x * dir_z,
        SH_TWO[4] * (sq_x - sq_y),
        SH_THREE[0] * dir_y * (3.0 * sq_x - sq_y),
        SH_THREE[1] * dir_x * dir_y * dir_z,
        SH_THREE[2] * dir_y * (4.0 * sq_z - sq_x - sq_y),
        SH_THREE[3] * dir_z * (2.0 * sq_z - 3.0 * sq_x - 3.0 * sq_y),
        SH_THREE[4] * dir_x * (4.0 * sq_z - sq_x - sq_y),
        SH_THREE[5] * dir_z * (sq_x - sq_y),
        SH_THREE[6] * dir_x * (sq_x - 3.0 * sq_y),
    ]


def request_kernel(list_ref, count_ref, cam_ref, out_ref):
    cam = [jnp.full((1, ASK), cam_ref[0, i], jnp.float32) for i in range(9)]
    a, b = cam[0:3], cam[3:6]
    normal = [
        a[1] * b[2] - a[2] * b[1],
        a[2] * b[0] - a[0] * b[2],
        a[0] * b[1] - a[1] * b[0],
    ]
    size = jnp.sqrt(normal[0] * normal[0] + normal[1] * normal[1] + normal[2] * normal[2])
    basis = harmonics(normal[0] / size, normal[1] / size, normal[2] / size)
    words = [jnp.full((1, ASK), -1.0, jnp.float32)] + cam + basis
    lane = lax.broadcasted_iota(jnp.int32, (1, ASK), 1)
    row = jnp.zeros((1, ASK), jnp.float32)
    for i, word in enumerate(words):
        row = jnp.where(lane == i, word, row)

    def fill(s, carry):
        out_ref[s] = row
        return carry

    lax.fori_loop(0, DEVICES, fill, 0, unroll=8)
    for i in range(LIST):

        @pl.when(i < count_ref[0, 0])
        def _(i=i):
            block = list_ref[0, 0, i]
            local = jnp.full((1, ASK), block % BLK_DEV, jnp.int32).astype(jnp.float32)
            out_ref[block // BLK_DEV] = jnp.where(lane == 0, local, row)


PAIRS = [(0, 0), (0, 1), (0, 2), (1, 1), (1, 2), (2, 2)]


def products(word):
    a = [word(W_CAM + i) for i in range(3)]
    b = [word(W_CAM + 3 + i) for i in range(3)]

    def product(p, q):
        return [p[i] * q[i] if i == j else p[i] * q[j] + p[j] * q[i] for i, j in PAIRS]

    return product(a, a), product(a, b), product(b, b)


def component(ref, c):
    return ref[c]


def shape_terms(g_ref):
    squares = [jnp.exp(2.0 * component(g_ref, 6 + c)) for c in range(3)]
    quat = [component(g_ref, 9 + c) for c in range(4)]
    size = jnp.sqrt(quat[0] * quat[0] + quat[1] * quat[1] + quat[2] * quat[2] + quat[3] * quat[3])
    r, x, y, z = [q / size for q in quat]
    rotation = [
        [1.0 - 2.0 * (y * y + z * z), 2.0 * (x * y - r * z), 2.0 * (x * z + r * y)],
        [2.0 * (x * y + r * z), 1.0 - 2.0 * (x * x + z * z), 2.0 * (y * z - r * x)],
        [2.0 * (x * z - r * y), 2.0 * (y * z + r * x), 1.0 - 2.0 * (x * x + y * y)],
    ]
    return squares, rotation, (r, x, y, z), size


def opacity_of(g_ref):
    return 1.0 / (1.0 + jnp.exp(-component(g_ref, 13)))


def shapes_kernel(g_ref, shape_ref, kept_ref):
    squares, rot, quat, size = shape_terms(g_ref)
    opacity = opacity_of(g_ref)
    kept = squares + rot[0] + rot[1] + rot[2] + list(quat) + [1.0 / size, 1.0 - opacity]
    for i, value in enumerate(kept):
        kept_ref[i] = value
    at = 0
    for i in range(3):
        for j in range(i, 3):
            shape_ref[at] = (
                rot[i][0] * rot[j][0] * squares[0]
                + rot[i][1] * rot[j][1] * squares[1]
                + rot[i][2] * rot[j][2] * squares[2]
            )
            at += 1
    shape_ref[6] = opacity


def listed_slots(word_ref, order_ref):
    def look(s, found):
        order_ref[found] = s
        return found + jnp.where(word_ref[W_ID, s] >= 0.0, 1, 0)

    return lax.fori_loop(0, DEVICES, look, 0, unroll=8)


def records_kernel(ask_ref, g_ref, shape_ref, out_ref, turned_ref, word_ref, order_ref, sem):
    turned_ref[...] = ask_ref[...].reshape(DEVICES, ASK).T[0:WORDS]
    copy = pltpu.make_async_copy(turned_ref, word_ref, sem)
    copy.start()
    copy.wait()
    count = listed_slots(word_ref, order_ref)

    def slot(n, carry):
        s = order_ref[n]
        k = word_ref[W_ID, s].astype(jnp.int32)

        def word(i):
            return word_ref[i, s]

        def comp(i):
            return g_ref[i, pl.ds(k, 1), :]

        def put(p, value):
            out_ref[s, :, pl.ds(p * BLOCK, BLOCK)] = value

        time = word(W_CAM + 8)
        centre = [comp(c) + time * comp(3 + c) for c in range(3)]
        for p in range(2):
            put(
                p,
                word(W_CAM + 3 * p) * centre[0]
                + word(W_CAM + 3 * p + 1) * centre[1]
                + word(W_CAM + 3 * p + 2) * centre[2]
                + word(W_CAM + 6 + p),
            )
        shapes = [shape_ref[i, pl.ds(k, 1), :] for i in range(6)]
        for p, (factor, extra) in enumerate(zip(products(word), (0.3, 0.0, 0.3))):
            total = factor[0] * shapes[0]
            for i in range(1, 6):
                total = total + factor[i] * shapes[i]
            put(2 + p, total + extra)
        put(5, shape_ref[6, pl.ds(k, 1), :])
        basis = [word(W_SH + q) for q in range(16)]
        for ch in range(3):
            colour = basis[0] * comp(14 + ch)
            for q in range(1, 16):
                colour = colour + basis[q] * comp(14 + 3 * q + ch)
            put(6 + ch, colour + 0.5)
        return carry

    lax.fori_loop(0, count, slot, 0)


def pixel_rows(row_base):
    px = lax.broadcasted_iota(jnp.int32, (ROWS, COLS), 1).astype(jnp.float32) + 0.5
    py = lax.broadcasted_iota(jnp.int32, (ROWS, COLS), 0).astype(jnp.float32) + 0.5
    py = py + row_base.astype(jnp.float32)
    return px[0:8], (py[0:8], py[8:16])


def row_of(ref, p, i):
    return jnp.broadcast_to(ref[p, pl.ds(i, 1), :], (8, COLS))


def alpha_of(table, i, px, py):
    dx = px - row_of(table, 0, i)
    slope = row_of(table, 3, i) * dx
    level = row_of(table, 2, i) * dx * dx
    bend, peak, middle = row_of(table, 4, i), row_of(table, 5, i), row_of(table, 1, i)
    return [
        peak * jnp.exp2(level + dy * (slope + bend * dy)) for dy in (py[0] - middle, py[1] - middle)
    ]


def render_kernel(
    list_ref,
    start_ref,
    end_ref,
    base_ref,
    got_ref,
    pred_ref,
    send_ref,
    compact_ref,
    table_ref,
    alpha_ref,
    weight_ref,
):
    for t in range(TILES):
        first = start_ref[0, 0, t]
        last = end_ref[0, 0, t]
        for j in range(TILE_MOST):
            live = first + j < last
            place = jnp.where(live, first + j, first)
            owner = list_ref[0, 0, place] // BLK_DEV
            there = jnp.where(live, 1.0, 0.0)
            for p in range(9):
                row = got_ref[owner, :, pl.ds(p * BLOCK, BLOCK)]
                if p == 5:
                    row = row * there
                compact_ref[p, pl.ds(t, 1), pl.ds(j * BLOCK, BLOCK)] = row
    ca, cb, cc = compact_ref[2], compact_ref[3], compact_ref[4]
    det = ca * cc - cb * cb
    forms = [
        compact_ref[0],
        compact_ref[1],
        (-0.5 * LOG2_E) * cc / det,
        LOG2_E * cb / det,
        (-0.5 * LOG2_E) * ca / det,
        compact_ref[5],
        compact_ref[6],
        compact_ref[7],
        compact_ref[8],
    ]
    for p, form in enumerate(forms):
        wide = jnp.broadcast_to(form[:, None, :], (TILES, TILE, GAUSS)).reshape(COLS, GAUSS)
        table_ref[p] = wide.T
    px, py = pixel_rows(base_ref[0])

    def blend(i, carry):
        alphas = alpha_of(table_ref, i, px, py)
        colours = [row_of(table_ref, 6 + ch, i) for ch in range(3)]
        after = []
        for half, alpha in enumerate(alphas):
            trans, *sums = carry[half]
            weight = alpha * trans
            rows = pl.ds(8 * half, 8)
            alpha_ref[i, rows, :] = alpha
            weight_ref[i, rows, :] = weight
            after.append(
                (trans - weight, *[a + weight * c for a, c in zip(sums, colours)])
            )
        return tuple(after)

    zero = jnp.zeros((8, COLS), jnp.float32)
    start = (zero + 1.0, zero, zero, zero)
    done = lax.fori_loop(0, GAUSS, blend, (start, start), unroll=16)
    even = base_ref[0] % (2 * ROWS) == 0
    for ch in range(3):
        pred = jnp.concatenate([done[0][1 + ch], done[1][1 + ch]], axis=0)
        pred_ref[ch] = pred
        low, top = pred[ROWS - HALO :], pred[:HALO]
        send_ref[0, ch] = jnp.where(even, low, top)
        send_ref[1, ch] = jnp.where(even, top, low)


def ssim_value(mean_x, mean_y, square_x, square_y, cross_xy):
    var_x = square_x - mean_x * mean_x
    var_y = square_y - mean_y * mean_y
    covar = cross_xy - mean_x * mean_y
    upper = (2.0 * mean_x * mean_y + STAB_MEAN) * (2.0 * covar + STAB_VAR)
    lower = (mean_x * mean_x + mean_y * mean_y + STAB_MEAN) * (var_x + var_y + STAB_VAR)
    return upper / lower


def exact_dot(a, b):
    return jnp.dot(a, b, precision=HIGHEST_MODE, preferred_element_type=jnp.float32)


def extended(mine, even, one, two):
    before, after = jnp.where(even, two, one), jnp.where(even, one, two)
    rest = jnp.zeros((EXT - ROWS - 2 * HALO, COLS), jnp.float32)
    return jnp.concatenate([before, mine, after, rest], axis=0)


def smoothed(maps, rows, across):
    height = maps[0].shape[0]
    wide = exact_dot(jnp.concatenate(maps, axis=0), across)
    side = [wide[height * m : height * (m + 1)] for m in range(len(maps))]
    done = exact_dot(rows, jnp.concatenate(side, axis=1))
    return [done[:, COLS * m : COLS * (m + 1)] for m in range(len(maps))]


def target_kernel(
    base_ref, target_ref, one_ref, two_ref, first_ref, across_ref, ext_ref, maps_ref
):
    even = base_ref[0] % (2 * ROWS) == 0
    first, across = first_ref[...], across_ref[...]
    maps = []
    for ch in range(3):
        y = extended(target_ref[ch], even, one_ref[ch], two_ref[ch])
        ext_ref[ch] = y
        maps = maps + [y, y * y]
    for i, done in enumerate(smoothed(maps, first, across)):
        maps_ref[i // 2, i % 2] = done


def loss_gradient(
    base, pred_ref, one_ref, two_ref, target_ref, maps_ref, first_ref, second_ref, across_ref
):
    first, second, across = first_ref[...], second_ref[...], across_ref[...]
    even = base % (2 * ROWS) == 0
    row = lax.broadcasted_iota(jnp.int32, (32, COLS), 0)
    image_row = row + base - 5
    inside = (image_row >= 0) & (image_row < IMG_ROWS) & (row < ROWS + 10)
    total = jnp.zeros((ROWS, COLS), jnp.float32)
    maps = []
    for ch in range(3):
        x = extended(pred_ref[ch], even, one_ref[ch], two_ref[ch])
        maps = maps + [x, x * x, x * target_ref[ch]]
    maps = smoothed(maps, first, across)
    values, adjoint = [], []
    for ch in range(3):
        mean, square, cross = maps[3 * ch : 3 * ch + 3]
        smooth = [mean, maps_ref[ch, 0], square, maps_ref[ch, 1], cross]
        value, pullback = jax.vjp(ssim_value, *smooth)
        parts = pullback(jnp.full_like(value, -SSIM_WEIGHT / 3.0))
        values.append(value)
        adjoint = adjoint + [jnp.where(inside, parts[m], 0.0) for m in (0, 2, 4)]
    back = smoothed(adjoint, second, across)
    slopes = []
    for ch in range(3):
        pred, target = pred_ref[ch], target_ref[ch, pl.ds(HALO, ROWS), :]
        error = pred - target
        sign = jnp.where(error > 0.0, 1.0, jnp.where(error < 0.0, -1.0, 0.0))
        slopes.append(
            ABS_WEIGHT / 3.0 * sign
            + back[3 * ch]
            + 2.0 * pred * back[3 * ch + 1]
            + target * back[3 * ch + 2]
        )
        total = total + (
            ABS_WEIGHT / 3.0 * jnp.abs(error)
            + SSIM_WEIGHT / 3.0 * (1.0 - values[ch][5 : 5 + ROWS])
        )
    total = jnp.sum(jnp.sum(total, axis=1, keepdims=True), axis=0, keepdims=True)
    return total, slopes


def backward_kernel(
    lists_in,
    base_ref,
    pred_ref,
    one_ref,
    two_ref,
    target_ref,
    maps_ref,
    first_ref,
    second_ref,
    across_ref,
    seg_ref,
    compact_ref,
    table_ref,
    alpha_ref,
    weight_ref,
    out_ref,
    power_ref,
    part_ref,
    moment_ref,
    grad_ref,
    lists_ref,
    lists_sem,
):
    copy = pltpu.make_async_copy(lists_in, lists_ref, lists_sem)
    copy.start()
    total, slopes = loss_gradient(
        base_ref[0:1],
        pred_ref,
        one_ref,
        two_ref,
        target_ref,
        maps_ref,
        first_ref,
        second_ref,
        across_ref,
    )
    loss_row = jnp.broadcast_to(total, (1, 128))
    empty = jnp.zeros((1, RECORD), jnp.float32)

    def tell(s, carry):
        out_ref[s, :, pl.ds(RECORD, 128)] = loss_row
        return carry

    lax.fori_loop(0, DEVICES, tell, 0, unroll=8)

    def clear(i, carry):
        out_ref[lists_ref[0, i] // BLK_DEV, :, pl.ds(0, RECORD)] = empty
        return carry

    copy.wait()
    lax.fori_loop(0, lists_ref[0, 32], clear, 0)
    px = lax.broadcasted_iota(jnp.int32, (8, COLS), 1).astype(jnp.float32) + 0.5
    middle = (base_ref[...] + ROWS // 2).astype(jnp.float32)
    slopes = [[slope[0:8], slope[8:16]] for slope in slopes]

    def reverse(step, behind):
        for part in range(UNROLL - 1, -1, -1):
            chunk = GAUSS // 8 - UNROLL * (step + 1) + part
            for r in range(7, -1, -1):
                i = chunk * 8 + r
                colours = [row_of(table_ref, 6 + ch, i) for ch in range(3)]
                weights, after = [], []
                for half in range(2):
                    rows = pl.ds(8 * half, 8)
                    weight = weight_ref[i, rows, :]
                    seen = (
                        colours[0] * slopes[0][half]
                        + colours[1] * slopes[1][half]
                        + colours[2] * slopes[2][half]
                    )
                    ahead = seen - behind[half]
                    after.append(behind[half] + alpha_ref[i, rows, :] * ahead)
                    power_ref[part, pl.ds(16 * r + 8 * half, 8), :] = weight * ahead
                    weights.append(weight)
                behind = after
                for ch in range(3):
                    part_ref[part, ch, pl.ds(8 * r, 8), :] = (
                        weights[0] * slopes[ch][0] + weights[1] * slopes[ch][1]
                    )
            plain = level = bend = None
            for s in range(8):
                upper = power_ref[part, pl.ds(s, 8, stride=16), :]
                lower = power_ref[part, pl.ds(15 - s, 8, stride=16), :]
                offset = 7.5 - s
                total, tilt = upper + lower, (lower - upper) * offset
                round_ = total * (offset * offset)
                plain = total if s == 0 else plain + total
                level = tilt if s == 0 else level + tilt
                bend = round_ if s == 0 else bend + round_
            here = pl.ds(pl.multiple_of(chunk * 8, 8), 8)
            dx = px - table_ref[0, here, :]
            rise = middle - table_ref[1, here, :]
            first_x = plain * dx
            first_y = level + rise * plain
            moment_ref[0, here, :] = plain
            moment_ref[1, here, :] = first_x
            moment_ref[2, here, :] = first_x * dx
            moment_ref[3, here, :] = first_y
            moment_ref[4, here, :] = first_y * dx
            moment_ref[5, here, :] = bend + rise * (level + first_y)
            for ch in range(3):
                piece = part_ref[part, ch, pl.ds(0, 8, stride=8), :]
                for s in range(1, 8):
                    piece = piece + part_ref[part, ch, pl.ds(s, 8, stride=8), :]
                moment_ref[6 + ch, here, :] = piece
        return tuple(behind)

    nothing = jnp.zeros((8, COLS), jnp.float32)
    lax.fori_loop(0, GAUSS // 8 // UNROLL, reverse, (nothing, nothing))
    seg = seg_ref[...].astype(jnp.bfloat16)

    def over_tile(value):
        return lax.dot_general(
            seg, value, (((1,), (1,)), ((), ())), preferred_element_type=jnp.float32
        )

    m = []
    for p in range(9):
        value = moment_ref[p]
        large = value.astype(jnp.bfloat16)
        small = (value - large.astype(jnp.float32)).astype(jnp.bfloat16)
        m.append(over_tile(large) + over_tile(small))
    ca, cb, cc = compact_ref[2], compact_ref[3], compact_ref[4]
    inverse = 1.0 / (ca * cc - cb * cb)
    d_inverse = -0.5 * cc * m[2] + cb * m[4] - 0.5 * ca * m[5]
    d_det = -inverse * inverse * d_inverse
    grad_ref[0] = (cc * m[1] - cb * m[3]) * inverse
    grad_ref[1] = (ca * m[3] - cb * m[1]) * inverse
    grad_ref[2] = -0.5 * inverse * m[5] + cc * d_det
    grad_ref[3] = inverse * m[4] - 2.0 * cb * d_det
    grad_ref[4] = -0.5 * inverse * m[2] + ca * d_det
    grad_ref[5] = m[0]
    for ch in range(3):
        grad_ref[6 + ch] = m[6 + ch]
    for t in range(TILES):
        first = lists_ref[0, 16 + t]
        for j in range(TILE_MOST):

            @pl.when(first + j < lists_ref[0, 24 + t])
            def _(t=t, j=j, first=first):
                owner = lists_ref[0, first + j] // BLK_DEV
                for p in range(9):
                    lanes = pl.ds(p * BLOCK, BLOCK)
                    out_ref[owner, :, lanes] = (
                        out_ref[owner, :, lanes]
                        + grad_ref[p, pl.ds(t, 1), pl.ds(j * BLOCK, BLOCK)]
                    )


def update_kernel(
    turned_ref,
    kept_ref,
    g_ref,
    one_ref,
    two_ref,
    got_ref,
    loss_ref,
    new_out,
    one_out,
    two_out,
    grad_out,
    new_ref,
    new_one_ref,
    new_two_ref,
    grad_ref,
    shape_ref,
    word_ref,
    order_ref,
    word_sem,
    done_sem,
):
    words = pltpu.make_async_copy(turned_ref, word_ref, word_sem)
    words.start()
    rates = [float(rate) / BIAS_FIRST for rate in learning_rates()]
    copies = []

    def finish(low, high):
        for c in range(low, high):
            gradient = grad_ref[c]
            new_one = 0.9 * one_ref[c] + 0.1 * gradient
            new_two = 0.999 * two_ref[c] + 0.001 * gradient * gradient
            root = jnp.sqrt(new_two * (1.0 / BIAS_SECOND)) + 1e-08
            new_ref[c] = g_ref[c] - rates[c] * new_one / root
            new_one_ref[c] = new_one
            new_two_ref[c] = new_two
        here = pl.ds(low, high - low)
        for held, out in (
            (new_ref, new_out),
            (new_one_ref, one_out),
            (new_two_ref, two_out),
            (grad_ref, grad_out),
        ):
            copy = pltpu.make_async_copy(held.at[here], out.at[here], done_sem.at[len(copies)])
            copy.start()
            copies.append(copy)

    losses = got_ref[:, :, pl.ds(RECORD, 128)]
    loss_ref[...] = jnp.sum(losses, axis=0) * (1.0 / (DEVICES * ROWS * COLS))
    grad_ref[...] = jnp.zeros(grad_ref.shape, jnp.float32)
    shape_ref[...] = jnp.zeros(shape_ref.shape, jnp.float32)
    words.wait()
    count = listed_slots(word_ref, order_ref)

    def slot(n, carry):
        s = order_ref[n]
        k = word_ref[W_ID, s].astype(jnp.int32)

        def word(i):
            return word_ref[i, s]

        here = pl.ds(k, 1)

        def add(c, value):
            grad_ref[c, here, :] = grad_ref[c, here, :] + value

        d = [got_ref[s, :, pl.ds(p * BLOCK, BLOCK)] for p in range(9)]
        time = word(W_CAM + 8)
        for c in range(3):
            d_centre = word(W_CAM + c) * d[0] + word(W_CAM + 3 + c) * d[1]
            add(c, d_centre)
            add(3 + c, time * d_centre)
        factors = products(word)
        for i in range(6):
            shape_ref[i, here, :] = shape_ref[i, here, :] + (
                factors[0][i] * d[2] + factors[1][i] * d[3] + factors[2][i] * d[4]
            )
        shape_ref[6, here, :] = shape_ref[6, here, :] + d[5]
        for q in range(16):
            basis = word(W_SH + q)
            for ch in range(3):
                add(14 + 3 * q + ch, basis * d[6 + ch])
        return carry

    lax.fori_loop(0, count, slot, 0)
    for low, high in ((14, 30), (30, 46), (46, COMPS)):
        finish(low, high)
    squares = [kept_ref[c] for c in range(3)]
    rot = [[kept_ref[3 + 3 * i + c] for c in range(3)] for i in range(3)]
    quat = [kept_ref[12 + c] for c in range(4)]
    s00, s01, s02, s11, s12, s22 = [shape_ref[i] for i in range(6)]
    twice = [[2.0 * s00, s01, s02], [s01, 2.0 * s11, s12], [s02, s12, 2.0 * s22]]
    d_rot = [[None] * 3 for _ in range(3)]

    def put(c, value):
        grad_ref[c] = value

    for c in range(3):
        pulled = [
            twice[i][0] * rot[0][c] + twice[i][1] * rot[1][c] + twice[i][2] * rot[2][c]
            for i in range(3)
        ]
        along = rot[0][c] * pulled[0] + rot[1][c] * pulled[1] + rot[2][c] * pulled[2]
        put(6 + c, squares[c] * along)
        for i in range(3):
            d_rot[i][c] = pulled[i] * squares[c]
    r, x, y, z = quat
    n = d_rot
    d_r = 2.0 * (
        -z * n[0][1] + y * n[0][2] + z * n[1][0] - x * n[1][2] - y * n[2][0] + x * n[2][1]
    )
    d_x = 2.0 * (
        y * n[0][1] + z * n[0][2] + y * n[1][0] - 2.0 * x * n[1][1] - r * n[1][2]
        + z * n[2][0] + r * n[2][1] - 2.0 * x * n[2][2]
    )
    d_y = 2.0 * (
        -2.0 * y * n[0][0] + x * n[0][1] + r * n[0][2] + x * n[1][0] + z * n[1][2]
        - r * n[2][0] + z * n[2][1] - 2.0 * y * n[2][2]
    )
    d_z = 2.0 * (
        -2.0 * z * n[0][0] - r * n[0][1] + x * n[0][2] + r * n[1][0] - 2.0 * z * n[1][1]
        + y * n[1][2] + x * n[2][0] + y * n[2][1]
    )
    d_quat = [d_r, d_x, d_y, d_z]
    along = r * d_r + x * d_x + y * d_y + z * d_z
    for c in range(4):
        put(9 + c, (d_quat[c] - quat[c] * along) * kept_ref[16])
    put(13, shape_ref[6] * kept_ref[17])
    finish(0, 14)
    for copy in copies:
        copy.wait()


def shaped(*shape):
    return jax.ShapeDtypeStruct(shape, jnp.float32)


def exchanged(slots):
    return lax.all_to_all(slots, AXES, split_axis=0, concat_axis=0, tiled=True)


def swapped(sent):
    first = [(i, i ^ 1) for i in range(BANDS)]
    second = [(i + 1, (i ^ 1) + 1) for i in range(BANDS - 2)]
    return (lax.ppermute(sent[0], "band", first), lax.ppermute(sent[1], "band", second))


def per_device(
    gaussians,
    first_moment,
    second_moment,
    camera,
    target,
    block_list,
    block_count,
    tile_start,
    tile_end,
):
    flat, flat_one, flat_two = [
        jnp.transpose(a, (1, 0, 2))
        for a in (gaussians, first_moment, second_moment)
    ]
    first, second, across = tap_matrices()
    base = (lax.axis_index("band") * ROWS).astype(jnp.int32).reshape(1)
    base_rows = jnp.broadcast_to(base.reshape(1, 1), (8, COLS))
    lists = jnp.concatenate(
        [block_list[0, 0], tile_start[0, 0], tile_end[0, 0], block_count[0]]
        + [jnp.zeros((95,), jnp.int32)]
    ).reshape(1, 128)
    request = pl.pallas_call(
        request_kernel,
        in_specs=[spec(SMEM)] * 3,
        out_specs=spec(VMEM),
        out_shape=shaped(DEVICES, 1, ASK),
        name="request",
    )(block_list, block_count, camera)
    asked = exchanged(request)
    target_band = target[0]
    shapes, kept = pl.pallas_call(
        shapes_kernel,
        in_specs=[spec(VMEM)],
        out_specs=[spec(VMEM)] * 2,
        out_shape=[shaped(7, BLK_DEV, BLOCK), shaped(KEPT, BLK_DEV, BLOCK)],
        compiler_params=params(16),
        name="shapes",
    )(flat)
    asked, shapes, kept = lax.optimization_barrier((asked, shapes, kept))
    records, words = pl.pallas_call(
        records_kernel,
        in_specs=[spec(VMEM)] * 3,
        out_specs=[spec(VMEM)] * 2,
        out_shape=[shaped(DEVICES, 1, RECORD), shaped(WORDS, DEVICES)],
        scratch_shapes=[
            SMEM((WORDS, DEVICES), jnp.float32),
            SMEM((DEVICES + 1,), jnp.int32),
            pltpu.SemaphoreType.DMA,
        ],
        compiler_params=params(16),
        name="records",
    )(asked, flat, shapes)
    records, target_band, lists, base_rows = lax.optimization_barrier(
        (records, target_band, lists, base_rows)
    )
    received = exchanged(records)
    even = base[0] % (2 * ROWS) == 0
    low, top = target_band[:, ROWS - HALO :], target_band[:, :HALO]
    target_sent = (jnp.where(even, low, top), jnp.where(even, top, low))
    target_ext, target_maps = pl.pallas_call(
        target_kernel,
        in_specs=[spec(SMEM)] + [spec(VMEM)] * 5,
        out_specs=[spec(VMEM)] * 2,
        out_shape=[shaped(3, EXT, COLS), shaped(3, 2, 32, COLS)],
        compiler_params=params(16),
        name="target",
    )(base, target_band, *swapped(target_sent), first, across)
    received, target_ext, target_maps = lax.optimization_barrier(
        (received, target_ext, target_maps)
    )
    pred, sent, compact, table, alpha, weight = pl.pallas_call(
        render_kernel,
        in_specs=[spec(SMEM)] * 4 + [spec(VMEM)],
        out_specs=[spec(VMEM)] * 6,
        out_shape=[
            shaped(3, ROWS, COLS),
            shaped(2, 3, HALO, COLS),
            shaped(9, TILES, GAUSS),
            shaped(9, GAUSS, COLS),
            shaped(GAUSS, ROWS, COLS),
            shaped(GAUSS, ROWS, COLS),
        ],
        compiler_params=params(16),
        name="render",
    )(block_list, tile_start, tile_end, base, received)
    pred_one, pred_two = swapped(sent)
    seg = (np.arange(COLS)[None, :] // TILE == np.arange(TILES)[:, None]).astype(np.float32)
    outgoing = pl.pallas_call(
        backward_kernel,
        in_specs=[spec(VMEM)] * 15,
        out_specs=spec(VMEM),
        out_shape=shaped(DEVICES, 1, SLOT),
        scratch_shapes=[
            VMEM((UNROLL, 128, COLS), jnp.float32),
            VMEM((UNROLL, 3, 64, COLS), jnp.float32),
            VMEM((9, GAUSS, COLS), jnp.float32),
            VMEM((9, TILES, GAUSS), jnp.float32),
            SMEM((1, 128), jnp.int32),
            pltpu.SemaphoreType.DMA,
        ],
        compiler_params=params(16),
        name="backward",
    )(
        lists,
        base_rows,
        pred,
        pred_one,
        pred_two,
        target_ext,
        target_maps,
        first,
        second,
        across,
        seg,
        compact,
        table,
        alpha,
        weight,
    )
    incoming = exchanged(outgoing)
    loss, *flats = pl.pallas_call(
        update_kernel,
        in_specs=[spec(VMEM)] * 6,
        out_specs=[spec(VMEM)] + [spec(pl.ANY)] * 4,
        out_shape=[shaped(1, 128)] + [shaped(COMPS, BLK_DEV, BLOCK)] * 4,
        scratch_shapes=[VMEM((COMPS, BLK_DEV, BLOCK), jnp.float32)] * 4
        + [
            VMEM((7, BLK_DEV, BLOCK), jnp.float32),
            SMEM((WORDS, DEVICES), jnp.float32),
            SMEM((DEVICES + 1,), jnp.int32),
            pltpu.SemaphoreType.DMA,
            pltpu.SemaphoreType.DMA((16,)),
        ],
        compiler_params=params(16),
        name="update",
    )(words, kept, flat, flat_one, flat_two, incoming)
    new_params, new_one, new_two, gradient = [jnp.transpose(a, (1, 0, 2)) for a in flats]
    return (new_params, new_one, new_two, loss[0, 0], gradient)


def solution(mesh):
    return jax.shard_map(
        per_device,
        mesh=mesh,
        in_specs=(
            P(AXES, None, None),
            P(AXES, None, None),
            P(AXES, None, None),
            P("view", None),
            P("view", None, "band", None),
            P("view", "band", None),
            P("view", "band"),
            P("view", "band", None),
            P("view", "band", None),
        ),
        out_specs=(
            P(AXES, None, None),
            P(AXES, None, None),
            P(AXES, None, None),
            P(),
            P(AXES, None, None),
        ),
        check_vma=False,
    )
```

```python
import math

import jax
import jax.numpy as jnp
import numpy as np
from jax import lax
from jax.experimental import pallas as pl
from jax.experimental.pallas import tpu as pltpu
from jax.sharding import PartitionSpec as P

TILE = 16
ROWS = 16
COLS = 128
TILES = 8
LIST = 16
BLOCK = 256
BLK_DEV = 16
DEVICES = 128
BANDS = 4
COMPS = 62
TILE_MOST = 2
GAUSS = TILE_MOST * BLOCK
HALO = 10
EXT = 48
WIDE = 32
RECORD = 9 * BLOCK
SLOT = RECORD + 128
ASK = 128
UNROLL = 8
KEPT = 18
IMG_ROWS = BANDS * ROWS
AXES = ("view", "band")

HIGHEST_MODE = lax.Precision.HIGHEST
SSIM_WEIGHT = 0.2
ABS_WEIGHT = 0.8
STAB_MEAN = 0.0001
STAB_VAR = 0.0009
BIAS_FIRST = 1.0 - math.exp(100.0 * math.log(0.9))
BIAS_SECOND = 1.0 - math.exp(100.0 * math.log(0.999))
SH_ZERO = 0.28209479177387814
SH_ONE = 0.4886025119029199
SH_TWO = [
    1.0925484305920792,
    -1.0925484305920792,
    0.31539156525252005,
    -1.0925484305920792,
    0.5462742152960396,
]
SH_THREE = [
    -0.5900435899266435,
    2.890611442640554,
    -0.4570457994644658,
    0.3731763325901154,
    -0.4570457994644658,
    1.445305721320277,
    -0.5900435899266435,
]

W_ID = 0
W_CAM = 1
W_SH = 10
WORDS = 32

LOG2_E = math.log2(math.e)

SMEM = pltpu.SMEM
VMEM = pltpu.VMEM


def spec(space):
    return pl.BlockSpec(memory_space=space)


def params(mib):
    return pltpu.CompilerParams(vmem_limit_bytes=mib * 1024 * 1024)


def kernel_taps():
    raw_taps = [math.exp(-(offset * offset) / 4.5) for offset in range(-5, 6)]
    tap_total = sum(raw_taps)
    return [raw_tap / tap_total for raw_tap in raw_taps]


def across_matrix():
    taps = kernel_taps()
    across = np.zeros((COLS, COLS), np.float32)
    for c in range(COLS):
        for o in range(11):
            if 0 <= c + o - 5 < COLS:
                across[c + o - 5, c] = taps[o]
    return across


def learning_rates():
    return np.concatenate(
        [
            np.full(6, 0.016),
            np.full(3, 0.005),
            np.full(4, 0.001),
            np.full(1, 0.05),
            np.full(3, 0.0025),
            np.full(45, 0.000125),
        ]
    ).astype(np.float32)


def harmonics(dir_x, dir_y, dir_z):
    sq_x, sq_y, sq_z = (dir_x * dir_x, dir_y * dir_y, dir_z * dir_z)
    return [
        SH_ZERO + 0.0 * dir_x,
        -SH_ONE * dir_y,
        SH_ONE * dir_z,
        -SH_ONE * dir_x,
        SH_TWO[0] * dir_x * dir_y,
        SH_TWO[1] * dir_y * dir_z,
        SH_TWO[2] * (2.0 * sq_z - sq_x - sq_y),
        SH_TWO[3] * dir_x * dir_z,
        SH_TWO[4] * (sq_x - sq_y),
        SH_THREE[0] * dir_y * (3.0 * sq_x - sq_y),
        SH_THREE[1] * dir_x * dir_y * dir_z,
        SH_THREE[2] * dir_y * (4.0 * sq_z - sq_x - sq_y),
        SH_THREE[3] * dir_z * (2.0 * sq_z - 3.0 * sq_x - 3.0 * sq_y),
        SH_THREE[4] * dir_x * (4.0 * sq_z - sq_x - sq_y),
        SH_THREE[5] * dir_z * (sq_x - sq_y),
        SH_THREE[6] * dir_x * (sq_x - 3.0 * sq_y),
    ]


def request_kernel(list_ref, count_ref, cam_ref, out_ref):
    cam = [jnp.full((1, ASK), cam_ref[0, i], jnp.float32) for i in range(9)]
    a, b = cam[0:3], cam[3:6]
    normal = [
        a[1] * b[2] - a[2] * b[1],
        a[2] * b[0] - a[0] * b[2],
        a[0] * b[1] - a[1] * b[0],
    ]
    size = jnp.sqrt(normal[0] * normal[0] + normal[1] * normal[1] + normal[2] * normal[2])
    basis = harmonics(normal[0] / size, normal[1] / size, normal[2] / size)
    words = [jnp.full((1, ASK), -1.0, jnp.float32)] + cam + basis
    lane = lax.broadcasted_iota(jnp.int32, (1, ASK), 1)
    row = jnp.zeros((1, ASK), jnp.float32)
    for i, word in enumerate(words):
        row = jnp.where(lane == i, word, row)

    def fill(s, carry):
        out_ref[s] = row
        return carry

    lax.fori_loop(0, DEVICES, fill, 0, unroll=8)
    for i in range(LIST):

        @pl.when(i < count_ref[0, 0])
        def _(i=i):
            block = list_ref[0, 0, i]
            local = jnp.full((1, ASK), block % BLK_DEV, jnp.int32).astype(jnp.float32)
            out_ref[block // BLK_DEV] = jnp.where(lane == 0, local, row)


PAIRS = [(0, 0), (0, 1), (0, 2), (1, 1), (1, 2), (2, 2)]


def products(word):
    a = [word(W_CAM + i) for i in range(3)]
    b = [word(W_CAM + 3 + i) for i in range(3)]

    def product(p, q):
        return [p[i] * q[i] if i == j else p[i] * q[j] + p[j] * q[i] for i, j in PAIRS]

    return product(a, a), product(a, b), product(b, b)


def component(ref, c):
    return ref[c]


def shape_terms(g_ref):
    squares = [jnp.exp(2.0 * component(g_ref, 6 + c)) for c in range(3)]
    quat = [component(g_ref, 9 + c) for c in range(4)]
    size = jnp.sqrt(quat[0] * quat[0] + quat[1] * quat[1] + quat[2] * quat[2] + quat[3] * quat[3])
    r, x, y, z = [q / size for q in quat]
    rotation = [
        [1.0 - 2.0 * (y * y + z * z), 2.0 * (x * y - r * z), 2.0 * (x * z + r * y)],
        [2.0 * (x * y + r * z), 1.0 - 2.0 * (x * x + z * z), 2.0 * (y * z - r * x)],
        [2.0 * (x * z - r * y), 2.0 * (y * z + r * x), 1.0 - 2.0 * (x * x + y * y)],
    ]
    return squares, rotation, (r, x, y, z), size


def opacity_of(g_ref):
    return 1.0 / (1.0 + jnp.exp(-component(g_ref, 13)))


def shapes_kernel(g_ref, shape_ref, kept_ref):
    squares, rot, quat, size = shape_terms(g_ref)
    opacity = opacity_of(g_ref)
    kept = squares + rot[0] + rot[1] + rot[2] + list(quat) + [1.0 / size, 1.0 - opacity]
    for i, value in enumerate(kept):
        kept_ref[i] = value
    at = 0
    for i in range(3):
        for j in range(i, 3):
            shape_ref[at] = (
                rot[i][0] * rot[j][0] * squares[0]
                + rot[i][1] * rot[j][1] * squares[1]
                + rot[i][2] * rot[j][2] * squares[2]
            )
            at += 1
    shape_ref[6] = opacity


def listed_slots(word_ref, order_ref):
    def look(s, found):
        order_ref[found] = s
        return found + jnp.where(word_ref[W_ID, s] >= 0.0, 1, 0)

    return lax.fori_loop(0, DEVICES, look, 0, unroll=32)


def records_kernel(ask_ref, g_ref, shape_ref, out_ref, turned_ref, word_ref, order_ref, sem):
    turned_ref[...] = ask_ref[...].reshape(DEVICES, ASK).T[0:WORDS]
    copy = pltpu.make_async_copy(turned_ref, word_ref, sem)
    copy.start()
    copy.wait()
    count = listed_slots(word_ref, order_ref)

    def slot(n, carry):
        s = order_ref[n]
        k = word_ref[W_ID, s].astype(jnp.int32)

        def word(i):
            return word_ref[i, s]

        def comp(i):
            return g_ref[i, pl.ds(k, 1), :]

        def put(p, value):
            out_ref[s, :, pl.ds(p * BLOCK, BLOCK)] = value

        time = word(W_CAM + 8)
        centre = [comp(c) + time * comp(3 + c) for c in range(3)]
        for p in range(2):
            put(
                p,
                word(W_CAM + 3 * p) * centre[0]
                + word(W_CAM + 3 * p + 1) * centre[1]
                + word(W_CAM + 3 * p + 2) * centre[2]
                + word(W_CAM + 6 + p),
            )
        shapes = [shape_ref[i, pl.ds(k, 1), :] for i in range(6)]
        for p, (factor, extra) in enumerate(zip(products(word), (0.3, 0.0, 0.3))):
            total = factor[0] * shapes[0]
            for i in range(1, 6):
                total = total + factor[i] * shapes[i]
            put(2 + p, total + extra)
        put(5, shape_ref[6, pl.ds(k, 1), :])
        basis = [word(W_SH + q) for q in range(16)]
        for ch in range(3):
            colour = basis[0] * comp(14 + ch)
            for q in range(1, 16):
                colour = colour + basis[q] * comp(14 + 3 * q + ch)
            put(6 + ch, colour + 0.5)
        return carry

    lax.fori_loop(0, count, slot, 0)


def pixel_rows(row_base):
    px = lax.broadcasted_iota(jnp.int32, (ROWS, COLS), 1).astype(jnp.float32) + 0.5
    py = lax.broadcasted_iota(jnp.int32, (ROWS, COLS), 0).astype(jnp.float32) + 0.5
    py = py + row_base.astype(jnp.float32)
    return px[0:8], (py[0:8], py[8:16])


def row_of(ref, p, i):
    return jnp.broadcast_to(ref[p, pl.ds(i, 1), :], (8, COLS))


def alpha_of(table, i, px, py):
    dx = px - row_of(table, 0, i)
    slope = row_of(table, 3, i) * dx
    level = row_of(table, 2, i) * dx * dx
    bend, peak, middle = row_of(table, 4, i), row_of(table, 5, i), row_of(table, 1, i)
    return [
        peak * jnp.exp2(level + dy * (slope + bend * dy)) for dy in (py[0] - middle, py[1] - middle)
    ]


def render_kernel(
    list_ref,
    start_ref,
    end_ref,
    base_ref,
    got_ref,
    pred_ref,
    send_ref,
    compact_ref,
    table_ref,
    alpha_ref,
    weight_ref,
):
    for t in range(TILES):
        first = start_ref[0, 0, t]
        last = end_ref[0, 0, t]
        for j in range(TILE_MOST):
            live = first + j < last
            place = jnp.where(live, first + j, first)
            owner = list_ref[0, 0, place] // BLK_DEV
            there = jnp.where(live, 1.0, 0.0)
            for p in range(9):
                row = got_ref[owner, :, pl.ds(p * BLOCK, BLOCK)]
                if p == 5:
                    row = row * there
                compact_ref[p, pl.ds(t, 1), pl.ds(j * BLOCK, BLOCK)] = row
    ca, cb, cc = compact_ref[2], compact_ref[3], compact_ref[4]
    det = ca * cc - cb * cb
    forms = [
        compact_ref[0],
        compact_ref[1],
        (-0.5 * LOG2_E) * cc / det,
        LOG2_E * cb / det,
        (-0.5 * LOG2_E) * ca / det,
        compact_ref[5],
        compact_ref[6],
        compact_ref[7],
        compact_ref[8],
    ]
    for p, form in enumerate(forms):
        wide = jnp.broadcast_to(form[:, None, :], (TILES, TILE, GAUSS)).reshape(COLS, GAUSS)
        table_ref[p] = wide.T
    px, py = pixel_rows(base_ref[0])

    def blend(i, carry):
        alphas = alpha_of(table_ref, i, px, py)
        colours = [row_of(table_ref, 6 + ch, i) for ch in range(3)]
        after = []
        for half, alpha in enumerate(alphas):
            trans, *sums = carry[half]
            weight = alpha * trans
            rows = pl.ds(8 * half, 8)
            alpha_ref[i, rows, :] = alpha
            weight_ref[i, rows, :] = weight
            after.append(
                (trans - weight, *[a + weight * c for a, c in zip(sums, colours)])
            )
        return tuple(after)

    zero = jnp.zeros((8, COLS), jnp.float32)
    start = (zero + 1.0, zero, zero, zero)
    done = lax.fori_loop(0, GAUSS, blend, (start, start), unroll=32)
    even = base_ref[0] % (2 * ROWS) == 0
    for ch in range(3):
        pred = jnp.concatenate([done[0][1 + ch], done[1][1 + ch]], axis=0)
        pred_ref[ch] = pred
        low, top = pred[ROWS - HALO :], pred[:HALO]
        send_ref[0, ch] = jnp.where(even, low, top)
        send_ref[1, ch] = jnp.where(even, top, low)


def ssim_value(mean_x, mean_y, square_x, square_y, cross_xy):
    var_x = square_x - mean_x * mean_x
    var_y = square_y - mean_y * mean_y
    covar = cross_xy - mean_x * mean_y
    upper = (2.0 * mean_x * mean_y + STAB_MEAN) * (2.0 * covar + STAB_VAR)
    lower = (mean_x * mean_x + mean_y * mean_y + STAB_MEAN) * (var_x + var_y + STAB_VAR)
    return upper / lower


def exact_dot(a, b):
    return jnp.dot(a, b, precision=HIGHEST_MODE, preferred_element_type=jnp.float32)


def extended(mine, even, one, two):
    before, after = jnp.where(even, two, one), jnp.where(even, one, two)
    rest = jnp.zeros((EXT - ROWS - 2 * HALO, COLS), jnp.float32)
    return jnp.concatenate([before, mine, after, rest], axis=0)


def smoothed(maps, rows_out, across, held_ref):
    taps = kernel_taps()
    height = maps[0].shape[0]
    for m, value in enumerate(maps):
        held_ref[pl.ds(height * m, height), :] = value
    done = []
    for m in range(len(maps)):

        def shifted(o, m=m):
            return held_ref[pl.ds(height * m + o, rows_out), :]

        total = taps[5] * shifted(5)
        for o in range(5):
            total = total + taps[o] * (shifted(o) + shifted(10 - o))
        done.append(total)
    wide = exact_dot(jnp.concatenate(done, axis=0), across)
    return [wide[rows_out * m : rows_out * (m + 1)] for m in range(len(maps))]


def target_kernel(
    base_ref, target_ref, one_ref, two_ref, across_ref, ext_ref, maps_ref, held_ref
):
    even = base_ref[0] % (2 * ROWS) == 0
    across = across_ref[...]
    maps = []
    for ch in range(3):
        y = extended(target_ref[ch], even, one_ref[ch], two_ref[ch])
        ext_ref[ch] = y
        maps = maps + [y, y * y]
    for i, done in enumerate(smoothed(maps, WIDE, across, held_ref)):
        maps_ref[i // 2, i % 2] = done


def loss_gradient(
    base, pred_ref, one_ref, two_ref, target_ref, maps_ref, across_ref, held_ref
):
    across = across_ref[...]
    even = base % (2 * ROWS) == 0
    row = lax.broadcasted_iota(jnp.int32, (WIDE, COLS), 0)
    image_row = row + base - 5
    inside = (image_row >= 0) & (image_row < IMG_ROWS) & (row < ROWS + 10)
    total = jnp.zeros((ROWS, COLS), jnp.float32)
    maps = []
    for ch in range(3):
        x = extended(pred_ref[ch], even, one_ref[ch], two_ref[ch])
        maps = maps + [x, x * x, x * target_ref[ch]]
    maps = smoothed(maps, WIDE, across, held_ref)
    values, adjoint = [], []
    for ch in range(3):
        mean, square, cross = maps[3 * ch : 3 * ch + 3]
        smooth = [mean, maps_ref[ch, 0], square, maps_ref[ch, 1], cross]
        value, pullback = jax.vjp(ssim_value, *smooth)
        parts = pullback(jnp.full_like(value, -SSIM_WEIGHT / 3.0))
        values.append(value)
        adjoint = adjoint + [jnp.where(inside, parts[m], 0.0) for m in (0, 2, 4)]
    back = smoothed(adjoint, ROWS, across, held_ref)
    slopes = []
    for ch in range(3):
        pred, target = pred_ref[ch], target_ref[ch, pl.ds(HALO, ROWS), :]
        error = pred - target
        sign = jnp.where(error > 0.0, 1.0, jnp.where(error < 0.0, -1.0, 0.0))
        slopes.append(
            ABS_WEIGHT / 3.0 * sign
            + back[3 * ch]
            + 2.0 * pred * back[3 * ch + 1]
            + target * back[3 * ch + 2]
        )
        total = total + (
            ABS_WEIGHT / 3.0 * jnp.abs(error)
            + SSIM_WEIGHT / 3.0 * (1.0 - values[ch][5 : 5 + ROWS])
        )
    total = jnp.sum(jnp.sum(total, axis=1, keepdims=True), axis=0, keepdims=True)
    return total, slopes


def backward_kernel(
    lists_in,
    base_ref,
    pred_ref,
    one_ref,
    two_ref,
    target_ref,
    maps_ref,
    across_ref,
    seg_ref,
    compact_ref,
    table_ref,
    alpha_ref,
    weight_ref,
    out_ref,
    power_ref,
    part_ref,
    moment_ref,
    grad_ref,
    held_ref,
    lists_ref,
    lists_sem,
):
    copy = pltpu.make_async_copy(lists_in, lists_ref, lists_sem)
    copy.start()
    total, slopes = loss_gradient(
        base_ref[0:1],
        pred_ref,
        one_ref,
        two_ref,
        target_ref,
        maps_ref,
        across_ref,
        held_ref,
    )
    loss_row = jnp.broadcast_to(total, (1, 128))
    empty = jnp.zeros((1, RECORD), jnp.float32)

    def tell(s, carry):
        out_ref[s, :, pl.ds(RECORD, 128)] = loss_row
        return carry

    lax.fori_loop(0, DEVICES, tell, 0, unroll=8)

    def clear(i, carry):
        out_ref[lists_ref[0, i] // BLK_DEV, :, pl.ds(0, RECORD)] = empty
        return carry

    copy.wait()
    lax.fori_loop(0, lists_ref[0, 32], clear, 0)
    px = lax.broadcasted_iota(jnp.int32, (8, COLS), 1).astype(jnp.float32) + 0.5
    middle = (base_ref[...] + ROWS // 2).astype(jnp.float32)
    slopes = [[slope[0:8], slope[8:16]] for slope in slopes]

    def reverse(step, behind):
        for part in range(UNROLL - 1, -1, -1):
            chunk = GAUSS // 8 - UNROLL * (step + 1) + part
            for r in range(7, -1, -1):
                i = chunk * 8 + r
                colours = [row_of(table_ref, 6 + ch, i) for ch in range(3)]
                weights, after = [], []
                for half in range(2):
                    rows = pl.ds(8 * half, 8)
                    weight = weight_ref[i, rows, :]
                    seen = (
                        colours[0] * slopes[0][half]
                        + colours[1] * slopes[1][half]
                        + colours[2] * slopes[2][half]
                    )
                    ahead = seen - behind[half]
                    after.append(behind[half] + alpha_ref[i, rows, :] * ahead)
                    power_ref[part, pl.ds(16 * r + 8 * half, 8), :] = weight * ahead
                    weights.append(weight)
                behind = after
                for ch in range(3):
                    part_ref[part, ch, pl.ds(8 * r, 8), :] = (
                        weights[0] * slopes[ch][0] + weights[1] * slopes[ch][1]
                    )
            plain = level = bend = None
            for s in range(8):
                upper = power_ref[part, pl.ds(s, 8, stride=16), :]
                lower = power_ref[part, pl.ds(15 - s, 8, stride=16), :]
                offset = 7.5 - s
                total, tilt = upper + lower, (lower - upper) * offset
                round_ = total * (offset * offset)
                plain = total if s == 0 else plain + total
                level = tilt if s == 0 else level + tilt
                bend = round_ if s == 0 else bend + round_
            here = pl.ds(pl.multiple_of(chunk * 8, 8), 8)
            dx = px - table_ref[0, here, :]
            rise = middle - table_ref[1, here, :]
            first_x = plain * dx
            first_y = level + rise * plain
            moment_ref[0, here, :] = plain
            moment_ref[1, here, :] = first_x
            moment_ref[2, here, :] = first_x * dx
            moment_ref[3, here, :] = first_y
            moment_ref[4, here, :] = first_y * dx
            moment_ref[5, here, :] = bend + rise * (level + first_y)
            for ch in range(3):
                piece = part_ref[part, ch, pl.ds(0, 8, stride=8), :]
                for s in range(1, 8):
                    piece = piece + part_ref[part, ch, pl.ds(s, 8, stride=8), :]
                moment_ref[6 + ch, here, :] = piece
        return tuple(behind)

    nothing = jnp.zeros((8, COLS), jnp.float32)
    lax.fori_loop(0, GAUSS // 8 // UNROLL, reverse, (nothing, nothing))
    seg = seg_ref[...].astype(jnp.bfloat16)

    def over_tile(value):
        return lax.dot_general(
            seg, value, (((1,), (1,)), ((), ())), preferred_element_type=jnp.float32
        )

    m = []
    for p in range(9):
        value = moment_ref[p]
        large = value.astype(jnp.bfloat16)
        small = (value - large.astype(jnp.float32)).astype(jnp.bfloat16)
        m.append(over_tile(large) + over_tile(small))
    ca, cb, cc = compact_ref[2], compact_ref[3], compact_ref[4]
    inverse = 1.0 / (ca * cc - cb * cb)
    d_inverse = -0.5 * cc * m[2] + cb * m[4] - 0.5 * ca * m[5]
    d_det = -inverse * inverse * d_inverse
    grad_ref[0] = (cc * m[1] - cb * m[3]) * inverse
    grad_ref[1] = (ca * m[3] - cb * m[1]) * inverse
    grad_ref[2] = -0.5 * inverse * m[5] + cc * d_det
    grad_ref[3] = inverse * m[4] - 2.0 * cb * d_det
    grad_ref[4] = -0.5 * inverse * m[2] + ca * d_det
    grad_ref[5] = m[0]
    for ch in range(3):
        grad_ref[6 + ch] = m[6 + ch]
    for t in range(TILES):
        first = lists_ref[0, 16 + t]
        for j in range(TILE_MOST):

            @pl.when(first + j < lists_ref[0, 24 + t])
            def _(t=t, j=j, first=first):
                owner = lists_ref[0, first + j] // BLK_DEV
                for p in range(9):
                    lanes = pl.ds(p * BLOCK, BLOCK)
                    out_ref[owner, :, lanes] = (
                        out_ref[owner, :, lanes]
                        + grad_ref[p, pl.ds(t, 1), pl.ds(j * BLOCK, BLOCK)]
                    )


def update_kernel(
    turned_ref,
    kept_ref,
    g_ref,
    one_ref,
    two_ref,
    got_ref,
    loss_ref,
    new_out,
    one_out,
    two_out,
    grad_out,
    new_ref,
    new_one_ref,
    new_two_ref,
    grad_ref,
    shape_ref,
    word_ref,
    order_ref,
    word_sem,
    done_sem,
):
    words = pltpu.make_async_copy(turned_ref, word_ref, word_sem)
    words.start()
    rates = [float(rate) / BIAS_FIRST for rate in learning_rates()]
    copies = []

    def finish(low, high):
        for c in range(low, high):
            gradient = grad_ref[c]
            new_one = 0.9 * one_ref[c] + 0.1 * gradient
            new_two = 0.999 * two_ref[c] + 0.001 * gradient * gradient
            root = jnp.sqrt(new_two * (1.0 / BIAS_SECOND)) + 1e-08
            new_ref[c] = g_ref[c] - rates[c] * new_one / root
            new_one_ref[c] = new_one
            new_two_ref[c] = new_two
        here = pl.ds(low, high - low)
        for held, out in (
            (new_ref, new_out),
            (new_one_ref, one_out),
            (new_two_ref, two_out),
            (grad_ref, grad_out),
        ):
            copy = pltpu.make_async_copy(held.at[here], out.at[here], done_sem.at[len(copies)])
            copy.start()
            copies.append(copy)

    losses = got_ref[:, :, pl.ds(RECORD, 128)]
    loss_ref[...] = jnp.sum(losses, axis=0) * (1.0 / (DEVICES * ROWS * COLS))
    grad_ref[...] = jnp.zeros(grad_ref.shape, jnp.float32)
    shape_ref[...] = jnp.zeros(shape_ref.shape, jnp.float32)
    words.wait()
    count = listed_slots(word_ref, order_ref)

    def slot(n, carry):
        s = order_ref[n]
        k = word_ref[W_ID, s].astype(jnp.int32)

        def word(i):
            return word_ref[i, s]

        here = pl.ds(k, 1)

        def add(c, value):
            grad_ref[c, here, :] = grad_ref[c, here, :] + value

        d = [got_ref[s, :, pl.ds(p * BLOCK, BLOCK)] for p in range(9)]
        time = word(W_CAM + 8)
        for c in range(3):
            d_centre = word(W_CAM + c) * d[0] + word(W_CAM + 3 + c) * d[1]
            add(c, d_centre)
            add(3 + c, time * d_centre)
        factors = products(word)
        for i in range(6):
            shape_ref[i, here, :] = shape_ref[i, here, :] + (
                factors[0][i] * d[2] + factors[1][i] * d[3] + factors[2][i] * d[4]
            )
        shape_ref[6, here, :] = shape_ref[6, here, :] + d[5]
        for q in range(16):
            basis = word(W_SH + q)
            for ch in range(3):
                add(14 + 3 * q + ch, basis * d[6 + ch])
        return carry

    lax.fori_loop(0, count, slot, 0)
    for low, high in ((14, 30), (30, 46), (46, COMPS)):
        finish(low, high)
    squares = [kept_ref[c] for c in range(3)]
    rot = [[kept_ref[3 + 3 * i + c] for c in range(3)] for i in range(3)]
    quat = [kept_ref[12 + c] for c in range(4)]
    s00, s01, s02, s11, s12, s22 = [shape_ref[i] for i in range(6)]
    twice = [[2.0 * s00, s01, s02], [s01, 2.0 * s11, s12], [s02, s12, 2.0 * s22]]
    d_rot = [[None] * 3 for _ in range(3)]

    def put(c, value):
        grad_ref[c] = value

    for c in range(3):
        pulled = [
            twice[i][0] * rot[0][c] + twice[i][1] * rot[1][c] + twice[i][2] * rot[2][c]
            for i in range(3)
        ]
        along = rot[0][c] * pulled[0] + rot[1][c] * pulled[1] + rot[2][c] * pulled[2]
        put(6 + c, squares[c] * along)
        for i in range(3):
            d_rot[i][c] = pulled[i] * squares[c]
    r, x, y, z = quat
    n = d_rot
    d_r = 2.0 * (
        -z * n[0][1] + y * n[0][2] + z * n[1][0] - x * n[1][2] - y * n[2][0] + x * n[2][1]
    )
    d_x = 2.0 * (
        y * n[0][1] + z * n[0][2] + y * n[1][0] - 2.0 * x * n[1][1] - r * n[1][2]
        + z * n[2][0] + r * n[2][1] - 2.0 * x * n[2][2]
    )
    d_y = 2.0 * (
        -2.0 * y * n[0][0] + x * n[0][1] + r * n[0][2] + x * n[1][0] + z * n[1][2]
        - r * n[2][0] + z * n[2][1] - 2.0 * y * n[2][2]
    )
    d_z = 2.0 * (
        -2.0 * z * n[0][0] - r * n[0][1] + x * n[0][2] + r * n[1][0] - 2.0 * z * n[1][1]
        + y * n[1][2] + x * n[2][0] + y * n[2][1]
    )
    d_quat = [d_r, d_x, d_y, d_z]
    along = r * d_r + x * d_x + y * d_y + z * d_z
    for c in range(4):
        put(9 + c, (d_quat[c] - quat[c] * along) * kept_ref[16])
    put(13, shape_ref[6] * kept_ref[17])
    finish(0, 14)
    for copy in copies:
        copy.wait()


def shaped(*shape):
    return jax.ShapeDtypeStruct(shape, jnp.float32)


def exchanged(slots):
    return lax.all_to_all(slots, AXES, split_axis=0, concat_axis=0, tiled=True)


def swapped(sent):
    first = [(i, i ^ 1) for i in range(BANDS)]
    second = [(i + 1, (i ^ 1) + 1) for i in range(BANDS - 2)]
    return (lax.ppermute(sent[0], "band", first), lax.ppermute(sent[1], "band", second))


def per_device(
    gaussians,
    first_moment,
    second_moment,
    camera,
    target,
    block_list,
    block_count,
    tile_start,
    tile_end,
):
    flat, flat_one, flat_two = [
        jnp.transpose(a, (1, 0, 2))
        for a in (gaussians, first_moment, second_moment)
    ]
    across = across_matrix()
    base = (lax.axis_index("band") * ROWS).astype(jnp.int32).reshape(1)
    base_rows = jnp.broadcast_to(base.reshape(1, 1), (8, COLS))
    lists = jnp.concatenate(
        [block_list[0, 0], tile_start[0, 0], tile_end[0, 0], block_count[0]]
        + [jnp.zeros((95,), jnp.int32)]
    ).reshape(1, 128)
    request = pl.pallas_call(
        request_kernel,
        in_specs=[spec(SMEM)] * 3,
        out_specs=spec(VMEM),
        out_shape=shaped(DEVICES, 1, ASK),
        name="request",
    )(block_list, block_count, camera)
    asked = exchanged(request)
    target_band = target[0]
    shapes, kept = pl.pallas_call(
        shapes_kernel,
        in_specs=[spec(VMEM)],
        out_specs=[spec(VMEM)] * 2,
        out_shape=[shaped(7, BLK_DEV, BLOCK), shaped(KEPT, BLK_DEV, BLOCK)],
        compiler_params=params(16),
        name="shapes",
    )(flat)
    asked, shapes, kept = lax.optimization_barrier((asked, shapes, kept))
    records, words = pl.pallas_call(
        records_kernel,
        in_specs=[spec(VMEM)] * 3,
        out_specs=[spec(VMEM)] * 2,
        out_shape=[shaped(DEVICES, 1, RECORD), shaped(WORDS, DEVICES)],
        scratch_shapes=[
            SMEM((WORDS, DEVICES), jnp.float32),
            SMEM((DEVICES + 1,), jnp.int32),
            pltpu.SemaphoreType.DMA,
        ],
        compiler_params=params(16),
        name="records",
    )(asked, flat, shapes)
    records, target_band, lists, base_rows = lax.optimization_barrier(
        (records, target_band, lists, base_rows)
    )
    received = exchanged(records)
    even = base[0] % (2 * ROWS) == 0
    low, top = target_band[:, ROWS - HALO :], target_band[:, :HALO]
    target_sent = (jnp.where(even, low, top), jnp.where(even, top, low))
    target_ext, target_maps = pl.pallas_call(
        target_kernel,
        in_specs=[spec(SMEM)] + [spec(VMEM)] * 4,
        out_specs=[spec(VMEM)] * 2,
        out_shape=[shaped(3, EXT, COLS), shaped(3, 2, WIDE, COLS)],
        scratch_shapes=[VMEM((6 * EXT, COLS), jnp.float32)],
        compiler_params=params(16),
        name="target",
    )(base, target_band, *swapped(target_sent), across)
    received, target_ext, target_maps = lax.optimization_barrier(
        (received, target_ext, target_maps)
    )
    pred, sent, compact, table, alpha, weight = pl.pallas_call(
        render_kernel,
        in_specs=[spec(SMEM)] * 4 + [spec(VMEM)],
        out_specs=[spec(VMEM)] * 6,
        out_shape=[
            shaped(3, ROWS, COLS),
            shaped(2, 3, HALO, COLS),
            shaped(9, TILES, GAUSS),
            shaped(9, GAUSS, COLS),
            shaped(GAUSS, ROWS, COLS),
            shaped(GAUSS, ROWS, COLS),
        ],
        compiler_params=params(16),
        name="render",
    )(block_list, tile_start, tile_end, base, received)
    pred_one, pred_two = swapped(sent)
    seg = (np.arange(COLS)[None, :] // TILE == np.arange(TILES)[:, None]).astype(np.float32)
    outgoing = pl.pallas_call(
        backward_kernel,
        in_specs=[spec(VMEM)] * 13,
        out_specs=spec(VMEM),
        out_shape=shaped(DEVICES, 1, SLOT),
        scratch_shapes=[
            VMEM((UNROLL, 128, COLS), jnp.float32),
            VMEM((UNROLL, 3, 64, COLS), jnp.float32),
            VMEM((9, GAUSS, COLS), jnp.float32),
            VMEM((9, TILES, GAUSS), jnp.float32),
            VMEM((9 * EXT, COLS), jnp.float32),
            SMEM((1, 128), jnp.int32),
            pltpu.SemaphoreType.DMA,
        ],
        compiler_params=params(16),
        name="backward",
    )(
        lists,
        base_rows,
        pred,
        pred_one,
        pred_two,
        target_ext,
        target_maps,
        across,
        seg,
        compact,
        table,
        alpha,
        weight,
    )
    incoming = exchanged(outgoing)
    loss, *flats = pl.pallas_call(
        update_kernel,
        in_specs=[spec(VMEM)] * 6,
        out_specs=[spec(VMEM)] + [spec(pl.ANY)] * 4,
        out_shape=[shaped(1, 128)] + [shaped(COMPS, BLK_DEV, BLOCK)] * 4,
        scratch_shapes=[VMEM((COMPS, BLK_DEV, BLOCK), jnp.float32)] * 4
        + [
            VMEM((7, BLK_DEV, BLOCK), jnp.float32),
            SMEM((WORDS, DEVICES), jnp.float32),
            SMEM((DEVICES + 1,), jnp.int32),
            pltpu.SemaphoreType.DMA,
            pltpu.SemaphoreType.DMA((16,)),
        ],
        compiler_params=params(16),
        name="update",
    )(words, kept, flat, flat_one, flat_two, incoming)
    new_params, new_one, new_two, gradient = [jnp.transpose(a, (1, 0, 2)) for a in flats]
    return (new_params, new_one, new_two, loss[0, 0], gradient)


def solution(mesh):
    return jax.shard_map(
        per_device,
        mesh=mesh,
        in_specs=(
            P(AXES, None, None),
            P(AXES, None, None),
            P(AXES, None, None),
            P("view", None),
            P("view", None, "band", None),
            P("view", "band", None),
            P("view", "band"),
            P("view", "band", None),
            P("view", "band", None),
        ),
        out_specs=(
            P(AXES, None, None),
            P(AXES, None, None),
            P(AXES, None, None),
            P(),
            P(AXES, None, None),
        ),
        check_vma=False,
    )
```

```python
import math

import jax
import jax.numpy as jnp
import numpy as np
from jax import lax
from jax.experimental import pallas as pl
from jax.experimental.pallas import tpu as pltpu
from jax.sharding import PartitionSpec as P

TILE = 16
ROWS = 16
COLS = 128
TILES = 8
LIST = 16
BLOCK = 256
BLK_DEV = 16
DEVICES = 128
BANDS = 4
COMPS = 62
TILE_MOST = 2
GAUSS = TILE_MOST * BLOCK
HALO = 10
EXT = 48
WIDE = 32
RECORD = 9 * BLOCK
SLOT = RECORD + 128
ASK = 128
UNROLL = 8
KEPT = 18
IMG_ROWS = BANDS * ROWS
AXES = ("view", "band")

HIGHEST_MODE = lax.Precision.HIGHEST
SSIM_WEIGHT = 0.2
ABS_WEIGHT = 0.8
STAB_MEAN = 0.0001
STAB_VAR = 0.0009
BIAS_FIRST = 1.0 - math.exp(100.0 * math.log(0.9))
BIAS_SECOND = 1.0 - math.exp(100.0 * math.log(0.999))
SH_ZERO = 0.28209479177387814
SH_ONE = 0.4886025119029199
SH_TWO = [
    1.0925484305920792,
    -1.0925484305920792,
    0.31539156525252005,
    -1.0925484305920792,
    0.5462742152960396,
]
SH_THREE = [
    -0.5900435899266435,
    2.890611442640554,
    -0.4570457994644658,
    0.3731763325901154,
    -0.4570457994644658,
    1.445305721320277,
    -0.5900435899266435,
]

W_ID = 0
W_CAM = 1
W_SH = 10
WORDS = 32

LOG2_E = math.log2(math.e)

SMEM = pltpu.SMEM
VMEM = pltpu.VMEM


def spec(space):
    return pl.BlockSpec(memory_space=space)


def params(mib):
    return pltpu.CompilerParams(vmem_limit_bytes=mib * 1024 * 1024)


def kernel_taps():
    raw_taps = [math.exp(-(offset * offset) / 4.5) for offset in range(-5, 6)]
    tap_total = sum(raw_taps)
    return [raw_tap / tap_total for raw_tap in raw_taps]


def across_matrix():
    taps = kernel_taps()
    across = np.zeros((COLS, COLS), np.float32)
    for c in range(COLS):
        for o in range(11):
            if 0 <= c + o - 5 < COLS:
                across[c + o - 5, c] = taps[o]
    return across


def learning_rates():
    return np.concatenate(
        [
            np.full(6, 0.016),
            np.full(3, 0.005),
            np.full(4, 0.001),
            np.full(1, 0.05),
            np.full(3, 0.0025),
            np.full(45, 0.000125),
        ]
    ).astype(np.float32)


def harmonics(dir_x, dir_y, dir_z):
    sq_x, sq_y, sq_z = (dir_x * dir_x, dir_y * dir_y, dir_z * dir_z)
    return [
        SH_ZERO + 0.0 * dir_x,
        -SH_ONE * dir_y,
        SH_ONE * dir_z,
        -SH_ONE * dir_x,
        SH_TWO[0] * dir_x * dir_y,
        SH_TWO[1] * dir_y * dir_z,
        SH_TWO[2] * (2.0 * sq_z - sq_x - sq_y),
        SH_TWO[3] * dir_x * dir_z,
        SH_TWO[4] * (sq_x - sq_y),
        SH_THREE[0] * dir_y * (3.0 * sq_x - sq_y),
        SH_THREE[1] * dir_x * dir_y * dir_z,
        SH_THREE[2] * dir_y * (4.0 * sq_z - sq_x - sq_y),
        SH_THREE[3] * dir_z * (2.0 * sq_z - 3.0 * sq_x - 3.0 * sq_y),
        SH_THREE[4] * dir_x * (4.0 * sq_z - sq_x - sq_y),
        SH_THREE[5] * dir_z * (sq_x - sq_y),
        SH_THREE[6] * dir_x * (sq_x - 3.0 * sq_y),
    ]


def request_kernel(list_ref, count_ref, cam_ref, out_ref):
    cam = [jnp.full((1, ASK), cam_ref[0, i], jnp.float32) for i in range(9)]
    a, b = cam[0:3], cam[3:6]
    normal = [
        a[1] * b[2] - a[2] * b[1],
        a[2] * b[0] - a[0] * b[2],
        a[0] * b[1] - a[1] * b[0],
    ]
    size = jnp.sqrt(normal[0] * normal[0] + normal[1] * normal[1] + normal[2] * normal[2])
    basis = harmonics(normal[0] / size, normal[1] / size, normal[2] / size)
    words = [jnp.full((1, ASK), -1.0, jnp.float32)] + cam + basis
    lane = lax.broadcasted_iota(jnp.int32, (1, ASK), 1)
    row = jnp.zeros((1, ASK), jnp.float32)
    for i, word in enumerate(words):
        row = jnp.where(lane == i, word, row)

    def fill(s, carry):
        out_ref[s] = row
        return carry

    lax.fori_loop(0, DEVICES, fill, 0, unroll=8)
    for i in range(LIST):

        @pl.when(i < count_ref[0, 0])
        def _(i=i):
            block = list_ref[0, 0, i]
            local = jnp.full((1, ASK), block % BLK_DEV, jnp.int32).astype(jnp.float32)
            out_ref[block // BLK_DEV] = jnp.where(lane == 0, local, row)


PAIRS = [(0, 0), (0, 1), (0, 2), (1, 1), (1, 2), (2, 2)]


def products(word):
    a = [word(W_CAM + i) for i in range(3)]
    b = [word(W_CAM + 3 + i) for i in range(3)]

    def product(p, q):
        return [p[i] * q[i] if i == j else p[i] * q[j] + p[j] * q[i] for i, j in PAIRS]

    return product(a, a), product(a, b), product(b, b)


def component(ref, c):
    return ref[c]


def shape_terms(g_ref):
    squares = [jnp.exp(2.0 * component(g_ref, 6 + c)) for c in range(3)]
    quat = [component(g_ref, 9 + c) for c in range(4)]
    size = jnp.sqrt(quat[0] * quat[0] + quat[1] * quat[1] + quat[2] * quat[2] + quat[3] * quat[3])
    r, x, y, z = [q / size for q in quat]
    rotation = [
        [1.0 - 2.0 * (y * y + z * z), 2.0 * (x * y - r * z), 2.0 * (x * z + r * y)],
        [2.0 * (x * y + r * z), 1.0 - 2.0 * (x * x + z * z), 2.0 * (y * z - r * x)],
        [2.0 * (x * z - r * y), 2.0 * (y * z + r * x), 1.0 - 2.0 * (x * x + y * y)],
    ]
    return squares, rotation, (r, x, y, z), size


def opacity_of(g_ref):
    return 1.0 / (1.0 + jnp.exp(-component(g_ref, 13)))


def shapes_kernel(g_ref, shape_ref, kept_ref):
    squares, rot, quat, size = shape_terms(g_ref)
    opacity = opacity_of(g_ref)
    kept = squares + rot[0] + rot[1] + rot[2] + list(quat) + [1.0 / size, 1.0 - opacity]
    for i, value in enumerate(kept):
        kept_ref[i] = value
    at = 0
    for i in range(3):
        for j in range(i, 3):
            shape_ref[at] = (
                rot[i][0] * rot[j][0] * squares[0]
                + rot[i][1] * rot[j][1] * squares[1]
                + rot[i][2] * rot[j][2] * squares[2]
            )
            at += 1
    shape_ref[6] = opacity


def listed_slots(word_ref, order_ref):
    def look(s, found):
        order_ref[found] = s
        return found + jnp.where(word_ref[W_ID, s] >= 0.0, 1, 0)

    return lax.fori_loop(0, DEVICES, look, 0, unroll=32)


def records_kernel(ask_ref, g_ref, shape_ref, out_ref, turned_ref, word_ref, order_ref, sem):
    turned_ref[...] = ask_ref[...].reshape(DEVICES, ASK).T[0:WORDS]
    copy = pltpu.make_async_copy(turned_ref, word_ref, sem)
    copy.start()
    copy.wait()
    count = listed_slots(word_ref, order_ref)

    def slot(n, carry):
        s = order_ref[n]
        k = word_ref[W_ID, s].astype(jnp.int32)

        def word(i):
            return word_ref[i, s]

        def comp(i):
            return g_ref[i, pl.ds(k, 1), :]

        def put(p, value):
            out_ref[s, :, pl.ds(p * BLOCK, BLOCK)] = value

        time = word(W_CAM + 8)
        centre = [comp(c) + time * comp(3 + c) for c in range(3)]
        for p in range(2):
            put(
                p,
                word(W_CAM + 3 * p) * centre[0]
                + word(W_CAM + 3 * p + 1) * centre[1]
                + word(W_CAM + 3 * p + 2) * centre[2]
                + word(W_CAM + 6 + p),
            )
        shapes = [shape_ref[i, pl.ds(k, 1), :] for i in range(6)]
        for p, (factor, extra) in enumerate(zip(products(word), (0.3, 0.0, 0.3))):
            total = factor[0] * shapes[0]
            for i in range(1, 6):
                total = total + factor[i] * shapes[i]
            put(2 + p, total + extra)
        put(5, shape_ref[6, pl.ds(k, 1), :])
        basis = [word(W_SH + q) for q in range(16)]
        for ch in range(3):
            colour = basis[0] * comp(14 + ch)
            for q in range(1, 16):
                colour = colour + basis[q] * comp(14 + 3 * q + ch)
            put(6 + ch, colour + 0.5)
        return carry

    lax.fori_loop(0, count, slot, 0)


def pixel_rows(row_base):
    px = lax.broadcasted_iota(jnp.int32, (ROWS, COLS), 1).astype(jnp.float32) + 0.5
    py = lax.broadcasted_iota(jnp.int32, (ROWS, COLS), 0).astype(jnp.float32) + 0.5
    py = py + row_base.astype(jnp.float32)
    return px[0:8], (py[0:8], py[8:16])


def row_of(ref, p, i):
    return jnp.broadcast_to(ref[p, pl.ds(i, 1), :], (8, COLS))


def alpha_of(table, i, px, py):
    dx = px - row_of(table, 0, i)
    slope = row_of(table, 3, i) * dx
    level = row_of(table, 2, i) * dx * dx
    bend, peak, middle = row_of(table, 4, i), row_of(table, 5, i), row_of(table, 1, i)
    return [
        peak * jnp.exp2(level + dy * (slope + bend * dy)) for dy in (py[0] - middle, py[1] - middle)
    ]


def render_kernel(
    list_ref,
    start_ref,
    end_ref,
    base_ref,
    got_ref,
    target_ref,
    pred_ref,
    send_ref,
    compact_ref,
    table_ref,
    alpha_ref,
    weight_ref,
):
    for t in range(TILES):
        first = start_ref[0, 0, t]
        last = end_ref[0, 0, t]
        for j in range(TILE_MOST):
            live = first + j < last
            place = jnp.where(live, first + j, first)
            owner = list_ref[0, 0, place] // BLK_DEV
            there = jnp.where(live, 1.0, 0.0)
            for p in range(9):
                row = got_ref[owner, :, pl.ds(p * BLOCK, BLOCK)]
                if p == 5:
                    row = row * there
                compact_ref[p, pl.ds(t, 1), pl.ds(j * BLOCK, BLOCK)] = row
    ca, cb, cc = compact_ref[2], compact_ref[3], compact_ref[4]
    det = ca * cc - cb * cb
    forms = [
        compact_ref[0],
        compact_ref[1],
        (-0.5 * LOG2_E) * cc / det,
        LOG2_E * cb / det,
        (-0.5 * LOG2_E) * ca / det,
        compact_ref[5],
        compact_ref[6],
        compact_ref[7],
        compact_ref[8],
    ]
    for p, form in enumerate(forms):
        wide = jnp.broadcast_to(form[:, None, :], (TILES, TILE, GAUSS)).reshape(COLS, GAUSS)
        table_ref[p] = wide.T
    px, py = pixel_rows(base_ref[0])

    def blend(i, carry):
        alphas = alpha_of(table_ref, i, px, py)
        colours = [row_of(table_ref, 6 + ch, i) for ch in range(3)]
        after = []
        for half, alpha in enumerate(alphas):
            trans, *sums = carry[half]
            weight = alpha * trans
            rows = pl.ds(8 * half, 8)
            alpha_ref[i, rows, :] = alpha
            weight_ref[i, rows, :] = weight
            after.append(
                (trans - weight, *[a + weight * c for a, c in zip(sums, colours)])
            )
        return tuple(after)

    zero = jnp.zeros((8, COLS), jnp.float32)
    start = (zero + 1.0, zero, zero, zero)
    done = lax.fori_loop(0, GAUSS, blend, (start, start), unroll=32)
    even = base_ref[0] % (2 * ROWS) == 0
    for ch in range(3):
        pred = jnp.concatenate([done[0][1 + ch], done[1][1 + ch]], axis=0)
        pred_ref[ch] = pred
        for at, rows in ((ch, pred), (3 + ch, target_ref[ch])):
            low, top = rows[ROWS - HALO :], rows[:HALO]
            send_ref[0, at] = jnp.where(even, low, top)
            send_ref[1, at] = jnp.where(even, top, low)


def ssim_value(mean_x, mean_y, square_x, square_y, cross_xy):
    var_x = square_x - mean_x * mean_x
    var_y = square_y - mean_y * mean_y
    covar = cross_xy - mean_x * mean_y
    upper = (2.0 * mean_x * mean_y + STAB_MEAN) * (2.0 * covar + STAB_VAR)
    lower = (mean_x * mean_x + mean_y * mean_y + STAB_MEAN) * (var_x + var_y + STAB_VAR)
    return upper / lower


def exact_dot(a, b):
    return jnp.dot(a, b, precision=HIGHEST_MODE, preferred_element_type=jnp.float32)


def extended(mine, even, one, two):
    before, after = jnp.where(even, two, one), jnp.where(even, one, two)
    rest = jnp.zeros((EXT - ROWS - 2 * HALO, COLS), jnp.float32)
    return jnp.concatenate([before, mine, after, rest], axis=0)


def smoothed(maps, rows_out, across, held_ref):
    taps = kernel_taps()
    height = maps[0].shape[0]
    for m, value in enumerate(maps):
        held_ref[pl.ds(height * m, height), :] = value
    done = []
    for m in range(len(maps)):

        def shifted(o, m=m):
            return held_ref[pl.ds(height * m + o, rows_out), :]

        total = taps[5] * shifted(5)
        for o in range(5):
            total = total + taps[o] * (shifted(o) + shifted(10 - o))
        done.append(total)
    wide = exact_dot(jnp.concatenate(done, axis=0), across)
    return [wide[rows_out * m : rows_out * (m + 1)] for m in range(len(maps))]


def loss_gradient(
    base, pred_ref, one_ref, two_ref, target_ref, across_ref, held_ref
):
    across = across_ref[...]
    even = base % (2 * ROWS) == 0
    row = lax.broadcasted_iota(jnp.int32, (WIDE, COLS), 0)
    image_row = row + base - 5
    inside = (image_row >= 0) & (image_row < IMG_ROWS) & (row < ROWS + 10)
    total = jnp.zeros((ROWS, COLS), jnp.float32)
    maps = []
    for ch in range(3):
        x = extended(pred_ref[ch], even, one_ref[ch], two_ref[ch])
        y = extended(target_ref[ch], even, one_ref[3 + ch], two_ref[3 + ch])
        maps = maps + [x, y, x * x, y * y, x * y]
    maps = smoothed(maps, WIDE, across, held_ref)
    values, adjoint = [], []
    for ch in range(3):
        value, pullback = jax.vjp(ssim_value, *maps[5 * ch : 5 * ch + 5])
        parts = pullback(jnp.full_like(value, -SSIM_WEIGHT / 3.0))
        values.append(value)
        adjoint = adjoint + [jnp.where(inside, parts[m], 0.0) for m in (0, 2, 4)]
    back = smoothed(adjoint, ROWS, across, held_ref)
    slopes = []
    for ch in range(3):
        pred, target = pred_ref[ch], target_ref[ch]
        error = pred - target
        sign = jnp.where(error > 0.0, 1.0, jnp.where(error < 0.0, -1.0, 0.0))
        slopes.append(
            ABS_WEIGHT / 3.0 * sign
            + back[3 * ch]
            + 2.0 * pred * back[3 * ch + 1]
            + target * back[3 * ch + 2]
        )
        total = total + (
            ABS_WEIGHT / 3.0 * jnp.abs(error)
            + SSIM_WEIGHT / 3.0 * (1.0 - values[ch][5 : 5 + ROWS])
        )
    total = jnp.sum(jnp.sum(total, axis=1, keepdims=True), axis=0, keepdims=True)
    return total, slopes


def backward_kernel(
    lists_in,
    base_ref,
    pred_ref,
    one_ref,
    two_ref,
    target_ref,
    across_ref,
    seg_ref,
    compact_ref,
    table_ref,
    alpha_ref,
    weight_ref,
    out_ref,
    power_ref,
    part_ref,
    moment_ref,
    grad_ref,
    held_ref,
    lists_ref,
    lists_sem,
):
    copy = pltpu.make_async_copy(lists_in, lists_ref, lists_sem)
    copy.start()
    total, slopes = loss_gradient(
        base_ref[0:1],
        pred_ref,
        one_ref,
        two_ref,
        target_ref,
        across_ref,
        held_ref,
    )
    loss_row = jnp.broadcast_to(total, (1, 128))
    empty = jnp.zeros((1, RECORD), jnp.float32)

    def tell(s, carry):
        out_ref[s, :, pl.ds(RECORD, 128)] = loss_row
        return carry

    lax.fori_loop(0, DEVICES, tell, 0, unroll=8)

    def clear(i, carry):
        out_ref[lists_ref[0, i] // BLK_DEV, :, pl.ds(0, RECORD)] = empty
        return carry

    copy.wait()
    lax.fori_loop(0, lists_ref[0, 32], clear, 0)
    px = lax.broadcasted_iota(jnp.int32, (8, COLS), 1).astype(jnp.float32) + 0.5
    middle = (base_ref[...] + ROWS // 2).astype(jnp.float32)
    slopes = [[slope[0:8], slope[8:16]] for slope in slopes]

    def reverse(step, behind):
        for part in range(UNROLL - 1, -1, -1):
            chunk = GAUSS // 8 - UNROLL * (step + 1) + part
            for r in range(7, -1, -1):
                i = chunk * 8 + r
                colours = [row_of(table_ref, 6 + ch, i) for ch in range(3)]
                weights, after = [], []
                for half in range(2):
                    rows = pl.ds(8 * half, 8)
                    weight = weight_ref[i, rows, :]
                    seen = (
                        colours[0] * slopes[0][half]
                        + colours[1] * slopes[1][half]
                        + colours[2] * slopes[2][half]
                    )
                    ahead = seen - behind[half]
                    after.append(behind[half] + alpha_ref[i, rows, :] * ahead)
                    power_ref[part, pl.ds(16 * r + 8 * half, 8), :] = weight * ahead
                    weights.append(weight)
                behind = after
                for ch in range(3):
                    part_ref[part, ch, pl.ds(8 * r, 8), :] = (
                        weights[0] * slopes[ch][0] + weights[1] * slopes[ch][1]
                    )
            plain = level = bend = None
            for s in range(8):
                upper = power_ref[part, pl.ds(s, 8, stride=16), :]
                lower = power_ref[part, pl.ds(15 - s, 8, stride=16), :]
                offset = 7.5 - s
                total, tilt = upper + lower, (lower - upper) * offset
                round_ = total * (offset * offset)
                plain = total if s == 0 else plain + total
                level = tilt if s == 0 else level + tilt
                bend = round_ if s == 0 else bend + round_
            here = pl.ds(pl.multiple_of(chunk * 8, 8), 8)
            dx = px - table_ref[0, here, :]
            rise = middle - table_ref[1, here, :]
            first_x = plain * dx
            first_y = level + rise * plain
            moment_ref[0, here, :] = plain
            moment_ref[1, here, :] = first_x
            moment_ref[2, here, :] = first_x * dx
            moment_ref[3, here, :] = first_y
            moment_ref[4, here, :] = first_y * dx
            moment_ref[5, here, :] = bend + rise * (level + first_y)
            for ch in range(3):
                piece = part_ref[part, ch, pl.ds(0, 8, stride=8), :]
                for s in range(1, 8):
                    piece = piece + part_ref[part, ch, pl.ds(s, 8, stride=8), :]
                moment_ref[6 + ch, here, :] = piece
        return tuple(behind)

    nothing = jnp.zeros((8, COLS), jnp.float32)
    lax.fori_loop(0, GAUSS // 8 // UNROLL, reverse, (nothing, nothing))
    seg = seg_ref[...].astype(jnp.bfloat16)

    def over_tile(value):
        return lax.dot_general(
            seg, value, (((1,), (1,)), ((), ())), preferred_element_type=jnp.float32
        )

    m = []
    for p in range(9):
        value = moment_ref[p]
        large = value.astype(jnp.bfloat16)
        small = (value - large.astype(jnp.float32)).astype(jnp.bfloat16)
        m.append(over_tile(large) + over_tile(small))
    ca, cb, cc = compact_ref[2], compact_ref[3], compact_ref[4]
    inverse = 1.0 / (ca * cc - cb * cb)
    d_inverse = -0.5 * cc * m[2] + cb * m[4] - 0.5 * ca * m[5]
    d_det = -inverse * inverse * d_inverse
    grad_ref[0] = (cc * m[1] - cb * m[3]) * inverse
    grad_ref[1] = (ca * m[3] - cb * m[1]) * inverse
    grad_ref[2] = -0.5 * inverse * m[5] + cc * d_det
    grad_ref[3] = inverse * m[4] - 2.0 * cb * d_det
    grad_ref[4] = -0.5 * inverse * m[2] + ca * d_det
    grad_ref[5] = m[0]
    for ch in range(3):
        grad_ref[6 + ch] = m[6 + ch]
    for t in range(TILES):
        first = lists_ref[0, 16 + t]
        for j in range(TILE_MOST):

            @pl.when(first + j < lists_ref[0, 24 + t])
            def _(t=t, j=j, first=first):
                owner = lists_ref[0, first + j] // BLK_DEV
                for p in range(9):
                    lanes = pl.ds(p * BLOCK, BLOCK)
                    out_ref[owner, :, lanes] = (
                        out_ref[owner, :, lanes]
                        + grad_ref[p, pl.ds(t, 1), pl.ds(j * BLOCK, BLOCK)]
                    )


def update_kernel(
    turned_ref,
    kept_ref,
    g_ref,
    one_ref,
    two_ref,
    got_ref,
    loss_ref,
    new_out,
    one_out,
    two_out,
    grad_out,
    new_ref,
    new_one_ref,
    new_two_ref,
    grad_ref,
    shape_ref,
    word_ref,
    order_ref,
    word_sem,
    done_sem,
):
    words = pltpu.make_async_copy(turned_ref, word_ref, word_sem)
    words.start()
    rates = [float(rate) / BIAS_FIRST for rate in learning_rates()]
    copies = []

    def finish(low, high):
        for c in range(low, high):
            gradient = grad_ref[c]
            new_one = 0.9 * one_ref[c] + 0.1 * gradient
            new_two = 0.999 * two_ref[c] + 0.001 * gradient * gradient
            root = jnp.sqrt(new_two * (1.0 / BIAS_SECOND)) + 1e-08
            new_ref[c] = g_ref[c] - rates[c] * new_one / root
            new_one_ref[c] = new_one
            new_two_ref[c] = new_two
        here = pl.ds(low, high - low)
        for held, out in (
            (new_ref, new_out),
            (new_one_ref, one_out),
            (new_two_ref, two_out),
            (grad_ref, grad_out),
        ):
            copy = pltpu.make_async_copy(held.at[here], out.at[here], done_sem.at[len(copies)])
            copy.start()
            copies.append(copy)

    losses = got_ref[:, :, pl.ds(RECORD, 128)]
    loss_ref[...] = jnp.sum(losses, axis=0) * (1.0 / (DEVICES * ROWS * COLS))
    grad_ref[...] = jnp.zeros(grad_ref.shape, jnp.float32)
    shape_ref[...] = jnp.zeros(shape_ref.shape, jnp.float32)
    words.wait()
    count = listed_slots(word_ref, order_ref)

    def slot(n, carry):
        s = order_ref[n]
        k = word_ref[W_ID, s].astype(jnp.int32)

        def word(i):
            return word_ref[i, s]

        here = pl.ds(k, 1)

        def add(c, value):
            grad_ref[c, here, :] = grad_ref[c, here, :] + value

        d = [got_ref[s, :, pl.ds(p * BLOCK, BLOCK)] for p in range(9)]
        time = word(W_CAM + 8)
        for c in range(3):
            d_centre = word(W_CAM + c) * d[0] + word(W_CAM + 3 + c) * d[1]
            add(c, d_centre)
            add(3 + c, time * d_centre)
        factors = products(word)
        for i in range(6):
            shape_ref[i, here, :] = shape_ref[i, here, :] + (
                factors[0][i] * d[2] + factors[1][i] * d[3] + factors[2][i] * d[4]
            )
        shape_ref[6, here, :] = shape_ref[6, here, :] + d[5]
        for q in range(16):
            basis = word(W_SH + q)
            for ch in range(3):
                add(14 + 3 * q + ch, basis * d[6 + ch])
        return carry

    lax.fori_loop(0, count, slot, 0)
    for low, high in ((14, 30), (30, 46), (46, COMPS)):
        finish(low, high)
    squares = [kept_ref[c] for c in range(3)]
    rot = [[kept_ref[3 + 3 * i + c] for c in range(3)] for i in range(3)]
    quat = [kept_ref[12 + c] for c in range(4)]
    s00, s01, s02, s11, s12, s22 = [shape_ref[i] for i in range(6)]
    twice = [[2.0 * s00, s01, s02], [s01, 2.0 * s11, s12], [s02, s12, 2.0 * s22]]
    d_rot = [[None] * 3 for _ in range(3)]

    def put(c, value):
        grad_ref[c] = value

    for c in range(3):
        pulled = [
            twice[i][0] * rot[0][c] + twice[i][1] * rot[1][c] + twice[i][2] * rot[2][c]
            for i in range(3)
        ]
        along = rot[0][c] * pulled[0] + rot[1][c] * pulled[1] + rot[2][c] * pulled[2]
        put(6 + c, squares[c] * along)
        for i in range(3):
            d_rot[i][c] = pulled[i] * squares[c]
    r, x, y, z = quat
    n = d_rot
    d_r = 2.0 * (
        -z * n[0][1] + y * n[0][2] + z * n[1][0] - x * n[1][2] - y * n[2][0] + x * n[2][1]
    )
    d_x = 2.0 * (
        y * n[0][1] + z * n[0][2] + y * n[1][0] - 2.0 * x * n[1][1] - r * n[1][2]
        + z * n[2][0] + r * n[2][1] - 2.0 * x * n[2][2]
    )
    d_y = 2.0 * (
        -2.0 * y * n[0][0] + x * n[0][1] + r * n[0][2] + x * n[1][0] + z * n[1][2]
        - r * n[2][0] + z * n[2][1] - 2.0 * y * n[2][2]
    )
    d_z = 2.0 * (
        -2.0 * z * n[0][0] - r * n[0][1] + x * n[0][2] + r * n[1][0] - 2.0 * z * n[1][1]
        + y * n[1][2] + x * n[2][0] + y * n[2][1]
    )
    d_quat = [d_r, d_x, d_y, d_z]
    along = r * d_r + x * d_x + y * d_y + z * d_z
    for c in range(4):
        put(9 + c, (d_quat[c] - quat[c] * along) * kept_ref[16])
    put(13, shape_ref[6] * kept_ref[17])
    finish(0, 14)
    for copy in copies:
        copy.wait()


def shaped(*shape):
    return jax.ShapeDtypeStruct(shape, jnp.float32)


def exchanged(slots):
    return lax.all_to_all(slots, AXES, split_axis=0, concat_axis=0, tiled=True)


def swapped(sent):
    first = [(i, i ^ 1) for i in range(BANDS)]
    second = [(i + 1, (i ^ 1) + 1) for i in range(BANDS - 2)]
    return (lax.ppermute(sent[0], "band", first), lax.ppermute(sent[1], "band", second))


def per_device(
    gaussians,
    first_moment,
    second_moment,
    camera,
    target,
    block_list,
    block_count,
    tile_start,
    tile_end,
):
    flat, flat_one, flat_two = [
        jnp.transpose(a, (1, 0, 2))
        for a in (gaussians, first_moment, second_moment)
    ]
    across = across_matrix()
    base = (lax.axis_index("band") * ROWS).astype(jnp.int32).reshape(1)
    base_rows = jnp.broadcast_to(base.reshape(1, 1), (8, COLS))
    lists = jnp.concatenate(
        [block_list[0, 0], tile_start[0, 0], tile_end[0, 0], block_count[0]]
        + [jnp.zeros((95,), jnp.int32)]
    ).reshape(1, 128)
    request = pl.pallas_call(
        request_kernel,
        in_specs=[spec(SMEM)] * 3,
        out_specs=spec(VMEM),
        out_shape=shaped(DEVICES, 1, ASK),
        name="request",
    )(block_list, block_count, camera)
    asked = exchanged(request)
    target_band = target[0]
    shapes, kept = pl.pallas_call(
        shapes_kernel,
        in_specs=[spec(VMEM)],
        out_specs=[spec(VMEM)] * 2,
        out_shape=[shaped(7, BLK_DEV, BLOCK), shaped(KEPT, BLK_DEV, BLOCK)],
        compiler_params=params(16),
        name="shapes",
    )(flat)
    asked, shapes, kept = lax.optimization_barrier((asked, shapes, kept))
    records, words = pl.pallas_call(
        records_kernel,
        in_specs=[spec(VMEM)] * 3,
        out_specs=[spec(VMEM)] * 2,
        out_shape=[shaped(DEVICES, 1, RECORD), shaped(WORDS, DEVICES)],
        scratch_shapes=[
            SMEM((WORDS, DEVICES), jnp.float32),
            SMEM((DEVICES + 1,), jnp.int32),
            pltpu.SemaphoreType.DMA,
        ],
        compiler_params=params(16),
        name="records",
    )(asked, flat, shapes)
    records, lists, base_rows = lax.optimization_barrier((records, lists, base_rows))
    received = exchanged(records)
    pred, sent, compact, table, alpha, weight = pl.pallas_call(
        render_kernel,
        in_specs=[spec(SMEM)] * 4 + [spec(VMEM)] * 2,
        out_specs=[spec(VMEM)] * 6,
        out_shape=[
            shaped(3, ROWS, COLS),
            shaped(2, 6, HALO, COLS),
            shaped(9, TILES, GAUSS),
            shaped(9, GAUSS, COLS),
            shaped(GAUSS, ROWS, COLS),
            shaped(GAUSS, ROWS, COLS),
        ],
        compiler_params=params(16),
        name="render",
    )(block_list, tile_start, tile_end, base, received, target_band)
    pred_one, pred_two = swapped(sent)
    seg = (np.arange(COLS)[None, :] // TILE == np.arange(TILES)[:, None]).astype(np.float32)
    outgoing = pl.pallas_call(
        backward_kernel,
        in_specs=[spec(VMEM)] * 12,
        out_specs=spec(VMEM),
        out_shape=shaped(DEVICES, 1, SLOT),
        scratch_shapes=[
            VMEM((UNROLL, 128, COLS), jnp.float32),
            VMEM((UNROLL, 3, 64, COLS), jnp.float32),
            VMEM((9, GAUSS, COLS), jnp.float32),
            VMEM((9, TILES, GAUSS), jnp.float32),
            VMEM((15 * EXT, COLS), jnp.float32),
            SMEM((1, 128), jnp.int32),
            pltpu.SemaphoreType.DMA,
        ],
        compiler_params=params(16),
        name="backward",
    )(
        lists,
        base_rows,
        pred,
        pred_one,
        pred_two,
        target_band,
        across,
        seg,
        compact,
        table,
        alpha,
        weight,
    )
    incoming = exchanged(outgoing)
    loss, *flats = pl.pallas_call(
        update_kernel,
        in_specs=[spec(VMEM)] * 6,
        out_specs=[spec(VMEM)] + [spec(pl.ANY)] * 4,
        out_shape=[shaped(1, 128)] + [shaped(COMPS, BLK_DEV, BLOCK)] * 4,
        scratch_shapes=[VMEM((COMPS, BLK_DEV, BLOCK), jnp.float32)] * 4
        + [
            VMEM((7, BLK_DEV, BLOCK), jnp.float32),
            SMEM((WORDS, DEVICES), jnp.float32),
            SMEM((DEVICES + 1,), jnp.int32),
            pltpu.SemaphoreType.DMA,
            pltpu.SemaphoreType.DMA((16,)),
        ],
        compiler_params=params(16),
        name="update",
    )(words, kept, flat, flat_one, flat_two, incoming)
    new_params, new_one, new_two, gradient = [jnp.transpose(a, (1, 0, 2)) for a in flats]
    return (new_params, new_one, new_two, loss[0, 0], gradient)


def solution(mesh):
    return jax.shard_map(
        per_device,
        mesh=mesh,
        in_specs=(
            P(AXES, None, None),
            P(AXES, None, None),
            P(AXES, None, None),
            P("view", None),
            P("view", None, "band", None),
            P("view", "band", None),
            P("view", "band"),
            P("view", "band", None),
            P("view", "band", None),
        ),
        out_specs=(
            P(AXES, None, None),
            P(AXES, None, None),
            P(AXES, None, None),
            P(),
            P(AXES, None, None),
        ),
        check_vma=False,
    )
```

```python
import math

import jax
import jax.numpy as jnp
import numpy as np
from jax import lax
from jax.experimental import pallas as pl
from jax.experimental.pallas import tpu as pltpu
from jax.sharding import PartitionSpec as P

TILE = 16
ROWS = 16
COLS = 128
TILES = 8
LIST = 16
BLOCK = 256
BLK_DEV = 16
DEVICES = 128
BANDS = 4
COMPS = 62
TILE_MOST = 2
GAUSS = TILE_MOST * BLOCK
HALO = 10
EXT = 48
WIDE = 32
RECORD = 9 * BLOCK
SLOT = RECORD + 128
ASK = 128
UNROLL = 8
KEPT = 18
IMG_ROWS = BANDS * ROWS
AXES = ("view", "band")

HIGHEST_MODE = lax.Precision.HIGHEST
SSIM_WEIGHT = 0.2
ABS_WEIGHT = 0.8
STAB_MEAN = 0.0001
STAB_VAR = 0.0009
BIAS_FIRST = 1.0 - math.exp(100.0 * math.log(0.9))
BIAS_SECOND = 1.0 - math.exp(100.0 * math.log(0.999))
SH_ZERO = 0.28209479177387814
SH_ONE = 0.4886025119029199
SH_TWO = [
    1.0925484305920792,
    -1.0925484305920792,
    0.31539156525252005,
    -1.0925484305920792,
    0.5462742152960396,
]
SH_THREE = [
    -0.5900435899266435,
    2.890611442640554,
    -0.4570457994644658,
    0.3731763325901154,
    -0.4570457994644658,
    1.445305721320277,
    -0.5900435899266435,
]

W_ID = 0
W_CAM = 1
W_SH = 10
WORDS = 32

LOG2_E = math.log2(math.e)

SMEM = pltpu.SMEM
VMEM = pltpu.VMEM


def spec(space):
    return pl.BlockSpec(memory_space=space)


def params(mib):
    return pltpu.CompilerParams(vmem_limit_bytes=mib * 1024 * 1024)


def kernel_taps():
    raw_taps = [math.exp(-(offset * offset) / 4.5) for offset in range(-5, 6)]
    tap_total = sum(raw_taps)
    return [raw_tap / tap_total for raw_tap in raw_taps]


def across_matrix():
    taps = kernel_taps()
    across = np.zeros((COLS, COLS), np.float32)
    for c in range(COLS):
        for o in range(11):
            if 0 <= c + o - 5 < COLS:
                across[c + o - 5, c] = taps[o]
    return across


def learning_rates():
    return np.concatenate(
        [
            np.full(6, 0.016),
            np.full(3, 0.005),
            np.full(4, 0.001),
            np.full(1, 0.05),
            np.full(3, 0.0025),
            np.full(45, 0.000125),
        ]
    ).astype(np.float32)


def harmonics(dir_x, dir_y, dir_z):
    sq_x, sq_y, sq_z = (dir_x * dir_x, dir_y * dir_y, dir_z * dir_z)
    return [
        SH_ZERO + 0.0 * dir_x,
        -SH_ONE * dir_y,
        SH_ONE * dir_z,
        -SH_ONE * dir_x,
        SH_TWO[0] * dir_x * dir_y,
        SH_TWO[1] * dir_y * dir_z,
        SH_TWO[2] * (2.0 * sq_z - sq_x - sq_y),
        SH_TWO[3] * dir_x * dir_z,
        SH_TWO[4] * (sq_x - sq_y),
        SH_THREE[0] * dir_y * (3.0 * sq_x - sq_y),
        SH_THREE[1] * dir_x * dir_y * dir_z,
        SH_THREE[2] * dir_y * (4.0 * sq_z - sq_x - sq_y),
        SH_THREE[3] * dir_z * (2.0 * sq_z - 3.0 * sq_x - 3.0 * sq_y),
        SH_THREE[4] * dir_x * (4.0 * sq_z - sq_x - sq_y),
        SH_THREE[5] * dir_z * (sq_x - sq_y),
        SH_THREE[6] * dir_x * (sq_x - 3.0 * sq_y),
    ]


def request_kernel(list_ref, count_ref, cam_ref, out_ref):
    cam = [jnp.full((1, ASK), cam_ref[0, i], jnp.float32) for i in range(9)]
    a, b = cam[0:3], cam[3:6]
    normal = [
        a[1] * b[2] - a[2] * b[1],
        a[2] * b[0] - a[0] * b[2],
        a[0] * b[1] - a[1] * b[0],
    ]
    size = jnp.sqrt(normal[0] * normal[0] + normal[1] * normal[1] + normal[2] * normal[2])
    basis = harmonics(normal[0] / size, normal[1] / size, normal[2] / size)
    words = [jnp.full((1, ASK), -1.0, jnp.float32)] + cam + basis
    lane = lax.broadcasted_iota(jnp.int32, (1, ASK), 1)
    row = jnp.zeros((1, ASK), jnp.float32)
    for i, word in enumerate(words):
        row = jnp.where(lane == i, word, row)

    def fill(s, carry):
        out_ref[s] = row
        return carry

    lax.fori_loop(0, DEVICES, fill, 0, unroll=8)
    for i in range(LIST):

        @pl.when(i < count_ref[0, 0])
        def _(i=i):
            block = list_ref[0, 0, i]
            local = jnp.full((1, ASK), block % BLK_DEV, jnp.int32).astype(jnp.float32)
            out_ref[block // BLK_DEV] = jnp.where(lane == 0, local, row)


PAIRS = [(0, 0), (0, 1), (0, 2), (1, 1), (1, 2), (2, 2)]


def products(word):
    a = [word(W_CAM + i) for i in range(3)]
    b = [word(W_CAM + 3 + i) for i in range(3)]

    def product(p, q):
        return [p[i] * q[i] if i == j else p[i] * q[j] + p[j] * q[i] for i, j in PAIRS]

    return product(a, a), product(a, b), product(b, b)


def component(ref, c):
    return ref[c]


def shape_terms(g_ref):
    squares = [jnp.exp(2.0 * component(g_ref, 6 + c)) for c in range(3)]
    quat = [component(g_ref, 9 + c) for c in range(4)]
    size = jnp.sqrt(quat[0] * quat[0] + quat[1] * quat[1] + quat[2] * quat[2] + quat[3] * quat[3])
    r, x, y, z = [q / size for q in quat]
    rotation = [
        [1.0 - 2.0 * (y * y + z * z), 2.0 * (x * y - r * z), 2.0 * (x * z + r * y)],
        [2.0 * (x * y + r * z), 1.0 - 2.0 * (x * x + z * z), 2.0 * (y * z - r * x)],
        [2.0 * (x * z - r * y), 2.0 * (y * z + r * x), 1.0 - 2.0 * (x * x + y * y)],
    ]
    return squares, rotation, (r, x, y, z), size


def opacity_of(g_ref):
    return 1.0 / (1.0 + jnp.exp(-component(g_ref, 13)))


def shapes_kernel(g_ref, shape_ref, kept_ref):
    squares, rot, quat, size = shape_terms(g_ref)
    opacity = opacity_of(g_ref)
    kept = squares + rot[0] + rot[1] + rot[2] + list(quat) + [1.0 / size, 1.0 - opacity]
    for i, value in enumerate(kept):
        kept_ref[i] = value
    at = 0
    for i in range(3):
        for j in range(i, 3):
            shape_ref[at] = (
                rot[i][0] * rot[j][0] * squares[0]
                + rot[i][1] * rot[j][1] * squares[1]
                + rot[i][2] * rot[j][2] * squares[2]
            )
            at += 1
    shape_ref[6] = opacity


def each_listed(slot, count):
    def pair(n, carry):
        slot(2 * n, 0)
        slot(2 * n + 1, 0)
        return carry

    lax.fori_loop(0, count // 2, pair, 0)
    lax.fori_loop(2 * (count // 2), count, slot, 0)


def listed_slots(word_ref, order_ref):
    def look(s, found):
        order_ref[found] = s
        return found + jnp.where(word_ref[W_ID, s] >= 0.0, 1, 0)

    return lax.fori_loop(0, DEVICES, look, 0, unroll=32)


def records_kernel(ask_ref, g_ref, shape_ref, out_ref, turned_ref, word_ref, order_ref, sem):
    turned_ref[...] = ask_ref[...].reshape(DEVICES, ASK).T[0:WORDS]
    copy = pltpu.make_async_copy(turned_ref, word_ref, sem)
    copy.start()
    copy.wait()
    count = listed_slots(word_ref, order_ref)

    def slot(n, carry):
        s = order_ref[n]
        k = word_ref[W_ID, s].astype(jnp.int32)

        def word(i):
            return word_ref[i, s]

        def comp(i):
            return g_ref[i, pl.ds(k, 1), :]

        def put(p, value):
            out_ref[s, :, pl.ds(p * BLOCK, BLOCK)] = value

        time = word(W_CAM + 8)
        centre = [comp(c) + time * comp(3 + c) for c in range(3)]
        for p in range(2):
            put(
                p,
                word(W_CAM + 3 * p) * centre[0]
                + word(W_CAM + 3 * p + 1) * centre[1]
                + word(W_CAM + 3 * p + 2) * centre[2]
                + word(W_CAM + 6 + p),
            )
        shapes = [shape_ref[i, pl.ds(k, 1), :] for i in range(6)]
        for p, (factor, extra) in enumerate(zip(products(word), (0.3, 0.0, 0.3))):
            total = factor[0] * shapes[0]
            for i in range(1, 6):
                total = total + factor[i] * shapes[i]
            put(2 + p, total + extra)
        put(5, shape_ref[6, pl.ds(k, 1), :])
        basis = [word(W_SH + q) for q in range(16)]
        for ch in range(3):
            colour = basis[0] * comp(14 + ch)
            for q in range(1, 16):
                colour = colour + basis[q] * comp(14 + 3 * q + ch)
            put(6 + ch, colour + 0.5)
        return carry

    each_listed(slot, count)


def pixel_rows(row_base):
    px = lax.broadcasted_iota(jnp.int32, (ROWS, COLS), 1).astype(jnp.float32) + 0.5
    py = lax.broadcasted_iota(jnp.int32, (ROWS, COLS), 0).astype(jnp.float32) + 0.5
    py = py + row_base.astype(jnp.float32)
    return px[0:8], (py[0:8], py[8:16])


def row_of(ref, p, i):
    return jnp.broadcast_to(ref[p, pl.ds(i, 1), :], (8, COLS))


def alpha_of(table, i, px, py):
    dx = px - row_of(table, 0, i)
    slope = row_of(table, 3, i) * dx
    level = row_of(table, 2, i) * dx * dx
    bend, peak, middle = row_of(table, 4, i), row_of(table, 5, i), row_of(table, 1, i)
    return [
        peak * jnp.exp2(level + dy * (slope + bend * dy)) for dy in (py[0] - middle, py[1] - middle)
    ]


def render_kernel(
    list_ref,
    start_ref,
    end_ref,
    base_ref,
    got_ref,
    target_ref,
    pred_ref,
    send_one_ref,
    send_two_ref,
    compact_ref,
    table_ref,
    alpha_ref,
    weight_ref,
):
    for t in range(TILES):
        first = start_ref[0, 0, t]
        last = end_ref[0, 0, t]
        for j in range(TILE_MOST):
            live = first + j < last
            place = jnp.where(live, first + j, first)
            owner = list_ref[0, 0, place] // BLK_DEV
            there = jnp.where(live, 1.0, 0.0)
            for p in range(9):
                row = got_ref[owner, :, pl.ds(p * BLOCK, BLOCK)]
                if p == 5:
                    row = row * there
                compact_ref[p, pl.ds(t, 1), pl.ds(j * BLOCK, BLOCK)] = row
    ca, cb, cc = compact_ref[2], compact_ref[3], compact_ref[4]
    det = ca * cc - cb * cb
    forms = [
        compact_ref[0],
        compact_ref[1],
        (-0.5 * LOG2_E) * cc / det,
        LOG2_E * cb / det,
        (-0.5 * LOG2_E) * ca / det,
        compact_ref[5],
        compact_ref[6],
        compact_ref[7],
        compact_ref[8],
    ]
    for p, form in enumerate(forms):
        wide = jnp.broadcast_to(form[:, None, :], (TILES, TILE, GAUSS)).reshape(COLS, GAUSS)
        table_ref[p] = wide.T
    px, py = pixel_rows(base_ref[0])

    def blend(i, carry):
        alphas = alpha_of(table_ref, i, px, py)
        colours = [row_of(table_ref, 6 + ch, i) for ch in range(3)]
        after = []
        for half, alpha in enumerate(alphas):
            trans, *sums = carry[half]
            weight = alpha * trans
            rows = pl.ds(8 * half, 8)
            alpha_ref[i, rows, :] = alpha
            weight_ref[i, rows, :] = weight
            after.append(
                (trans - weight, *[a + weight * c for a, c in zip(sums, colours)])
            )
        return tuple(after)

    zero = jnp.zeros((8, COLS), jnp.float32)
    start = (zero + 1.0, zero, zero, zero)
    done = lax.fori_loop(0, GAUSS, blend, (start, start), unroll=32)
    even = base_ref[0] % (2 * ROWS) == 0
    for ch in range(3):
        pred = jnp.concatenate([done[0][1 + ch], done[1][1 + ch]], axis=0)
        pred_ref[ch] = pred
        for at, rows in ((ch, pred), (3 + ch, target_ref[ch])):
            low, top = rows[ROWS - HALO :], rows[:HALO]
            send_one_ref[at] = jnp.where(even, low, top)
            send_two_ref[at] = jnp.where(even, top, low)


def ssim_value(mean_x, mean_y, square_x, square_y, cross_xy):
    var_x = square_x - mean_x * mean_x
    var_y = square_y - mean_y * mean_y
    covar = cross_xy - mean_x * mean_y
    upper = (2.0 * mean_x * mean_y + STAB_MEAN) * (2.0 * covar + STAB_VAR)
    lower = (mean_x * mean_x + mean_y * mean_y + STAB_MEAN) * (var_x + var_y + STAB_VAR)
    return upper / lower


def exact_dot(a, b):
    return jnp.dot(a, b, precision=HIGHEST_MODE, preferred_element_type=jnp.float32)


def extended(mine, even, one, two):
    before, after = jnp.where(even, two, one), jnp.where(even, one, two)
    rest = jnp.zeros((EXT - ROWS - 2 * HALO, COLS), jnp.float32)
    return jnp.concatenate([before, mine, after, rest], axis=0)


def smoothed(maps, rows_out, across, held_ref):
    taps = kernel_taps()
    height = maps[0].shape[0]
    for m, value in enumerate(maps):
        held_ref[pl.ds(height * m, height), :] = value
    done = []
    for m in range(len(maps)):

        def shifted(o, m=m):
            return held_ref[pl.ds(height * m + o, rows_out), :]

        total = taps[5] * shifted(5)
        for o in range(5):
            total = total + taps[o] * (shifted(o) + shifted(10 - o))
        done.append(total)
    wide = exact_dot(jnp.concatenate(done, axis=0), across)
    return [wide[rows_out * m : rows_out * (m + 1)] for m in range(len(maps))]


def loss_gradient(
    base, pred_ref, one_ref, two_ref, target_ref, across_ref, held_ref
):
    across = across_ref[...]
    even = base % (2 * ROWS) == 0
    row = lax.broadcasted_iota(jnp.int32, (WIDE, COLS), 0)
    image_row = row + base - 5
    inside = (image_row >= 0) & (image_row < IMG_ROWS) & (row < ROWS + 10)
    total = jnp.zeros((ROWS, COLS), jnp.float32)
    maps = []
    for ch in range(3):
        x = extended(pred_ref[ch], even, one_ref[ch], two_ref[ch])
        y = extended(target_ref[ch], even, one_ref[3 + ch], two_ref[3 + ch])
        maps = maps + [x, y, x * x, y * y, x * y]
    maps = smoothed(maps, WIDE, across, held_ref)
    values, adjoint = [], []
    for ch in range(3):
        value, pullback = jax.vjp(ssim_value, *maps[5 * ch : 5 * ch + 5])
        parts = pullback(jnp.full_like(value, -SSIM_WEIGHT / 3.0))
        values.append(value)
        adjoint = adjoint + [jnp.where(inside, parts[m], 0.0) for m in (0, 2, 4)]
    back = smoothed(adjoint, ROWS, across, held_ref)
    slopes = []
    for ch in range(3):
        pred, target = pred_ref[ch], target_ref[ch]
        error = pred - target
        sign = jnp.where(error > 0.0, 1.0, jnp.where(error < 0.0, -1.0, 0.0))
        slopes.append(
            ABS_WEIGHT / 3.0 * sign
            + back[3 * ch]
            + 2.0 * pred * back[3 * ch + 1]
            + target * back[3 * ch + 2]
        )
        total = total + (
            ABS_WEIGHT / 3.0 * jnp.abs(error)
            + SSIM_WEIGHT / 3.0 * (1.0 - values[ch][5 : 5 + ROWS])
        )
    total = jnp.sum(jnp.sum(total, axis=1, keepdims=True), axis=0, keepdims=True)
    return total, slopes


def backward_kernel(
    lists_in,
    base_ref,
    pred_ref,
    one_ref,
    two_ref,
    target_ref,
    across_ref,
    seg_ref,
    compact_ref,
    table_ref,
    alpha_ref,
    weight_ref,
    out_ref,
    power_ref,
    part_ref,
    moment_ref,
    grad_ref,
    held_ref,
    lists_ref,
    lists_sem,
):
    copy = pltpu.make_async_copy(lists_in, lists_ref, lists_sem)
    copy.start()
    total, slopes = loss_gradient(
        base_ref[0:1],
        pred_ref,
        one_ref,
        two_ref,
        target_ref,
        across_ref,
        held_ref,
    )
    loss_row = jnp.broadcast_to(total, (1, 128))
    empty = jnp.zeros((1, RECORD), jnp.float32)

    def tell(s, carry):
        out_ref[s, :, pl.ds(RECORD, 128)] = loss_row
        return carry

    lax.fori_loop(0, DEVICES, tell, 0, unroll=8)

    def clear(i, carry):
        out_ref[lists_ref[0, i] // BLK_DEV, :, pl.ds(0, RECORD)] = empty
        return carry

    copy.wait()
    lax.fori_loop(0, lists_ref[0, 32], clear, 0)
    px = lax.broadcasted_iota(jnp.int32, (8, COLS), 1).astype(jnp.float32) + 0.5
    middle = (base_ref[...] + ROWS // 2).astype(jnp.float32)
    slopes = [[slope[0:8], slope[8:16]] for slope in slopes]

    def reverse(step, behind):
        for part in range(UNROLL - 1, -1, -1):
            chunk = GAUSS // 8 - UNROLL * (step + 1) + part
            for r in range(7, -1, -1):
                i = chunk * 8 + r
                colours = [row_of(table_ref, 6 + ch, i) for ch in range(3)]
                weights, after = [], []
                for half in range(2):
                    rows = pl.ds(8 * half, 8)
                    weight = weight_ref[i, rows, :]
                    seen = (
                        colours[0] * slopes[0][half]
                        + colours[1] * slopes[1][half]
                        + colours[2] * slopes[2][half]
                    )
                    ahead = seen - behind[half]
                    after.append(behind[half] + alpha_ref[i, rows, :] * ahead)
                    power_ref[part, pl.ds(16 * r + 8 * half, 8), :] = weight * ahead
                    weights.append(weight)
                behind = after
                for ch in range(3):
                    part_ref[part, ch, pl.ds(8 * r, 8), :] = (
                        weights[0] * slopes[ch][0] + weights[1] * slopes[ch][1]
                    )
            plain = level = bend = None
            for s in range(8):
                upper = power_ref[part, pl.ds(s, 8, stride=16), :]
                lower = power_ref[part, pl.ds(15 - s, 8, stride=16), :]
                offset = 7.5 - s
                total, tilt = upper + lower, (lower - upper) * offset
                round_ = total * (offset * offset)
                plain = total if s == 0 else plain + total
                level = tilt if s == 0 else level + tilt
                bend = round_ if s == 0 else bend + round_
            here = pl.ds(pl.multiple_of(chunk * 8, 8), 8)
            dx = px - table_ref[0, here, :]
            rise = middle - table_ref[1, here, :]
            first_x = plain * dx
            first_y = level + rise * plain
            moment_ref[0, here, :] = plain
            moment_ref[1, here, :] = first_x
            moment_ref[2, here, :] = first_x * dx
            moment_ref[3, here, :] = first_y
            moment_ref[4, here, :] = first_y * dx
            moment_ref[5, here, :] = bend + rise * (level + first_y)
            for ch in range(3):
                piece = part_ref[part, ch, pl.ds(0, 8, stride=8), :]
                for s in range(1, 8):
                    piece = piece + part_ref[part, ch, pl.ds(s, 8, stride=8), :]
                moment_ref[6 + ch, here, :] = piece
        return tuple(behind)

    nothing = jnp.zeros((8, COLS), jnp.float32)
    lax.fori_loop(0, GAUSS // 8 // UNROLL, reverse, (nothing, nothing))
    seg = seg_ref[...].astype(jnp.bfloat16)

    def over_tile(value):
        return lax.dot_general(
            seg, value, (((1,), (1,)), ((), ())), preferred_element_type=jnp.float32
        )

    wide_seg = jnp.concatenate([seg, seg], axis=1)
    m = []
    for p in range(9):
        value = moment_ref[p]
        large = value.astype(jnp.bfloat16)
        small = (value - large.astype(jnp.float32)).astype(jnp.bfloat16)
        m.append(
            lax.dot_general(
                wide_seg,
                jnp.concatenate([large, small], axis=1),
                (((1,), (1,)), ((), ())),
                preferred_element_type=jnp.float32,
            )
        )
    ca, cb, cc = compact_ref[2], compact_ref[3], compact_ref[4]
    inverse = 1.0 / (ca * cc - cb * cb)
    d_inverse = -0.5 * cc * m[2] + cb * m[4] - 0.5 * ca * m[5]
    d_det = -inverse * inverse * d_inverse
    grad_ref[0] = (cc * m[1] - cb * m[3]) * inverse
    grad_ref[1] = (ca * m[3] - cb * m[1]) * inverse
    grad_ref[2] = -0.5 * inverse * m[5] + cc * d_det
    grad_ref[3] = inverse * m[4] - 2.0 * cb * d_det
    grad_ref[4] = -0.5 * inverse * m[2] + ca * d_det
    grad_ref[5] = m[0]
    for ch in range(3):
        grad_ref[6 + ch] = m[6 + ch]
    for t in range(TILES):
        first = lists_ref[0, 16 + t]
        for j in range(TILE_MOST):

            @pl.when(first + j < lists_ref[0, 24 + t])
            def _(t=t, j=j, first=first):
                owner = lists_ref[0, first + j] // BLK_DEV
                for p in range(9):
                    lanes = pl.ds(p * BLOCK, BLOCK)
                    out_ref[owner, :, lanes] = (
                        out_ref[owner, :, lanes]
                        + grad_ref[p, pl.ds(t, 1), pl.ds(j * BLOCK, BLOCK)]
                    )


def update_kernel(
    turned_ref,
    kept_ref,
    g_ref,
    one_ref,
    two_ref,
    got_ref,
    loss_ref,
    new_out,
    one_out,
    two_out,
    grad_out,
    new_ref,
    new_one_ref,
    new_two_ref,
    grad_ref,
    shape_ref,
    word_ref,
    order_ref,
    word_sem,
    done_sem,
):
    words = pltpu.make_async_copy(turned_ref, word_ref, word_sem)
    words.start()
    rates = [float(rate) / BIAS_FIRST for rate in learning_rates()]
    copies = []

    def finish(low, high):
        for c in range(low, high):
            gradient = grad_ref[c]
            new_one = 0.9 * one_ref[c] + 0.1 * gradient
            new_two = 0.999 * two_ref[c] + 0.001 * gradient * gradient
            root = jnp.sqrt(new_two * (1.0 / BIAS_SECOND)) + 1e-08
            new_ref[c] = g_ref[c] - rates[c] * new_one / root
            new_one_ref[c] = new_one
            new_two_ref[c] = new_two
        here = pl.ds(low, high - low)
        for held, out in (
            (new_ref, new_out),
            (new_one_ref, one_out),
            (new_two_ref, two_out),
            (grad_ref, grad_out),
        ):
            copy = pltpu.make_async_copy(held.at[here], out.at[here], done_sem.at[len(copies)])
            copy.start()
            copies.append(copy)

    losses = got_ref[:, :, pl.ds(RECORD, 128)]
    loss_ref[...] = jnp.sum(losses, axis=0) * (1.0 / (DEVICES * ROWS * COLS))
    grad_ref[...] = jnp.zeros(grad_ref.shape, jnp.float32)
    shape_ref[...] = jnp.zeros(shape_ref.shape, jnp.float32)
    words.wait()
    count = listed_slots(word_ref, order_ref)

    def slot(n, carry):
        s = order_ref[n]
        k = word_ref[W_ID, s].astype(jnp.int32)

        def word(i):
            return word_ref[i, s]

        here = pl.ds(k, 1)

        def add(c, value):
            grad_ref[c, here, :] = grad_ref[c, here, :] + value

        d = [got_ref[s, :, pl.ds(p * BLOCK, BLOCK)] for p in range(9)]
        time = word(W_CAM + 8)
        for c in range(3):
            d_centre = word(W_CAM + c) * d[0] + word(W_CAM + 3 + c) * d[1]
            add(c, d_centre)
            add(3 + c, time * d_centre)
        factors = products(word)
        for i in range(6):
            shape_ref[i, here, :] = shape_ref[i, here, :] + (
                factors[0][i] * d[2] + factors[1][i] * d[3] + factors[2][i] * d[4]
            )
        shape_ref[6, here, :] = shape_ref[6, here, :] + d[5]
        for q in range(16):
            basis = word(W_SH + q)
            for ch in range(3):
                add(14 + 3 * q + ch, basis * d[6 + ch])
        return carry

    each_listed(slot, count)
    for low, high in ((14, 30), (30, 46), (46, COMPS)):
        finish(low, high)
    squares = [kept_ref[c] for c in range(3)]
    rot = [[kept_ref[3 + 3 * i + c] for c in range(3)] for i in range(3)]
    quat = [kept_ref[12 + c] for c in range(4)]
    s00, s01, s02, s11, s12, s22 = [shape_ref[i] for i in range(6)]
    twice = [[2.0 * s00, s01, s02], [s01, 2.0 * s11, s12], [s02, s12, 2.0 * s22]]
    d_rot = [[None] * 3 for _ in range(3)]

    def put(c, value):
        grad_ref[c] = value

    for c in range(3):
        pulled = [
            twice[i][0] * rot[0][c] + twice[i][1] * rot[1][c] + twice[i][2] * rot[2][c]
            for i in range(3)
        ]
        along = rot[0][c] * pulled[0] + rot[1][c] * pulled[1] + rot[2][c] * pulled[2]
        put(6 + c, squares[c] * along)
        for i in range(3):
            d_rot[i][c] = pulled[i] * squares[c]
    r, x, y, z = quat
    n = d_rot
    d_r = 2.0 * (
        -z * n[0][1] + y * n[0][2] + z * n[1][0] - x * n[1][2] - y * n[2][0] + x * n[2][1]
    )
    d_x = 2.0 * (
        y * n[0][1] + z * n[0][2] + y * n[1][0] - 2.0 * x * n[1][1] - r * n[1][2]
        + z * n[2][0] + r * n[2][1] - 2.0 * x * n[2][2]
    )
    d_y = 2.0 * (
        -2.0 * y * n[0][0] + x * n[0][1] + r * n[0][2] + x * n[1][0] + z * n[1][2]
        - r * n[2][0] + z * n[2][1] - 2.0 * y * n[2][2]
    )
    d_z = 2.0 * (
        -2.0 * z * n[0][0] - r * n[0][1] + x * n[0][2] + r * n[1][0] - 2.0 * z * n[1][1]
        + y * n[1][2] + x * n[2][0] + y * n[2][1]
    )
    d_quat = [d_r, d_x, d_y, d_z]
    along = r * d_r + x * d_x + y * d_y + z * d_z
    for c in range(4):
        put(9 + c, (d_quat[c] - quat[c] * along) * kept_ref[16])
    put(13, shape_ref[6] * kept_ref[17])
    finish(0, 14)
    for copy in copies:
        copy.wait()


def shaped(*shape):
    return jax.ShapeDtypeStruct(shape, jnp.float32)


def exchanged(slots):
    return lax.all_to_all(slots, AXES, split_axis=0, concat_axis=0, tiled=True)


def swapped(one, two):
    first = [(i, i ^ 1) for i in range(BANDS)]
    second = [(i + 1, (i ^ 1) + 1) for i in range(BANDS - 2)]
    return (lax.ppermute(one, "band", first), lax.ppermute(two, "band", second))


def per_device(
    gaussians,
    first_moment,
    second_moment,
    camera,
    target,
    block_list,
    block_count,
    tile_start,
    tile_end,
):
    flat, flat_one, flat_two = [
        jnp.transpose(a, (1, 0, 2))
        for a in (gaussians, first_moment, second_moment)
    ]
    across = across_matrix()
    base = (lax.axis_index("band") * ROWS).astype(jnp.int32).reshape(1)
    base_rows = jnp.broadcast_to(base.reshape(1, 1), (8, COLS))
    lists = jnp.concatenate(
        [block_list[0, 0], tile_start[0, 0], tile_end[0, 0], block_count[0]]
        + [jnp.zeros((95,), jnp.int32)]
    ).reshape(1, 128)
    request = pl.pallas_call(
        request_kernel,
        in_specs=[spec(SMEM)] * 3,
        out_specs=spec(VMEM),
        out_shape=shaped(DEVICES, 1, ASK),
        name="request",
    )(block_list, block_count, camera)
    asked = exchanged(request)
    target_band = target[0]
    shapes, kept = pl.pallas_call(
        shapes_kernel,
        in_specs=[spec(VMEM)],
        out_specs=[spec(VMEM)] * 2,
        out_shape=[shaped(7, BLK_DEV, BLOCK), shaped(KEPT, BLK_DEV, BLOCK)],
        compiler_params=params(16),
        name="shapes",
    )(flat)
    asked, shapes, kept = lax.optimization_barrier((asked, shapes, kept))
    records, words = pl.pallas_call(
        records_kernel,
        in_specs=[spec(VMEM)] * 3,
        out_specs=[spec(VMEM)] * 2,
        out_shape=[shaped(DEVICES, 1, RECORD), shaped(WORDS, DEVICES)],
        scratch_shapes=[
            SMEM((WORDS, DEVICES), jnp.float32),
            SMEM((DEVICES + 1,), jnp.int32),
            pltpu.SemaphoreType.DMA,
        ],
        compiler_params=params(16),
        name="records",
    )(asked, flat, shapes)
    records, lists, base_rows = lax.optimization_barrier((records, lists, base_rows))
    received = exchanged(records)
    pred, sent_one, sent_two, compact, table, alpha, weight = pl.pallas_call(
        render_kernel,
        in_specs=[spec(SMEM)] * 4 + [spec(VMEM)] * 2,
        out_specs=[spec(VMEM)] * 7,
        out_shape=[
            shaped(3, ROWS, COLS),
            shaped(6, HALO, COLS),
            shaped(6, HALO, COLS),
            shaped(9, TILES, GAUSS),
            shaped(9, GAUSS, COLS),
            shaped(GAUSS, ROWS, COLS),
            shaped(GAUSS, ROWS, COLS),
        ],
        compiler_params=params(16),
        name="render",
    )(block_list, tile_start, tile_end, base, received, target_band)
    pred_one, pred_two = swapped(sent_one, sent_two)
    seg = (np.arange(COLS)[None, :] // TILE == np.arange(TILES)[:, None]).astype(np.float32)
    outgoing = pl.pallas_call(
        backward_kernel,
        in_specs=[spec(VMEM)] * 12,
        out_specs=spec(VMEM),
        out_shape=shaped(DEVICES, 1, SLOT),
        scratch_shapes=[
            VMEM((UNROLL, 128, COLS), jnp.float32),
            VMEM((UNROLL, 3, 64, COLS), jnp.float32),
            VMEM((9, GAUSS, COLS), jnp.float32),
            VMEM((9, TILES, GAUSS), jnp.float32),
            VMEM((15 * EXT, COLS), jnp.float32),
            SMEM((1, 128), jnp.int32),
            pltpu.SemaphoreType.DMA,
        ],
        compiler_params=params(16),
        name="backward",
    )(
        lists,
        base_rows,
        pred,
        pred_one,
        pred_two,
        target_band,
        across,
        seg,
        compact,
        table,
        alpha,
        weight,
    )
    incoming = exchanged(outgoing)
    loss, *flats = pl.pallas_call(
        update_kernel,
        in_specs=[spec(VMEM)] * 6,
        out_specs=[spec(VMEM)] + [spec(pl.ANY)] * 4,
        out_shape=[shaped(1, 128)] + [shaped(COMPS, BLK_DEV, BLOCK)] * 4,
        scratch_shapes=[VMEM((COMPS, BLK_DEV, BLOCK), jnp.float32)] * 4
        + [
            VMEM((7, BLK_DEV, BLOCK), jnp.float32),
            SMEM((WORDS, DEVICES), jnp.float32),
            SMEM((DEVICES + 1,), jnp.int32),
            pltpu.SemaphoreType.DMA,
            pltpu.SemaphoreType.DMA((16,)),
        ],
        compiler_params=params(16),
        name="update",
    )(words, kept, flat, flat_one, flat_two, incoming)
    new_params, new_one, new_two, gradient = [jnp.transpose(a, (1, 0, 2)) for a in flats]
    return (new_params, new_one, new_two, loss[0, 0], gradient)


def solution(mesh):
    return jax.shard_map(
        per_device,
        mesh=mesh,
        in_specs=(
            P(AXES, None, None),
            P(AXES, None, None),
            P(AXES, None, None),
            P("view", None),
            P("view", None, "band", None),
            P("view", "band", None),
            P("view", "band"),
            P("view", "band", None),
            P("view", "band", None),
        ),
        out_specs=(
            P(AXES, None, None),
            P(AXES, None, None),
            P(AXES, None, None),
            P(),
            P(AXES, None, None),
        ),
        check_vma=False,
    )
```

```python
import math

import jax
import jax.numpy as jnp
import numpy as np
from jax import lax
from jax.experimental import pallas as pl
from jax.experimental.pallas import tpu as pltpu
from jax.sharding import PartitionSpec as P

TILE = 16
ROWS = 16
COLS = 128
TILES = 8
LIST = 16
BLOCK = 256
BLK_DEV = 16
DEVICES = 128
BANDS = 4
COMPS = 62
TILE_MOST = 2
GAUSS = TILE_MOST * BLOCK
HALO = 10
EXT = 48
WIDE = 32
RECORD = 9 * BLOCK
SLOT = RECORD + 128
ASK = 128
UNROLL = 8
KEPT = 18
IMG_ROWS = BANDS * ROWS
AXES = ("view", "band")

HIGHEST_MODE = lax.Precision.HIGHEST
SSIM_WEIGHT = 0.2
ABS_WEIGHT = 0.8
STAB_MEAN = 0.0001
STAB_VAR = 0.0009
BIAS_FIRST = 1.0 - math.exp(100.0 * math.log(0.9))
BIAS_SECOND = 1.0 - math.exp(100.0 * math.log(0.999))
SH_ZERO = 0.28209479177387814
SH_ONE = 0.4886025119029199
SH_TWO = [
    1.0925484305920792,
    -1.0925484305920792,
    0.31539156525252005,
    -1.0925484305920792,
    0.5462742152960396,
]
SH_THREE = [
    -0.5900435899266435,
    2.890611442640554,
    -0.4570457994644658,
    0.3731763325901154,
    -0.4570457994644658,
    1.445305721320277,
    -0.5900435899266435,
]

W_ID = 0
W_CAM = 1
W_SH = 10
WORDS = 32

LOG2_E = math.log2(math.e)

SMEM = pltpu.SMEM
VMEM = pltpu.VMEM


def spec(space):
    return pl.BlockSpec(memory_space=space)


def params(mib):
    return pltpu.CompilerParams(vmem_limit_bytes=mib * 1024 * 1024)


def kernel_taps():
    raw_taps = [math.exp(-(offset * offset) / 4.5) for offset in range(-5, 6)]
    tap_total = sum(raw_taps)
    return [raw_tap / tap_total for raw_tap in raw_taps]


def across_matrix():
    taps = kernel_taps()
    across = np.zeros((COLS, COLS), np.float32)
    for c in range(COLS):
        for o in range(11):
            if 0 <= c + o - 5 < COLS:
                across[c + o - 5, c] = taps[o]
    return across


def learning_rates():
    return np.concatenate(
        [
            np.full(6, 0.016),
            np.full(3, 0.005),
            np.full(4, 0.001),
            np.full(1, 0.05),
            np.full(3, 0.0025),
            np.full(45, 0.000125),
        ]
    ).astype(np.float32)


def harmonics(dir_x, dir_y, dir_z):
    sq_x, sq_y, sq_z = (dir_x * dir_x, dir_y * dir_y, dir_z * dir_z)
    return [
        SH_ZERO + 0.0 * dir_x,
        -SH_ONE * dir_y,
        SH_ONE * dir_z,
        -SH_ONE * dir_x,
        SH_TWO[0] * dir_x * dir_y,
        SH_TWO[1] * dir_y * dir_z,
        SH_TWO[2] * (2.0 * sq_z - sq_x - sq_y),
        SH_TWO[3] * dir_x * dir_z,
        SH_TWO[4] * (sq_x - sq_y),
        SH_THREE[0] * dir_y * (3.0 * sq_x - sq_y),
        SH_THREE[1] * dir_x * dir_y * dir_z,
        SH_THREE[2] * dir_y * (4.0 * sq_z - sq_x - sq_y),
        SH_THREE[3] * dir_z * (2.0 * sq_z - 3.0 * sq_x - 3.0 * sq_y),
        SH_THREE[4] * dir_x * (4.0 * sq_z - sq_x - sq_y),
        SH_THREE[5] * dir_z * (sq_x - sq_y),
        SH_THREE[6] * dir_x * (sq_x - 3.0 * sq_y),
    ]


def request_kernel(list_ref, count_ref, cam_ref, out_ref):
    cam = [jnp.full((1, ASK), cam_ref[0, i], jnp.float32) for i in range(9)]
    a, b = cam[0:3], cam[3:6]
    normal = [
        a[1] * b[2] - a[2] * b[1],
        a[2] * b[0] - a[0] * b[2],
        a[0] * b[1] - a[1] * b[0],
    ]
    size = jnp.sqrt(normal[0] * normal[0] + normal[1] * normal[1] + normal[2] * normal[2])
    basis = harmonics(normal[0] / size, normal[1] / size, normal[2] / size)
    words = [jnp.full((1, ASK), -1.0, jnp.float32)] + cam + basis
    lane = lax.broadcasted_iota(jnp.int32, (1, ASK), 1)
    row = jnp.zeros((1, ASK), jnp.float32)
    for i, word in enumerate(words):
        row = jnp.where(lane == i, word, row)

    def fill(s, carry):
        out_ref[s] = row
        return carry

    lax.fori_loop(0, DEVICES, fill, 0, unroll=8)
    for i in range(LIST):

        @pl.when(i < count_ref[0, 0])
        def _(i=i):
            block = list_ref[0, 0, i]
            local = jnp.full((1, ASK), block % BLK_DEV, jnp.int32).astype(jnp.float32)
            out_ref[block // BLK_DEV] = jnp.where(lane == 0, local, row)


PAIRS = [(0, 0), (0, 1), (0, 2), (1, 1), (1, 2), (2, 2)]


def products(word):
    a = [word(W_CAM + i) for i in range(3)]
    b = [word(W_CAM + 3 + i) for i in range(3)]

    def product(p, q):
        return [p[i] * q[i] if i == j else p[i] * q[j] + p[j] * q[i] for i, j in PAIRS]

    return product(a, a), product(a, b), product(b, b)


def component(ref, c):
    return ref[c]


def shape_terms(g_ref):
    squares = [jnp.exp(2.0 * component(g_ref, 6 + c)) for c in range(3)]
    quat = [component(g_ref, 9 + c) for c in range(4)]
    size = jnp.sqrt(quat[0] * quat[0] + quat[1] * quat[1] + quat[2] * quat[2] + quat[3] * quat[3])
    r, x, y, z = [q / size for q in quat]
    rotation = [
        [1.0 - 2.0 * (y * y + z * z), 2.0 * (x * y - r * z), 2.0 * (x * z + r * y)],
        [2.0 * (x * y + r * z), 1.0 - 2.0 * (x * x + z * z), 2.0 * (y * z - r * x)],
        [2.0 * (x * z - r * y), 2.0 * (y * z + r * x), 1.0 - 2.0 * (x * x + y * y)],
    ]
    return squares, rotation, (r, x, y, z), size


def opacity_of(g_ref):
    return 1.0 / (1.0 + jnp.exp(-component(g_ref, 13)))


def shapes_kernel(g_ref, shape_ref, kept_ref):
    squares, rot, quat, size = shape_terms(g_ref)
    opacity = opacity_of(g_ref)
    kept = squares + rot[0] + rot[1] + rot[2] + list(quat) + [1.0 / size, 1.0 - opacity]
    for i, value in enumerate(kept):
        kept_ref[i] = value
    at = 0
    for i in range(3):
        for j in range(i, 3):
            shape_ref[at] = (
                rot[i][0] * rot[j][0] * squares[0]
                + rot[i][1] * rot[j][1] * squares[1]
                + rot[i][2] * rot[j][2] * squares[2]
            )
            at += 1
    shape_ref[6] = opacity


def each_listed(slot, count):
    def pair(n, carry):
        slot(2 * n, 0)
        slot(2 * n + 1, 0)
        return carry

    lax.fori_loop(0, count // 2, pair, 0)
    lax.fori_loop(2 * (count // 2), count, slot, 0)


def listed_slots(word_ref, order_ref):
    def look(s, found):
        order_ref[found] = s
        return found + jnp.where(word_ref[W_ID, s] >= 0.0, 1, 0)

    return lax.fori_loop(0, DEVICES, look, 0, unroll=32)


def records_kernel(ask_ref, g_ref, shape_ref, out_ref, turned_ref, word_ref, order_ref, sem):
    turned_ref[...] = ask_ref[...].reshape(DEVICES, ASK).T[0:WORDS]
    copy = pltpu.make_async_copy(turned_ref, word_ref, sem)
    copy.start()
    copy.wait()
    count = listed_slots(word_ref, order_ref)

    def slot(n, carry):
        s = order_ref[n]
        k = word_ref[W_ID, s].astype(jnp.int32)

        def word(i):
            return word_ref[i, s]

        def comp(i):
            return g_ref[i, pl.ds(k, 1), :]

        def put(p, value):
            out_ref[s, :, pl.ds(p * BLOCK, BLOCK)] = value

        time = word(W_CAM + 8)
        centre = [comp(c) + time * comp(3 + c) for c in range(3)]
        for p in range(2):
            put(
                p,
                word(W_CAM + 3 * p) * centre[0]
                + word(W_CAM + 3 * p + 1) * centre[1]
                + word(W_CAM + 3 * p + 2) * centre[2]
                + word(W_CAM + 6 + p),
            )
        shapes = [shape_ref[i, pl.ds(k, 1), :] for i in range(6)]
        for p, (factor, extra) in enumerate(zip(products(word), (0.3, 0.0, 0.3))):
            total = factor[0] * shapes[0]
            for i in range(1, 6):
                total = total + factor[i] * shapes[i]
            put(2 + p, total + extra)
        put(5, shape_ref[6, pl.ds(k, 1), :])
        basis = [word(W_SH + q) for q in range(16)]
        for ch in range(3):
            colour = basis[0] * comp(14 + ch)
            for q in range(1, 16):
                colour = colour + basis[q] * comp(14 + 3 * q + ch)
            put(6 + ch, colour + 0.5)
        return carry

    each_listed(slot, count)


def pixel_rows(row_base):
    px = lax.broadcasted_iota(jnp.int32, (ROWS, COLS), 1).astype(jnp.float32) + 0.5
    py = lax.broadcasted_iota(jnp.int32, (ROWS, COLS), 0).astype(jnp.float32) + 0.5
    py = py + row_base.astype(jnp.float32)
    return px[0:8], (py[0:8], py[8:16])


def row_of(ref, p, i):
    return jnp.broadcast_to(ref[p, pl.ds(i, 1), :], (8, COLS))


def alpha_of(table, i, px, py):
    dx = px - row_of(table, 0, i)
    slope = row_of(table, 3, i) * dx
    level = row_of(table, 2, i) * dx * dx
    bend, peak, middle = row_of(table, 4, i), row_of(table, 5, i), row_of(table, 1, i)
    return [
        peak * jnp.exp2(level + dy * (slope + bend * dy)) for dy in (py[0] - middle, py[1] - middle)
    ]


def render_kernel(
    list_ref,
    start_ref,
    end_ref,
    base_ref,
    got_ref,
    target_ref,
    pred_ref,
    send_one_ref,
    send_two_ref,
    compact_ref,
    table_ref,
    alpha_ref,
    weight_ref,
):
    for t in range(TILES):
        first = start_ref[0, 0, t]
        last = end_ref[0, 0, t]
        for j in range(TILE_MOST):
            live = first + j < last
            place = jnp.where(live, first + j, first)
            owner = list_ref[0, 0, place] // BLK_DEV
            there = jnp.where(live, 1.0, 0.0)
            for p in range(9):
                row = got_ref[owner, :, pl.ds(p * BLOCK, BLOCK)]
                if p == 5:
                    row = row * there
                compact_ref[p, pl.ds(t, 1), pl.ds(j * BLOCK, BLOCK)] = row
    ca, cb, cc = compact_ref[2], compact_ref[3], compact_ref[4]
    det = ca * cc - cb * cb
    forms = [
        compact_ref[0],
        compact_ref[1],
        (-0.5 * LOG2_E) * cc / det,
        LOG2_E * cb / det,
        (-0.5 * LOG2_E) * ca / det,
        compact_ref[5],
        compact_ref[6],
        compact_ref[7],
        compact_ref[8],
    ]
    for p, form in enumerate(forms):
        wide = jnp.broadcast_to(form[:, None, :], (TILES, TILE, GAUSS)).reshape(COLS, GAUSS)
        table_ref[p] = wide.T
    px, py = pixel_rows(base_ref[0])

    def blend(i, carry):
        alphas = alpha_of(table_ref, i, px, py)
        colours = [row_of(table_ref, 6 + ch, i) for ch in range(3)]
        after = []
        for half, alpha in enumerate(alphas):
            trans, *sums = carry[half]
            weight = alpha * trans
            rows = pl.ds(8 * half, 8)
            alpha_ref[i, rows, :] = alpha
            weight_ref[i, rows, :] = weight
            after.append(
                (trans - weight, *[a + weight * c for a, c in zip(sums, colours)])
            )
        return tuple(after)

    zero = jnp.zeros((8, COLS), jnp.float32)
    start = (zero + 1.0, zero, zero, zero)
    done = lax.fori_loop(0, GAUSS, blend, (start, start), unroll=32)
    even = base_ref[0] % (2 * ROWS) == 0
    for ch in range(3):
        pred = jnp.concatenate([done[0][1 + ch], done[1][1 + ch]], axis=0)
        pred_ref[ch] = pred
        for at, rows in ((ch, pred), (3 + ch, target_ref[ch])):
            low, top = rows[ROWS - HALO :], rows[:HALO]
            send_one_ref[at] = jnp.where(even, low, top)
            send_two_ref[at] = jnp.where(even, top, low)


def ssim_value(mean_x, mean_y, square_x, square_y, cross_xy):
    var_x = square_x - mean_x * mean_x
    var_y = square_y - mean_y * mean_y
    covar = cross_xy - mean_x * mean_y
    upper = (2.0 * mean_x * mean_y + STAB_MEAN) * (2.0 * covar + STAB_VAR)
    lower = (mean_x * mean_x + mean_y * mean_y + STAB_MEAN) * (var_x + var_y + STAB_VAR)
    return upper / lower


def exact_dot(a, b):
    return jnp.dot(a, b, precision=HIGHEST_MODE, preferred_element_type=jnp.float32)


def extended(mine, even, one, two):
    before, after = jnp.where(even, two, one), jnp.where(even, one, two)
    rest = jnp.zeros((EXT - ROWS - 2 * HALO, COLS), jnp.float32)
    return jnp.concatenate([before, mine, after, rest], axis=0)


def smoothed(maps, rows_out, across, held_ref):
    taps = kernel_taps()
    height = maps[0].shape[0]
    for m, value in enumerate(maps):
        held_ref[pl.ds(height * m, height), :] = value
    done = []
    for m in range(len(maps)):

        def shifted(o, m=m):
            return held_ref[pl.ds(height * m + o, rows_out), :]

        total = taps[5] * shifted(5)
        for o in range(5):
            total = total + taps[o] * (shifted(o) + shifted(10 - o))
        done.append(total)
    wide = exact_dot(jnp.concatenate(done, axis=0), across)
    return [wide[rows_out * m : rows_out * (m + 1)] for m in range(len(maps))]


def loss_gradient(
    base, pred_ref, one_ref, two_ref, target_ref, across_ref, held_ref
):
    across = across_ref[...]
    even = base % (2 * ROWS) == 0
    row = lax.broadcasted_iota(jnp.int32, (WIDE, COLS), 0)
    image_row = row + base - 5
    inside = (image_row >= 0) & (image_row < IMG_ROWS) & (row < ROWS + 10)
    total = jnp.zeros((ROWS, COLS), jnp.float32)
    maps = []
    for ch in range(3):
        x = extended(pred_ref[ch], even, one_ref[ch], two_ref[ch])
        y = extended(target_ref[ch], even, one_ref[3 + ch], two_ref[3 + ch])
        maps = maps + [x, y, x * x, y * y, x * y]
    maps = smoothed(maps, WIDE, across, held_ref)
    values, adjoint = [], []
    for ch in range(3):
        value, pullback = jax.vjp(ssim_value, *maps[5 * ch : 5 * ch + 5])
        parts = pullback(jnp.full_like(value, -SSIM_WEIGHT / 3.0))
        values.append(value)
        adjoint = adjoint + [jnp.where(inside, parts[m], 0.0) for m in (0, 2, 4)]
    back = smoothed(adjoint, ROWS, across, held_ref)
    slopes = []
    for ch in range(3):
        pred, target = pred_ref[ch], target_ref[ch]
        error = pred - target
        sign = jnp.where(error > 0.0, 1.0, jnp.where(error < 0.0, -1.0, 0.0))
        slopes.append(
            ABS_WEIGHT / 3.0 * sign
            + back[3 * ch]
            + 2.0 * pred * back[3 * ch + 1]
            + target * back[3 * ch + 2]
        )
        total = total + (
            ABS_WEIGHT / 3.0 * jnp.abs(error)
            + SSIM_WEIGHT / 3.0 * (1.0 - values[ch][5 : 5 + ROWS])
        )
    total = jnp.sum(jnp.sum(total, axis=1, keepdims=True), axis=0, keepdims=True)
    return total, slopes


def backward_kernel(
    lists_in,
    base_ref,
    pred_ref,
    one_ref,
    two_ref,
    target_ref,
    across_ref,
    seg_ref,
    compact_ref,
    table_ref,
    alpha_ref,
    weight_ref,
    out_ref,
    power_ref,
    part_ref,
    moment_ref,
    grad_ref,
    held_ref,
    lists_ref,
    lists_sem,
):
    copy = pltpu.make_async_copy(lists_in, lists_ref, lists_sem)
    copy.start()
    total, slopes = loss_gradient(
        base_ref[0:1],
        pred_ref,
        one_ref,
        two_ref,
        target_ref,
        across_ref,
        held_ref,
    )
    loss_row = jnp.broadcast_to(total, (1, 128))
    empty = jnp.zeros((1, RECORD), jnp.float32)

    def tell(s, carry):
        out_ref[s, :, pl.ds(RECORD, 128)] = loss_row
        return carry

    lax.fori_loop(0, DEVICES, tell, 0, unroll=8)

    def clear(i, carry):
        out_ref[lists_ref[0, i] // BLK_DEV, :, pl.ds(0, RECORD)] = empty
        return carry

    copy.wait()
    lax.fori_loop(0, lists_ref[0, 32], clear, 0)
    px = lax.broadcasted_iota(jnp.int32, (8, COLS), 1).astype(jnp.float32) + 0.5
    middle = (base_ref[...] + ROWS // 2).astype(jnp.float32)
    slopes = [[slope[0:8], slope[8:16]] for slope in slopes]

    def reverse(step, behind):
        for part in range(UNROLL - 1, -1, -1):
            chunk = GAUSS // 8 - UNROLL * (step + 1) + part
            for r in range(7, -1, -1):
                i = chunk * 8 + r
                colours = [row_of(table_ref, 6 + ch, i) for ch in range(3)]
                weights, after = [], []
                for half in range(2):
                    rows = pl.ds(8 * half, 8)
                    weight = weight_ref[i, rows, :]
                    seen = (
                        colours[0] * slopes[0][half]
                        + colours[1] * slopes[1][half]
                        + colours[2] * slopes[2][half]
                    )
                    ahead = seen - behind[half]
                    after.append(behind[half] + alpha_ref[i, rows, :] * ahead)
                    power_ref[part, pl.ds(16 * r + 8 * half, 8), :] = weight * ahead
                    weights.append(weight)
                behind = after
                for ch in range(3):
                    part_ref[part, ch, pl.ds(8 * r, 8), :] = (
                        weights[0] * slopes[ch][0] + weights[1] * slopes[ch][1]
                    )
            plain = level = bend = None
            for s in range(8):
                upper = power_ref[part, pl.ds(s, 8, stride=16), :]
                lower = power_ref[part, pl.ds(15 - s, 8, stride=16), :]
                offset = 7.5 - s
                total, tilt = upper + lower, (lower - upper) * offset
                round_ = total * (offset * offset)
                plain = total if s == 0 else plain + total
                level = tilt if s == 0 else level + tilt
                bend = round_ if s == 0 else bend + round_
            here = pl.ds(pl.multiple_of(chunk * 8, 8), 8)
            dx = px - table_ref[0, here, :]
            rise = middle - table_ref[1, here, :]
            first_x = plain * dx
            first_y = level + rise * plain
            moment_ref[0, here, :] = plain
            moment_ref[1, here, :] = first_x
            moment_ref[2, here, :] = first_x * dx
            moment_ref[3, here, :] = first_y
            moment_ref[4, here, :] = first_y * dx
            moment_ref[5, here, :] = bend + rise * (level + first_y)
            for ch in range(3):
                piece = part_ref[part, ch, pl.ds(0, 8, stride=8), :]
                for s in range(1, 8):
                    piece = piece + part_ref[part, ch, pl.ds(s, 8, stride=8), :]
                moment_ref[6 + ch, here, :] = piece
        return tuple(behind)

    nothing = jnp.zeros((8, COLS), jnp.float32)
    lax.fori_loop(0, GAUSS // 8 // UNROLL, reverse, (nothing, nothing))
    seg = seg_ref[...].astype(jnp.bfloat16)

    def over_tile(value):
        return lax.dot_general(
            seg, value, (((1,), (1,)), ((), ())), preferred_element_type=jnp.float32
        )

    wide_seg = jnp.concatenate([seg, seg], axis=1)
    m = []
    for p in range(9):
        value = moment_ref[p]
        large = value.astype(jnp.bfloat16)
        small = (value - large.astype(jnp.float32)).astype(jnp.bfloat16)
        m.append(
            lax.dot_general(
                wide_seg,
                jnp.concatenate([large, small], axis=1),
                (((1,), (1,)), ((), ())),
                preferred_element_type=jnp.float32,
            )
        )
    ca, cb, cc = compact_ref[2], compact_ref[3], compact_ref[4]
    inverse = 1.0 / (ca * cc - cb * cb)
    d_inverse = -0.5 * cc * m[2] + cb * m[4] - 0.5 * ca * m[5]
    d_det = -inverse * inverse * d_inverse
    grad_ref[0] = (cc * m[1] - cb * m[3]) * inverse
    grad_ref[1] = (ca * m[3] - cb * m[1]) * inverse
    grad_ref[2] = -0.5 * inverse * m[5] + cc * d_det
    grad_ref[3] = inverse * m[4] - 2.0 * cb * d_det
    grad_ref[4] = -0.5 * inverse * m[2] + ca * d_det
    grad_ref[5] = m[0]
    for ch in range(3):
        grad_ref[6 + ch] = m[6 + ch]
    for t in range(TILES):
        first = lists_ref[0, 16 + t]
        for j in range(TILE_MOST):

            @pl.when(first + j < lists_ref[0, 24 + t])
            def _(t=t, j=j, first=first):
                owner = lists_ref[0, first + j] // BLK_DEV
                for p in range(9):
                    lanes = pl.ds(p * BLOCK, BLOCK)
                    out_ref[owner, :, lanes] = (
                        out_ref[owner, :, lanes]
                        + grad_ref[p, pl.ds(t, 1), pl.ds(j * BLOCK, BLOCK)]
                    )


def update_kernel(
    turned_ref,
    kept_ref,
    g_ref,
    one_ref,
    two_ref,
    got_ref,
    loss_ref,
    new_out,
    one_out,
    two_out,
    grad_out,
    new_ref,
    new_one_ref,
    new_two_ref,
    grad_ref,
    shape_ref,
    word_ref,
    order_ref,
    word_sem,
    done_sem,
):
    words = pltpu.make_async_copy(turned_ref, word_ref, word_sem)
    words.start()
    rates = [float(rate) / BIAS_FIRST for rate in learning_rates()]
    copies = []

    def finish(low, high):
        for c in range(low, high):
            gradient = grad_ref[c]
            new_one = 0.9 * one_ref[c] + 0.1 * gradient
            new_two = 0.999 * two_ref[c] + 0.001 * gradient * gradient
            root = jnp.sqrt(new_two * (1.0 / BIAS_SECOND)) + 1e-08
            new_ref[c] = g_ref[c] - rates[c] * new_one / root
            new_one_ref[c] = new_one
            new_two_ref[c] = new_two
        here = pl.ds(low, high - low)
        for held, out in (
            (new_ref, new_out),
            (new_one_ref, one_out),
            (new_two_ref, two_out),
            (grad_ref, grad_out),
        ):
            copy = pltpu.make_async_copy(held.at[here], out.at[here], done_sem.at[len(copies)])
            copy.start()
            copies.append(copy)

    losses = got_ref[:, :, pl.ds(RECORD, 128)]
    loss_ref[...] = jnp.sum(losses, axis=0) * (1.0 / (DEVICES * ROWS * COLS))
    grad_ref[...] = jnp.zeros(grad_ref.shape, jnp.float32)
    shape_ref[...] = jnp.zeros(shape_ref.shape, jnp.float32)
    words.wait()
    count = listed_slots(word_ref, order_ref)

    def slot(n, carry):
        s = order_ref[n]
        k = word_ref[W_ID, s].astype(jnp.int32)

        def word(i):
            return word_ref[i, s]

        here = pl.ds(k, 1)

        def add(c, value):
            grad_ref[c, here, :] = grad_ref[c, here, :] + value

        d = [got_ref[s, :, pl.ds(p * BLOCK, BLOCK)] for p in range(9)]
        time = word(W_CAM + 8)
        for c in range(3):
            d_centre = word(W_CAM + c) * d[0] + word(W_CAM + 3 + c) * d[1]
            add(c, d_centre)
            add(3 + c, time * d_centre)
        factors = products(word)
        for i in range(6):
            shape_ref[i, here, :] = shape_ref[i, here, :] + (
                factors[0][i] * d[2] + factors[1][i] * d[3] + factors[2][i] * d[4]
            )
        shape_ref[6, here, :] = shape_ref[6, here, :] + d[5]
        for q in range(16):
            basis = word(W_SH + q)
            for ch in range(3):
                add(14 + 3 * q + ch, basis * d[6 + ch])
        return carry

    each_listed(slot, count)
    for low, high in ((14, 18), (18, 26), (26, 44), (44, COMPS)):
        finish(low, high)
    squares = [kept_ref[c] for c in range(3)]
    rot = [[kept_ref[3 + 3 * i + c] for c in range(3)] for i in range(3)]
    quat = [kept_ref[12 + c] for c in range(4)]
    s00, s01, s02, s11, s12, s22 = [shape_ref[i] for i in range(6)]
    twice = [[2.0 * s00, s01, s02], [s01, 2.0 * s11, s12], [s02, s12, 2.0 * s22]]
    d_rot = [[None] * 3 for _ in range(3)]

    def put(c, value):
        grad_ref[c] = value

    for c in range(3):
        pulled = [
            twice[i][0] * rot[0][c] + twice[i][1] * rot[1][c] + twice[i][2] * rot[2][c]
            for i in range(3)
        ]
        along = rot[0][c] * pulled[0] + rot[1][c] * pulled[1] + rot[2][c] * pulled[2]
        put(6 + c, squares[c] * along)
        for i in range(3):
            d_rot[i][c] = pulled[i] * squares[c]
    r, x, y, z = quat
    n = d_rot
    d_r = 2.0 * (
        -z * n[0][1] + y * n[0][2] + z * n[1][0] - x * n[1][2] - y * n[2][0] + x * n[2][1]
    )
    d_x = 2.0 * (
        y * n[0][1] + z * n[0][2] + y * n[1][0] - 2.0 * x * n[1][1] - r * n[1][2]
        + z * n[2][0] + r * n[2][1] - 2.0 * x * n[2][2]
    )
    d_y = 2.0 * (
        -2.0 * y * n[0][0] + x * n[0][1] + r * n[0][2] + x * n[1][0] + z * n[1][2]
        - r * n[2][0] + z * n[2][1] - 2.0 * y * n[2][2]
    )
    d_z = 2.0 * (
        -2.0 * z * n[0][0] - r * n[0][1] + x * n[0][2] + r * n[1][0] - 2.0 * z * n[1][1]
        + y * n[1][2] + x * n[2][0] + y * n[2][1]
    )
    d_quat = [d_r, d_x, d_y, d_z]
    along = r * d_r + x * d_x + y * d_y + z * d_z
    for c in range(4):
        put(9 + c, (d_quat[c] - quat[c] * along) * kept_ref[16])
    put(13, shape_ref[6] * kept_ref[17])
    finish(0, 14)
    for copy in copies:
        copy.wait()


def shaped(*shape):
    return jax.ShapeDtypeStruct(shape, jnp.float32)


def exchanged(slots):
    return lax.all_to_all(slots, AXES, split_axis=0, concat_axis=0, tiled=True)


def swapped(one, two):
    first = [(i, i ^ 1) for i in range(BANDS)]
    second = [(i + 1, (i ^ 1) + 1) for i in range(BANDS - 2)]
    return (lax.ppermute(one, "band", first), lax.ppermute(two, "band", second))


def per_device(
    gaussians,
    first_moment,
    second_moment,
    camera,
    target,
    block_list,
    block_count,
    tile_start,
    tile_end,
):
    flat, flat_one, flat_two = [
        jnp.transpose(a, (1, 0, 2))
        for a in (gaussians, first_moment, second_moment)
    ]
    across = across_matrix()
    base = (lax.axis_index("band") * ROWS).astype(jnp.int32).reshape(1)
    base_rows = jnp.broadcast_to(base.reshape(1, 1), (8, COLS))
    lists = jnp.concatenate(
        [block_list[0, 0], tile_start[0, 0], tile_end[0, 0], block_count[0]]
        + [jnp.zeros((95,), jnp.int32)]
    ).reshape(1, 128)
    request = pl.pallas_call(
        request_kernel,
        in_specs=[spec(SMEM)] * 3,
        out_specs=spec(VMEM),
        out_shape=shaped(DEVICES, 1, ASK),
        name="request",
    )(block_list, block_count, camera)
    asked = exchanged(request)
    target_band = target[0]
    shapes, kept = pl.pallas_call(
        shapes_kernel,
        in_specs=[spec(VMEM)],
        out_specs=[spec(VMEM)] * 2,
        out_shape=[shaped(7, BLK_DEV, BLOCK), shaped(KEPT, BLK_DEV, BLOCK)],
        compiler_params=params(16),
        name="shapes",
    )(flat)
    asked, shapes, kept = lax.optimization_barrier((asked, shapes, kept))
    records, words = pl.pallas_call(
        records_kernel,
        in_specs=[spec(VMEM)] * 3,
        out_specs=[spec(VMEM)] * 2,
        out_shape=[shaped(DEVICES, 1, RECORD), shaped(WORDS, DEVICES)],
        scratch_shapes=[
            SMEM((WORDS, DEVICES), jnp.float32),
            SMEM((DEVICES + 1,), jnp.int32),
            pltpu.SemaphoreType.DMA,
        ],
        compiler_params=params(16),
        name="records",
    )(asked, flat, shapes)
    records, lists, base_rows = lax.optimization_barrier((records, lists, base_rows))
    received = exchanged(records)
    pred, sent_one, sent_two, compact, table, alpha, weight = pl.pallas_call(
        render_kernel,
        in_specs=[spec(SMEM)] * 4 + [spec(VMEM)] * 2,
        out_specs=[spec(VMEM)] * 7,
        out_shape=[
            shaped(3, ROWS, COLS),
            shaped(6, HALO, COLS),
            shaped(6, HALO, COLS),
            shaped(9, TILES, GAUSS),
            shaped(9, GAUSS, COLS),
            shaped(GAUSS, ROWS, COLS),
            shaped(GAUSS, ROWS, COLS),
        ],
        compiler_params=params(16),
        name="render",
    )(block_list, tile_start, tile_end, base, received, target_band)
    pred_one, pred_two = swapped(sent_one, sent_two)
    seg = (np.arange(COLS)[None, :] // TILE == np.arange(TILES)[:, None]).astype(np.float32)
    outgoing = pl.pallas_call(
        backward_kernel,
        in_specs=[spec(VMEM)] * 12,
        out_specs=spec(VMEM),
        out_shape=shaped(DEVICES, 1, SLOT),
        scratch_shapes=[
            VMEM((UNROLL, 128, COLS), jnp.float32),
            VMEM((UNROLL, 3, 64, COLS), jnp.float32),
            VMEM((9, GAUSS, COLS), jnp.float32),
            VMEM((9, TILES, GAUSS), jnp.float32),
            VMEM((15 * EXT, COLS), jnp.float32),
            SMEM((1, 128), jnp.int32),
            pltpu.SemaphoreType.DMA,
        ],
        compiler_params=params(16),
        name="backward",
    )(
        lists,
        base_rows,
        pred,
        pred_one,
        pred_two,
        target_band,
        across,
        seg,
        compact,
        table,
        alpha,
        weight,
    )
    incoming = exchanged(outgoing)
    loss, *flats = pl.pallas_call(
        update_kernel,
        in_specs=[spec(VMEM)] * 6,
        out_specs=[spec(VMEM)] + [spec(pl.ANY)] * 4,
        out_shape=[shaped(1, 128)] + [shaped(COMPS, BLK_DEV, BLOCK)] * 4,
        scratch_shapes=[VMEM((COMPS, BLK_DEV, BLOCK), jnp.float32)] * 4
        + [
            VMEM((7, BLK_DEV, BLOCK), jnp.float32),
            SMEM((WORDS, DEVICES), jnp.float32),
            SMEM((DEVICES + 1,), jnp.int32),
            pltpu.SemaphoreType.DMA,
            pltpu.SemaphoreType.DMA((20,)),
        ],
        compiler_params=params(16),
        name="update",
    )(words, kept, flat, flat_one, flat_two, incoming)
    new_params, new_one, new_two, gradient = [jnp.transpose(a, (1, 0, 2)) for a in flats]
    return (new_params, new_one, new_two, loss[0, 0], gradient)


def solution(mesh):
    return jax.shard_map(
        per_device,
        mesh=mesh,
        in_specs=(
            P(AXES, None, None),
            P(AXES, None, None),
            P(AXES, None, None),
            P("view", None),
            P("view", None, "band", None),
            P("view", "band", None),
            P("view", "band"),
            P("view", "band", None),
            P("view", "band", None),
        ),
        out_specs=(
            P(AXES, None, None),
            P(AXES, None, None),
            P(AXES, None, None),
            P(),
            P(AXES, None, None),
        ),
        check_vma=False,
    )
```
